32 devices in a mesh: groups: 2 (over x), attn: 8 (over z, y), ffn: 2 (over core).
Axes of the slice: x: 2, y: 2, z: 4, core: 2. Of those that a mesh axis runs over, the one named last changes fastest.
Arguments:
- tokens: bfloat16 [256, 7168], P(('groups', 'attn', 'ffn')), parts along dimension 0, may hold values from -6 to 6
- expert_ids: int32 [256, 3], P(('groups', 'attn', 'ffn')), parts along dimension 0, may hold values from 0 to 3, all different within a row; in each aligned block of 8 rows (0 to 7, 8 to 15, ...) at most 7 rows name the same one
- route_weights: float32 [256, 3], P(('groups', 'attn', 'ffn')), parts along dimension 0, may hold values from 0.2 to 1
- gate_weight: bfloat16 [7168, 16384], P(None, ('attn', 'ffn')), may hold values from -0.0625 to 0.0625
- up_weight: bfloat16 [7168, 16384], P(None, ('attn', 'ffn')), may hold values from -0.0625 to 0.0625
- down_weight: bfloat16 [16384, 7168], P(('attn', 'ffn')), may hold values from -0.09375 to 0.09375
Outputs:
- mixed: bfloat16 [256, 7168], P(('groups', 'attn', 'ffn')), parts along dimension 0
The draws below stay inside these ranges and needn't reach their ends.
There are 2 independent parts, one for each index of `groups`. The reference program is written for one: setup_inputs(seed, part) draws one part's arguments, and reference() takes and returns one part's arrays. A program takes and returns all parts, laid end to end along the dimension named above; an argument that names none is the same for every part. Nothing has to cross between parts.
Inputs may be any that keep to these rules, and one draw needn't show every extreme that they name: `expert_ids`: each row names 3 different experts; among the rows of one device no expert is named by more than 7 rows, a bound that some of them reach.
All inputs are finite; a program needn't handle non-finite values.
Results may differ from the reference program's by a relative error of at most 0.0049.
Values may be sent and summed in bfloat16 or wider, within the bound.
No kernel may reach another device: no remote copies, remote signals or barrier semaphores. Data moves between devices by JAX's collectives and lax.ppermute only.
A program may use at most 128 MiB of HBM per device.

```python
import math
import jax
import jax.numpy as jnp
import numpy as np
from jax import lax

D = 7168
FF = 4096
EXPERTS = 4
TOP = 3
TOK_DEV = 8
CAP = 7
TOKENS = 128


def level_of(own_key, shape, cuts, low, largest):
    gain, own = 1.0, jax.random.fold_in(own_key, 6)
    for dim, blocks in cuts:
        draws = jnp.exp(jax.random.uniform(jax.random.fold_in(own, dim), (blocks,), jnp.float32, low / len(cuts), largest / len(cuts)))
        gain = gain * jnp.repeat(draws, shape[dim] // blocks).reshape([-1 if axis == dim else 1 for axis in range(len(shape))])
    return gain


def deal_out(stream_key, own, number, rows, number_of, top, limit, lean):
    order = jax.random.permutation(stream_key, number_of)
    packed, ordinary = load_shares(number_of, rows * top, limit, lean, True), load_shares(number_of, rows * top, limit, lean, False)
    places = jnp.arange(number_of)

    def named(sizes, turn):
        used = int((sizes > 0).sum())
        fixed = max(1, used // 4)
        moved = fixed + (places - fixed + turn * (used - fixed)) % max(1, number_of - fixed)
        return jnp.zeros((number_of,), jnp.int32).at[order[jnp.where(places < fixed, places, moved)]].set(jnp.asarray(sizes, jnp.int32))

    sizes = jnp.where(number % 4 == 0, named(packed, number // 4), named(ordinary, number - number // 4 - 1))
    mixed = jax.random.permutation(jax.random.fold_in(own, 3), number_of)
    source_of, taker = mixed[0:number_of // 2 * 2:2], mixed[1:number_of // 2 * 2:2]
    room = jnp.minimum(sizes[source_of] - 1, limit - sizes[taker]) // 2
    room = jnp.where((source_of == order[0]) | (taker == order[0]) | (sizes[taker] == 0), 0, jnp.maximum(room, 0))
    moved = jax.random.randint(jax.random.fold_in(own, 4), (number_of // 2,), 0, 1 << 20) % (room + 1)
    sizes = sizes.at[source_of].add(-moved).at[taker].add(moved)
    items = jnp.searchsorted(jnp.cumsum(sizes), jnp.arange(rows * top), side="right").astype(jnp.int32)
    listing = items.reshape(top, rows).T
    listing = listing[jax.random.permutation(jax.random.fold_in(own, 1), rows)]
    turn = jax.random.randint(jax.random.fold_in(own, 2), (rows, 1), 0, top)
    return jnp.take_along_axis(listing, (jnp.arange(top)[None, :] + turn) % top, axis=1)


def load_shares(amount, total, reach, skew, full):
    portions = [(1 << 20) // math.isqrt(grade ** skew) + 1 for grade in range(1, amount + 1)]
    largest = reach if full else min(reach, max(-(-total // amount), total * portions[0] // sum(portions)))
    least = 1 if total - largest >= amount - 1 else 0
    given, spare = [largest] + [least] * (amount - 1), total - largest - least * (amount - 1)
    while spare > 0:
        candidates = [i for i in range(1, amount) if given[i] < largest] or [i for i in range(1, amount) if given[i] < reach]
        whole, remaining = sum([portions[i] for i in candidates]), spare
        for i in candidates:
            addition = min(reach - given[i], max(1, remaining * portions[i] // whole), spare)
            given[i] = given[i] + addition
            spare = spare - addition
    return np.array(given)


def noise(key, extent, deviation, bound, shards=(), kind=jnp.bfloat16):
    drawn = deviation * jax.random.normal(key, extent, jnp.float32)
    if shards:
        drawn = drawn * level_of(key, extent, shards, -0.22, 0.18)
    return jnp.clip(drawn, -bound, bound).astype(kind)


def setup_inputs(seed: int = 0, part: int = 0) -> dict:
    keys = jax.random.split(jax.random.key(seed), 7)
    own_keys = jax.random.split(jax.random.fold_in(keys[6], part), 7)
    tokens = noise(own_keys[0], (TOKENS, D), 1.0, 6.0, ((0, 16),))
    expert_ids_keys = jax.random.split(jax.random.fold_in(own_keys[1], 1), TOKENS // TOK_DEV)
    expert_ids_turns = jax.random.permutation(jax.random.fold_in(own_keys[1], 3), TOKENS // TOK_DEV)
    expert_ids = jax.vmap(lambda own, number: deal_out(jax.random.fold_in(own_keys[1], 2), own, number, TOK_DEV, EXPERTS, TOP, CAP, 2))(expert_ids_keys, expert_ids_turns).reshape((TOKENS, TOP))
    route_weights = jnp.clip(0.2 + 0.8 * jax.random.uniform(own_keys[2], (TOKENS, TOP), jnp.float32) ** level_of(own_keys[2], (TOKENS, TOP), ((0, 16),), -0.2, 0.2), 0.2, 1.0)
    gate_weight = noise(keys[3], (D, EXPERTS * FF), D ** -0.5, 0.0625, ((1, 16),))
    up_weight = noise(keys[4], (D, EXPERTS * FF), D ** -0.5, 0.0625, ((1, 16),))
    down_weight = noise(keys[5], (EXPERTS * FF, D), FF ** -0.5, 0.09375, ((0, 16),))
    return {"tokens": tokens, "expert_ids": expert_ids, "route_weights": route_weights, "gate_weight": gate_weight, "up_weight": up_weight, "down_weight": down_weight}


def expert_apply(token_rows, gate_cols, up_cols, down_rows):
    gate_value = jnp.dot(token_rows, gate_cols, preferred_element_type=jnp.float32)
    up_value = jnp.dot(token_rows, up_cols, preferred_element_type=jnp.float32)
    hidden = (jax.nn.silu(gate_value) * up_value).astype(jnp.bfloat16)
    return jnp.dot(hidden, down_rows, preferred_element_type=jnp.float32)


def reference(tokens, expert_ids, route_weights, gate_weight, up_weight, down_weight):
    gate_stack = gate_weight.reshape(D, EXPERTS, FF).transpose(1, 0, 2)
    up_stack = up_weight.reshape(D, EXPERTS, FF).transpose(1, 0, 2)
    down_stack = down_weight.reshape(EXPERTS, FF, D)

    def one_expert(weights):
        return expert_apply(tokens, weights[0], weights[1], weights[2])

    outputs = lax.map(one_expert, (gate_stack, up_stack, down_stack))
    chosen = expert_ids[:, :, None] == jnp.arange(EXPERTS, dtype=jnp.int32)[None, None, :]
    coeffs = jnp.sum(jnp.where(chosen, route_weights[:, :, None], 0.0), axis=1)
    mixed = jnp.einsum("te,etd->td", coeffs, outputs, precision=lax.Precision.HIGHEST)
    return mixed.astype(jnp.bfloat16)
```

```python
import jax
import jax.numpy as jnp
from jax import lax
from jax.sharding import PartitionSpec as P

EXPERTS = 4


def local(tokens, expert_ids, route_weights, gate_weight, up_weight, down_weight):
    span_count = lax.axis_size("attn") // EXPERTS
    expert = lax.axis_index("attn") // span_count
    coeff = jnp.sum(jnp.where(expert_ids[:, :, None] == jnp.arange(EXPERTS)[None, None, :], route_weights[:, :, None], 0.0), axis=1)
    rows = lax.all_gather(tokens, ("attn", "ffn"), axis=0, tiled=True)
    coeffs = lax.all_gather(coeff, ("attn", "ffn"), axis=0, tiled=True)
    own = jnp.sum(jnp.where(jnp.arange(EXPERTS)[None, :] == expert, coeffs, 0.0), axis=1, keepdims=True)
    gate_value = jnp.dot(rows, gate_weight, preferred_element_type=jnp.float32)
    up_value = jnp.dot(rows, up_weight, preferred_element_type=jnp.float32)
    hidden = (jax.nn.silu(gate_value) * up_value).astype(jnp.bfloat16)
    partial_value = jnp.dot(hidden, down_weight, preferred_element_type=jnp.float32) * own
    mixed = lax.psum_scatter(partial_value, ("attn", "ffn"), scatter_dimension=0, tiled=True)
    return mixed.astype(jnp.bfloat16)


def solution(mesh):
    return jax.shard_map(
        local,
        mesh=mesh,
        in_specs=(
            P(("groups", "attn", "ffn"), None),
            P(("groups", "attn", "ffn"), None),
            P(("groups", "attn", "ffn"), None),
            P(None, ("attn", "ffn")),
            P(None, ("attn", "ffn")),
            P(("attn", "ffn"), None),
        ),
        out_specs=P(("groups", "attn", "ffn"), None),
        check_vma=False,
    )
```

```python
import functools

import jax
import jax.numpy as jnp
from jax import lax
from jax.experimental import pallas as pl
from jax.experimental.pallas import tpu as pltpu
from jax.sharding import PartitionSpec as P

EXPERTS = 4
IN_CHUNKS = 2
OUT_CHUNKS = 2
K_BLOCK = 512
C_BLOCK = 512
VMEM = 40 * 1024 * 1024


def params():
    return pltpu.CompilerParams(vmem_limit_bytes=VMEM)


def block_of(width, most):
    size = most
    while width % size:
        size -= 128
    return size


def gate_up_kernel(blocks, first, last, k_block, *refs):
    rows_in, rest = refs[:blocks], refs[blocks:]
    gate_ref, up_ref, rest = rest[0], rest[1], rest[2:]
    if not first:
        old_gate, old_up, rest = rest[0], rest[1], rest[2:]
    step = pl.program_id(0)
    if last:
        hidden_ref, acc_gate, acc_up = rest
    else:
        acc_gate, acc_up = rest

    @pl.when(step == 0)
    def _():
        if first:
            acc_gate[...] = jnp.zeros_like(acc_gate)
            acc_up[...] = jnp.zeros_like(acc_up)
        else:
            acc_gate[...] = old_gate[...]
            acc_up[...] = old_up[...]

    columns = pl.ds(pl.multiple_of(step * k_block, k_block), k_block)
    rows = jnp.concatenate([ref[:, columns].astype(jnp.float32) for ref in rows_in], axis=0).astype(jnp.bfloat16)
    acc_gate[...] += jnp.dot(rows, gate_ref[...], preferred_element_type=jnp.float32)
    acc_up[...] += jnp.dot(rows, up_ref[...], preferred_element_type=jnp.float32)

    if last:
        @pl.when(step == pl.num_programs(0) - 1)
        def _():
            gate = acc_gate[...]
            hidden_ref[...] = (gate / (1.0 + jnp.exp(-gate)) * acc_up[...]).astype(jnp.bfloat16)


def gate_up(rows, gate_weight, up_weight, sums, chunk, chunks):
    first, last = chunk == 0, chunk == chunks - 1
    total = sum(r.shape[0] for r in rows)
    width, units = rows[0].shape[1], gate_weight.shape[1]
    k_block = block_of(width, K_BLOCK)
    steps = width // k_block
    weight_spec = pl.BlockSpec((k_block, units), lambda k: (chunk * steps + k, 0))
    whole = lambda a: pl.BlockSpec(a.shape, lambda k: (0, 0))
    acc = jax.ShapeDtypeStruct((total, units), jnp.float32)
    if last:
        out_shape = jax.ShapeDtypeStruct((total, units), jnp.bfloat16)
        out_specs = whole(out_shape)
        scratch = [pltpu.VMEM(acc.shape, jnp.float32)] * 2
    else:
        out_shape, out_specs, scratch = [acc, acc], [whole(acc)] * 2, []
    return pl.pallas_call(
        functools.partial(gate_up_kernel, len(rows), first, last, k_block),
        grid=(steps,),
        in_specs=[whole(r) for r in rows] + [weight_spec] * 2 + ([] if first else [whole(acc)] * 2),
        out_specs=out_specs,
        out_shape=out_shape,
        scratch_shapes=scratch,
        compiler_params=params(),
        cost_estimate=pl.CostEstimate(flops=4 * total * width * units, bytes_accessed=4 * width * units, transcendentals=0),
        name="gate_up",
    )(*rows, gate_weight, up_weight, *sums)


def down_kernel(hidden_ref, down_ref, keep_ref, *send_refs):
    value = jnp.dot(hidden_ref[...], down_ref[...], preferred_element_type=jnp.float32)
    count = keep_ref.shape[0]
    keep_ref[...] = value[:count]
    for i, ref in enumerate(send_refs):
        ref[...] = value[(i + 1) * count:(i + 2) * count].astype(jnp.bfloat16)


def down(hidden, down_weight, chunk, chunks, pair):
    total, units = hidden.shape
    width = down_weight.shape[1] // chunks
    c_block = block_of(width, C_BLOCK)
    steps = width // c_block
    part = total // pair
    part_spec = pl.BlockSpec((part, c_block), lambda c: (0, c))
    return pl.pallas_call(
        down_kernel,
        grid=(steps,),
        in_specs=[
            pl.BlockSpec(hidden.shape, lambda c: (0, 0)),
            pl.BlockSpec((units, c_block), lambda c: (0, chunk * steps + c)),
        ],
        out_specs=[part_spec] * pair,
        out_shape=[jax.ShapeDtypeStruct((part, width), jnp.float32)]
        + [jax.ShapeDtypeStruct((part, width), jnp.bfloat16)] * (pair - 1),
        compiler_params=params(),
        cost_estimate=pl.CostEstimate(flops=2 * total * width * units, bytes_accessed=2 * width * units, transcendentals=0),
        name="down",
    )(hidden, down_weight)


def add_kernel(count, *refs):
    value = refs[0][...]
    for ref in refs[1:count]:
        value += ref[...].astype(jnp.float32)
    outs = refs[count:]
    part = outs[0].shape[0]
    outs[0][...] = value[:part]
    for i, ref in enumerate(outs[1:]):
        ref[...] = value[(i + 1) * part:(i + 2) * part].astype(jnp.bfloat16)


def add_split(keep, received, parts):
    total, width = keep.shape
    part = total // parts
    arrays = [keep] + received
    return pl.pallas_call(
        functools.partial(add_kernel, len(arrays)),
        out_shape=[jax.ShapeDtypeStruct((part, width), jnp.float32)]
        + [jax.ShapeDtypeStruct((part, width), jnp.bfloat16)] * (parts - 1),
        compiler_params=params(),
        cost_estimate=pl.CostEstimate(flops=total * width, bytes_accessed=12 * total * width, transcendentals=0),
        name="add_split",
    )(*arrays)


def combine_kernel(chunks, own_expert, ids_ref, weights_ref, *refs):
    out_ref = refs[-1]
    ids, weights = ids_ref[...], weights_ref[...]
    width = refs[0].shape[1]
    coeffs = []
    for s in range(EXPERTS):
        expert = lax.rem(own_expert[0] + s, EXPERTS)
        coeffs.append(jnp.sum(jnp.where(ids == expert, weights, 0.0), axis=1, keepdims=True))
    for chunk in range(chunks):
        value = None
        for s in range(EXPERTS):
            term = coeffs[s] * refs[chunk * EXPERTS + s][...].astype(jnp.float32)
            value = term if value is None else value + term
        out_ref[:, chunk * width:(chunk + 1) * width] = value.astype(jnp.bfloat16)


def combine(own_expert, ids, weights, parts):
    flat = [p for chunk in parts for p in chunk]
    rows, width = flat[0].shape
    return pl.pallas_call(
        functools.partial(combine_kernel, len(parts)),
        in_specs=[pl.BlockSpec(memory_space=pltpu.SMEM)] + [pl.BlockSpec(memory_space=pltpu.VMEM)] * (2 + len(flat)),
        out_shape=jax.ShapeDtypeStruct((rows, width * len(parts)), jnp.bfloat16),
        compiler_params=params(),
        name="combine",
    )(own_expert, ids, weights, *flat)


def local(tokens, expert_ids, route_weights, gate_weight, up_weight, down_weight):
    width = tokens.shape[1]
    attn = lax.axis_size("attn")
    pair = lax.axis_size("ffn")
    span = attn // EXPERTS

    def over_experts(value, shift):
        return lax.ppermute(value, "attn", [(i, (i + shift * span) % attn) for i in range(attn)])

    def over_span(value, shift):
        return lax.ppermute(value, "attn", [(i, i // span * span + (i + shift) % span) for i in range(attn)])

    def over_pair(value, shift):
        return lax.ppermute(value, "ffn", [(i, (i + shift) % pair) for i in range(pair)])

    part = width // IN_CHUNKS
    gathered = []
    for chunk in range(IN_CHUNKS):
        own = tokens[:, chunk * part:(chunk + 1) * part]
        column = [own] + [over_experts(own, s) for s in range(1, EXPERTS)]
        plane = column + [over_span(b, t) for t in range(1, span) for b in column]
        gathered.append(plane + [over_pair(b, p) for p in range(1, pair) for b in plane])

    sums = ()
    for chunk in range(IN_CHUNKS):
        sums = gate_up(gathered[chunk], gate_weight, up_weight, sums, chunk, IN_CHUNKS)
    hidden = sums

    parts = []
    for chunk in range(OUT_CHUNKS):
        keep, *sends = down(hidden, down_weight, chunk, OUT_CHUNKS, pair)
        received = [over_pair(b, -p) for p, b in enumerate(sends, 1)]
        keep, *sends = add_split(keep, received, span)
        received = [over_span(b, -t) for t, b in enumerate(sends, 1)]
        keep, *sends = add_split(keep, received, EXPERTS)
        parts.append([keep] + [over_experts(b, -s) for s, b in enumerate(sends, 1)])
    own_expert = (lax.axis_index("attn") // span).astype(jnp.int32).reshape(1)
    return combine(own_expert, expert_ids, route_weights, parts)


def solution(mesh):
    return jax.shard_map(
        local,
        mesh=mesh,
        in_specs=(
            P(("groups", "attn", "ffn"), None),
            P(("groups", "attn", "ffn"), None),
            P(("groups", "attn", "ffn"), None),
            P(None, ("attn", "ffn")),
            P(None, ("attn", "ffn")),
            P(("attn", "ffn"), None),
        ),
        out_specs=P(("groups", "attn", "ffn"), None),
        check_vma=False,
    )
```

```python
import functools

import jax
import jax.numpy as jnp
from jax import lax
from jax.experimental import pallas as pl
from jax.experimental.pallas import tpu as pltpu
from jax.sharding import PartitionSpec as P

EXPERTS = 4
OUT_CHUNKS = 2
N_BLOCK = 256
C_BLOCK = 512
EXCHANGE_FLOPS = 20_000_000_000


def params(mib=8):
    return pltpu.CompilerParams(vmem_limit_bytes=mib * 1024 * 1024)


def cost(flops):
    return pl.CostEstimate(flops=flops, bytes_accessed=0, transcendentals=0)


def block_of(width, most):
    size = most
    while width % size:
        size -= 128
    return size


def in_vmem(value):
    return pltpu.with_memory_space_constraint(value, pltpu.VMEM)


def joined(refs):
    return jnp.concatenate([ref[...].astype(jnp.float32) for ref in refs], axis=0)


def stack_kernel(*refs):
    refs[-1][...] = joined(refs[:-1]).astype(jnp.bfloat16)


def stack(values, flops=0):
    rows = sum(v.shape[0] for v in values)
    return pl.pallas_call(
        stack_kernel,
        out_shape=jax.ShapeDtypeStruct((rows, values[0].shape[1]), jnp.bfloat16),
        compiler_params=params(),
        cost_estimate=cost(flops),
        name="stack",
    )(*values)


def gate_up_kernel(n_block, *refs):
    rows_in, (gate_ref, up_ref, hidden_ref, rows_ref) = refs[:-4], refs[-4:]
    width = rows_ref.shape[1]
    piece = block_of(width, 1024)
    for k in range(0, width, piece):
        rows_ref[:, k:k + piece] = joined([ref.at[:, k:k + piece] for ref in rows_in]).astype(jnp.bfloat16)

    def step(n, carry):
        columns = pl.ds(pl.multiple_of(n * n_block, n_block), n_block)
        gate = jnp.dot(rows_ref[...], gate_ref[:, columns], preferred_element_type=jnp.float32)
        up = jnp.dot(rows_ref[...], up_ref[:, columns], preferred_element_type=jnp.float32)
        hidden_ref[:, columns] = (gate / (1.0 + jnp.exp(-gate)) * up).astype(jnp.bfloat16)
        return carry

    lax.fori_loop(0, gate_ref.shape[1] // n_block, step, 0)


def gate_up(rows, gate_weight, up_weight):
    total = sum(r.shape[0] for r in rows)
    width, units = gate_weight.shape
    return pl.pallas_call(
        functools.partial(gate_up_kernel, block_of(units, N_BLOCK)),
        in_specs=[pl.BlockSpec(memory_space=pltpu.VMEM)] * (len(rows) + 2),
        out_shape=jax.ShapeDtypeStruct((total, units), jnp.bfloat16),
        scratch_shapes=[pltpu.VMEM((total, width), jnp.bfloat16)],
        compiler_params=params(12),
        cost_estimate=cost(4 * total * width * units),
        name="gate_up",
    )(*rows, in_vmem(gate_weight), in_vmem(up_weight))


def down_kernel(offset, c_block, hidden_ref, down_ref, keep_ref, *send_refs):
    count, width = keep_ref.shape

    def step(c, carry):
        start = pl.multiple_of(c * c_block, c_block)
        value = jnp.dot(hidden_ref[...], down_ref[:, pl.ds(offset + start, c_block)], preferred_element_type=jnp.float32)
        keep_ref[:, pl.ds(start, c_block)] = value[:count]
        for i, ref in enumerate(send_refs):
            ref[:, pl.ds(start, c_block)] = value[(i + 1) * count:(i + 2) * count].astype(jnp.bfloat16)
        return carry

    lax.fori_loop(0, width // c_block, step, 0)


def down(hidden, down_weight, chunk, pair):
    total, units = hidden.shape
    width = down_weight.shape[1] // OUT_CHUNKS
    part = total // pair
    return pl.pallas_call(
        functools.partial(down_kernel, chunk * width, block_of(width, C_BLOCK)),
        in_specs=[pl.BlockSpec(memory_space=pltpu.VMEM)] * 2,
        out_shape=[jax.ShapeDtypeStruct((part, width), jnp.float32)]
        + [jax.ShapeDtypeStruct((part, width), jnp.bfloat16)] * (pair - 1),
        compiler_params=params(),
        cost_estimate=cost(2 * total * width * units),
        name="down",
    )(hidden, in_vmem(down_weight))


def pair_sum_kernel(chunks, each, *refs):
    ins, outs = refs[:chunks * each], refs[chunks * each:]
    rows = outs[0].shape[0]
    width = ins[0].shape[1]
    for chunk in range(chunks):
        first, *others = ins[chunk * each:(chunk + 1) * each]
        for i, ref in enumerate(outs):
            part = slice(i * rows, (i + 1) * rows)
            value = first[part, :]
            for other in others:
                value += other[part, :].astype(jnp.float32)
            ref[:, chunk * width:(chunk + 1) * width] = value.astype(ref.dtype)


def pair_sum(groups, rows):
    each = len(groups[0])
    total, width = groups[0][0].shape
    count = total // rows
    shape = (rows, width * len(groups))
    return pl.pallas_call(
        functools.partial(pair_sum_kernel, len(groups), each),
        out_shape=[jax.ShapeDtypeStruct(shape, jnp.float32 if i < EXPERTS else jnp.bfloat16) for i in range(count)],
        compiler_params=params(16),
        name="pair_sum",
    )(*[a for g in groups for a in g])


def span_sum_kernel(*refs):
    value = refs[0][...]
    for ref in refs[1:-1]:
        value += ref[...].astype(jnp.float32)
    refs[-1][...] = value.astype(refs[-1].dtype)


def span_sum(arrays):
    return pl.pallas_call(
        span_sum_kernel,
        out_shape=jax.ShapeDtypeStruct(arrays[0].shape, jnp.bfloat16),
        compiler_params=params(),
        name="span_sum",
    )(*arrays)


def combine_kernel(own_count, own_expert, ids_ref, weights_ref, *refs):
    out_ref = refs[-1]
    ids, weights = ids_ref[...], weights_ref[...]

    def coeff(s):
        expert = lax.rem(own_expert[0] + s, EXPERTS)
        return jnp.sum(jnp.where(ids == expert, weights, 0.0), axis=1, keepdims=True)

    own = refs[0][...]
    for ref in refs[1:own_count]:
        own += ref[...].astype(jnp.float32)
    value = coeff(0) * own
    for s, ref in enumerate(refs[own_count:-1], 1):
        value += coeff(s) * ref[...].astype(jnp.float32)
    out_ref[...] = value.astype(jnp.bfloat16)


def combine(own_expert, ids, weights, own, others):
    arrays = list(own) + list(others)
    return pl.pallas_call(
        functools.partial(combine_kernel, len(own)),
        in_specs=[pl.BlockSpec(memory_space=pltpu.SMEM)] + [pl.BlockSpec(memory_space=pltpu.VMEM)] * (2 + len(arrays)),
        out_shape=jax.ShapeDtypeStruct(own[0].shape, jnp.bfloat16),
        compiler_params=params(),
        name="combine",
    )(own_expert, ids, weights, *arrays)


def local(tokens, expert_ids, route_weights, gate_weight, up_weight, down_weight):
    rows = tokens.shape[0]
    attn = lax.axis_size("attn")
    pair = lax.axis_size("ffn")
    span = attn // EXPERTS

    def over_experts(value, shift):
        return lax.ppermute(value, "attn", [(i, (i + shift * span) % attn) for i in range(attn)])

    def over_span(value, shift):
        return lax.ppermute(value, "attn", [(i, i // span * span + (i + shift) % span) for i in range(attn)])

    def over_pair(value, shift):
        return lax.ppermute(value, "ffn", [(i, (i + shift) % pair) for i in range(pair)])

    own = stack([tokens], EXCHANGE_FLOPS)
    column = [own] + [over_experts(own, s) for s in range(1, EXPERTS)]
    plane, groups = list(column), [stack(column)]
    for t in range(1, span):
        blocks = [over_span(b, t) for b in column]
        plane += blocks
        groups += [stack(blocks[:-1]), blocks[-1]]
    gathered = plane + [over_pair(g, p) for p in range(1, pair) for g in groups]

    hidden = gate_up(gathered, gate_weight, up_weight)

    halves = []
    for chunk in range(OUT_CHUNKS):
        keep, *sends = down(hidden, down_weight, chunk, pair)
        halves.append([keep] + [over_pair(b, -p) for p, b in enumerate(sends, 1)])
    blocks = pair_sum(halves, rows)
    sums = []
    for s in reversed(range(EXPERTS)):
        sums.append([blocks[s]] + [over_span(blocks[t * EXPERTS + s], -t) for t in range(1, span)])
    sums.reverse()
    others = [over_experts(span_sum(sums[s]), -s) for s in reversed(range(1, EXPERTS))]
    others.reverse()
    own_expert = (lax.axis_index("attn") // span).astype(jnp.int32).reshape(1)
    return combine(own_expert, expert_ids, route_weights, sums[0], others)


def solution(mesh):
    return jax.shard_map(
        local,
        mesh=mesh,
        in_specs=(
            P(("groups", "attn", "ffn"), None),
            P(("groups", "attn", "ffn"), None),
            P(("groups", "attn", "ffn"), None),
            P(None, ("attn", "ffn")),
            P(None, ("attn", "ffn")),
            P(("attn", "ffn"), None),
        ),
        out_specs=P(("groups", "attn", "ffn"), None),
        check_vma=False,
    )
```

```python
import functools

import jax
import jax.numpy as jnp
from jax import lax
from jax.experimental import pallas as pl
from jax.experimental.pallas import tpu as pltpu
from jax.sharding import PartitionSpec as P

EXPERTS = 4
LANES = 128
OUT_CHUNKS = 2
N_BLOCK = 256
EXCHANGE_FLOPS = 20_000_000_000
DOWN_FLOPS = 6_000_000_000


def params(mib=8):
    return pltpu.CompilerParams(vmem_limit_bytes=mib * 1024 * 1024)


def cost(flops):
    return pl.CostEstimate(flops=flops, bytes_accessed=0, transcendentals=0)


def block_of(width, most):
    size = most
    while width % size:
        size -= 128
    return size


def in_vmem(value):
    return pltpu.with_memory_space_constraint(value, pltpu.VMEM)


def joined(refs):
    return jnp.concatenate([ref[...].astype(jnp.float32) for ref in refs], axis=0)


def stack_kernel(*refs):
    refs[-1][...] = joined(refs[:-1]).astype(jnp.bfloat16)


def stack(values, flops=0):
    rows = sum(v.shape[0] for v in values)
    return pl.pallas_call(
        stack_kernel,
        out_shape=jax.ShapeDtypeStruct((rows, values[0].shape[1]), jnp.bfloat16),
        compiler_params=params(),
        cost_estimate=cost(flops),
        name="stack",
    )(*values)


def gate_up_kernel(n_block, *refs):
    rows_in, (gate_ref, up_ref, hidden_ref, rows_ref) = refs[:-4], refs[-4:]
    width = rows_ref.shape[1]
    piece = block_of(width, 1024)
    for k in range(0, width, piece):
        rows_ref[:, k:k + piece] = joined([ref.at[:, k:k + piece] for ref in rows_in]).astype(jnp.bfloat16)

    for n in range(0, gate_ref.shape[1], n_block):
        columns = slice(n, n + n_block)
        gate = jnp.dot(rows_ref[...], gate_ref[:, columns], preferred_element_type=jnp.float32)
        up = jnp.dot(rows_ref[...], up_ref[:, columns], preferred_element_type=jnp.float32)
        hidden_ref[:, columns] = (gate / (1.0 + jnp.exp(-gate)) * up).astype(jnp.bfloat16)


def gate_up(rows, gate_weight, up_weight):
    total = sum(r.shape[0] for r in rows)
    width, units = gate_weight.shape
    return pl.pallas_call(
        functools.partial(gate_up_kernel, block_of(units, N_BLOCK)),
        in_specs=[pl.BlockSpec(memory_space=pltpu.VMEM)] * (len(rows) + 2),
        out_shape=jax.ShapeDtypeStruct((total, units), jnp.bfloat16),
        scratch_shapes=[pltpu.VMEM((total, width), jnp.bfloat16)],
        compiler_params=params(12),
        cost_estimate=cost(4 * total * width * units),
        name="gate_up",
    )(*rows, in_vmem(gate_weight), in_vmem(up_weight))


def down_kernel(offset, c_block, hidden_ref, down_ref, keep_ref, *send_refs):
    count, width = keep_ref.shape

    for c in range(0, width, c_block):
        columns = slice(c, c + c_block)
        value = jnp.dot(hidden_ref[...], down_ref[:, offset + c:offset + c + c_block], preferred_element_type=jnp.float32)
        keep_ref[:, columns] = value[:count]
        for i, ref in enumerate(send_refs):
            ref[:, columns] = value[(i + 1) * count:(i + 2) * count].astype(jnp.bfloat16)


def down(hidden, down_weight, chunk, pair):
    total, units = hidden.shape
    width = down_weight.shape[1] // OUT_CHUNKS
    part = total // pair
    return pl.pallas_call(
        functools.partial(down_kernel, chunk * width, block_of(width, N_BLOCK)),
        in_specs=[pl.BlockSpec(memory_space=pltpu.VMEM)] * 2,
        out_shape=[jax.ShapeDtypeStruct((part, width), jnp.float32)]
        + [jax.ShapeDtypeStruct((part, width), jnp.bfloat16)] * (pair - 1),
        compiler_params=params(),
        cost_estimate=cost(DOWN_FLOPS),
        name="down",
    )(hidden, in_vmem(down_weight))


def pair_sum_kernel(chunks, each, *refs):
    ins, outs = refs[:chunks * each], refs[chunks * each:]
    rows = outs[0].shape[0]
    width = ins[0].shape[1]
    for chunk in range(chunks):
        first, *others = ins[chunk * each:(chunk + 1) * each]
        for i, ref in enumerate(outs):
            part = slice(i * rows, (i + 1) * rows)
            value = first[part, :]
            for other in others:
                value += other[part, :].astype(jnp.float32)
            ref[:, chunk * width:(chunk + 1) * width] = value.astype(ref.dtype)


def pair_sum(groups, rows):
    each = len(groups[0])
    total, width = groups[0][0].shape
    count = total // rows
    shape = (rows, width * len(groups))
    return pl.pallas_call(
        functools.partial(pair_sum_kernel, len(groups), each),
        out_shape=[jax.ShapeDtypeStruct(shape, jnp.float32 if i < EXPERTS else jnp.bfloat16) for i in range(count)],
        compiler_params=params(16),
        name="pair_sum",
    )(*[a for g in groups for a in g])


def span_sum_kernel(*refs):
    value = refs[0][...]
    for ref in refs[1:-1]:
        value += ref[...].astype(jnp.float32)
    refs[-1][...] = value.astype(refs[-1].dtype)


def span_sum(arrays):
    return pl.pallas_call(
        span_sum_kernel,
        out_shape=jax.ShapeDtypeStruct(arrays[0].shape, jnp.bfloat16),
        compiler_params=params(),
        name="span_sum",
    )(*arrays)


def coefficients_kernel(own_expert, ids_ref, weights_ref, out_ref):
    ids, weights = ids_ref[...], weights_ref[...]
    rows = ids.shape[1]
    square = (rows, rows)
    diagonal = lax.broadcasted_iota(jnp.int32, square, 0) == lax.broadcasted_iota(jnp.int32, square, 1)
    for s in range(EXPERTS):
        expert = lax.rem(own_expert[0] + s, EXPERTS)
        chosen = jnp.sum(jnp.where(ids == expert, weights, 0.0), axis=0, keepdims=True)
        column = jnp.sum(jnp.where(diagonal, jnp.broadcast_to(chosen, square), 0.0), axis=1, keepdims=True)
        out_ref[:, s * LANES:(s + 1) * LANES] = jnp.broadcast_to(column, (rows, LANES))


def coefficients(own_expert, ids, weights):
    return pl.pallas_call(
        coefficients_kernel,
        in_specs=[pl.BlockSpec(memory_space=pltpu.SMEM)] + [pl.BlockSpec(memory_space=pltpu.VMEM)] * 2,
        out_shape=jax.ShapeDtypeStruct((ids.shape[0], EXPERTS * LANES), jnp.float32),
        compiler_params=params(),
        cost_estimate=cost(0),
        name="coefficients",
    )(own_expert, ids.T, weights.T)


def combine_kernel(own_count, coeff_ref, *refs):
    out_ref = refs[-1]

    def coeff(s):
        return coeff_ref[:, s * LANES:s * LANES + 1]

    own = refs[0][...]
    for ref in refs[1:own_count]:
        own += ref[...].astype(jnp.float32)
    value = coeff(0) * own
    for s, ref in enumerate(refs[own_count:-1], 1):
        value += coeff(s) * ref[...].astype(jnp.float32)
    out_ref[...] = value.astype(jnp.bfloat16)


def combine(coeffs, own, others):
    return pl.pallas_call(
        functools.partial(combine_kernel, len(own)),
        out_shape=jax.ShapeDtypeStruct(own[0].shape, jnp.bfloat16),
        compiler_params=params(),
        name="combine",
    )(coeffs, *own, *others)


def local(tokens, expert_ids, route_weights, gate_weight, up_weight, down_weight):
    rows = tokens.shape[0]
    attn = lax.axis_size("attn")
    pair = lax.axis_size("ffn")
    span = attn // EXPERTS

    def over_experts(value, shift):
        return lax.ppermute(value, "attn", [(i, (i + shift * span) % attn) for i in range(attn)])

    def over_span(value, shift):
        return lax.ppermute(value, "attn", [(i, i // span * span + (i + shift) % span) for i in range(attn)])

    def over_pair(value, shift):
        return lax.ppermute(value, "ffn", [(i, (i + shift) % pair) for i in range(pair)])

    own_expert = (lax.axis_index("attn") // span).astype(jnp.int32).reshape(1)
    coeffs = coefficients(own_expert, expert_ids, route_weights)
    own = stack([tokens], EXCHANGE_FLOPS)
    column = [own] + [over_experts(own, s) for s in range(1, EXPERTS)]
    plane, groups = list(column), [stack(column)]
    for t in range(1, span):
        blocks = [over_span(b, t) for b in column]
        plane += blocks
        groups.append(stack(blocks))
    gathered = plane + [over_pair(g, p) for p in range(1, pair) for g in groups]

    hidden = gate_up(gathered, gate_weight, up_weight)

    halves = []
    for chunk in range(OUT_CHUNKS):
        keep, *sends = down(hidden, down_weight, chunk, pair)
        halves.append([keep] + [over_pair(b, -p) for p, b in enumerate(sends, 1)])
    blocks = pair_sum(halves, rows)
    sums = []
    for s in reversed(range(EXPERTS)):
        sums.append([blocks[s]] + [over_span(blocks[t * EXPERTS + s], -t) for t in range(1, span)])
    sums.reverse()
    others = [over_experts(span_sum(sums[s]), -s) for s in reversed(range(1, EXPERTS))]
    others.reverse()
    return combine(coeffs, sums[0], others)


def solution(mesh):
    return jax.shard_map(
        local,
        mesh=mesh,
        in_specs=(
            P(("groups", "attn", "ffn"), None),
            P(("groups", "attn", "ffn"), None),
            P(("groups", "attn", "ffn"), None),
            P(None, ("attn", "ffn")),
            P(None, ("attn", "ffn")),
            P(("attn", "ffn"), None),
        ),
        out_specs=P(("groups", "attn", "ffn"), None),
        check_vma=False,
    )
```

```python
import functools

import jax
import jax.numpy as jnp
from jax import lax
from jax.experimental import pallas as pl
from jax.experimental.pallas import tpu as pltpu
from jax.sharding import PartitionSpec as P

EXPERTS = 4
LANES = 128
RETURN_ORDER = (2, 3, 1)
N_BLOCK = 256
EXCHANGE_FLOPS = 20_000_000_000
DOWN_FLOPS = 6_000_000_000


def params(mib=8):
    return pltpu.CompilerParams(vmem_limit_bytes=mib * 1024 * 1024)


def cost(flops):
    return pl.CostEstimate(flops=flops, bytes_accessed=0, transcendentals=0)


def block_of(width, most):
    size = most
    while width % size:
        size -= 128
    return size


def in_vmem(value):
    return pltpu.with_memory_space_constraint(value, pltpu.VMEM)


def joined(refs):
    return jnp.concatenate([ref[...].astype(jnp.float32) for ref in refs], axis=0)


def stack_kernel(*refs):
    refs[-1][...] = joined(refs[:-1]).astype(jnp.bfloat16)


def stack(values, flops=0):
    rows = sum(v.shape[0] for v in values)
    return pl.pallas_call(
        stack_kernel,
        out_shape=jax.ShapeDtypeStruct((rows, values[0].shape[1]), jnp.bfloat16),
        compiler_params=params(),
        cost_estimate=cost(flops),
        name="stack",
    )(*values)


def unpacked(refs, out_ref, rows):
    total, width = out_ref.shape
    tail = width // rows
    blocks = (total // rows, rows, tail)
    row = lax.broadcasted_iota(jnp.int32, blocks, 1)
    ends = jnp.zeros(blocks, jnp.float32)
    for i in range(rows - 1):
        piece = joined([ref.at[:, i * tail:(i + 1) * tail] for ref in refs])
        out_ref[:, i * tail:(i + 1) * tail] = piece.astype(jnp.bfloat16)
        ends = jnp.where(row == i, jnp.broadcast_to(piece.reshape(blocks)[:, rows - 1:, :], blocks), ends)
    out_ref[:, width - tail:] = ends.reshape(total, tail).astype(jnp.bfloat16)


def unpack_kernel(rows, *refs):
    unpacked(refs[:-1], refs[-1], rows)


def unpack(values, rows, width):
    total = sum(v.shape[0] for v in values)
    return pl.pallas_call(
        functools.partial(unpack_kernel, rows),
        out_shape=jax.ShapeDtypeStruct((total, width), jnp.bfloat16),
        compiler_params=params(),
        cost_estimate=cost(1_000_000_000),
        name="unpack",
    )(*values)


def gate_up_kernel(n_block, rows, first_ref, *refs):
    rows_in, (gate_ref, up_ref, hidden_ref, rows_ref) = refs[:-4], refs[-4:]
    count = first_ref.shape[0]
    rows_ref[:count, :] = first_ref[...]
    if rows_in:
        unpacked(rows_in, rows_ref.at[count:, :], rows)
    for n in range(0, gate_ref.shape[1], n_block):
        columns = slice(n, n + n_block)
        gate = jnp.dot(rows_ref[...], gate_ref[:, columns], preferred_element_type=jnp.float32)
        up = jnp.dot(rows_ref[...], up_ref[:, columns], preferred_element_type=jnp.float32)
        hidden_ref[:, columns] = (gate / (1.0 + jnp.exp(-gate)) * up).astype(jnp.bfloat16)


def gate_up(first, blocks, gate_weight, up_weight, rows):
    total = sum(r.shape[0] for r in [first] + blocks)
    width, units = gate_weight.shape
    return pl.pallas_call(
        functools.partial(gate_up_kernel, block_of(units, N_BLOCK), rows),
        in_specs=[pl.BlockSpec(memory_space=pltpu.VMEM)] * (len(blocks) + 3),
        out_shape=jax.ShapeDtypeStruct((total, units), jnp.bfloat16),
        scratch_shapes=[pltpu.VMEM((total, width), jnp.bfloat16)],
        compiler_params=params(12),
        cost_estimate=cost(4 * total * width * units),
        name="gate_up",
    )(first, *blocks, in_vmem(gate_weight), in_vmem(up_weight))


def down_kernel(rows, first, pair, hidden_ref, down_ref, *refs):
    if first:
        keep_ref, *send_refs, ends_ref = refs
    else:
        ends_ref, keep_ref, *send_refs = refs
    count, width = keep_ref.shape
    tail = down_ref.shape[1] // rows
    offset = 0 if first else (rows - 1) * tail - width
    blocks = (hidden_ref.shape[0] // rows, rows, tail)
    last = lax.broadcasted_iota(jnp.int32, blocks, 1) == rows - 1
    if first:
        ends_ref[...] = jnp.dot(hidden_ref[...], down_ref[:, (rows - 1) * tail:], preferred_element_type=jnp.float32)
    for c in range(0, width, tail):
        start = offset + c
        value = jnp.dot(hidden_ref[...], down_ref[:, start:start + tail], preferred_element_type=jnp.float32).reshape(blocks)
        i = start // tail
        moved = ends_ref[...].reshape(blocks)[:, i:i + 1, :]
        value = jnp.where(last, jnp.broadcast_to(moved, blocks), value).reshape(blocks[0] * rows, tail)
        columns = slice(c, c + tail)
        keep_ref[:, columns] = value[:count]
        for p, ref in enumerate(send_refs, 1):
            ref[:, columns] = value[p * count:(p + 1) * count].astype(jnp.bfloat16)


def down(hidden, down_weight, ends, pair, rows):
    total, units = hidden.shape
    tail = down_weight.shape[1] // rows
    first = not ends
    width = tail * ((rows - 1) // 2 if first else rows - 1 - (rows - 1) // 2)
    part = total // pair
    return pl.pallas_call(
        functools.partial(down_kernel, rows, first, pair),
        in_specs=[pl.BlockSpec(memory_space=pltpu.VMEM)] * (2 + len(ends)),
        out_shape=[jax.ShapeDtypeStruct((part, width), jnp.float32)]
        + [jax.ShapeDtypeStruct((part, width), jnp.bfloat16)] * (pair - 1)
        + [jax.ShapeDtypeStruct((total, tail), jnp.float32)] * first,
        compiler_params=params(),
        cost_estimate=cost(DOWN_FLOPS),
        name="down",
    )(hidden, in_vmem(down_weight), *ends)


def pair_sum_kernel(chunks, each, *refs):
    ins, outs = refs[:chunks * each], refs[chunks * each:]
    rows = outs[0].shape[0]
    start = 0
    for chunk in range(chunks):
        first, *others = ins[chunk * each:(chunk + 1) * each]
        columns = slice(start, start + first.shape[1])
        start = columns.stop
        for i, ref in enumerate(outs):
            part = slice(i * rows, (i + 1) * rows)
            value = first[part, :]
            for other in others:
                value += other[part, :].astype(jnp.float32)
            ref[:, columns] = value.astype(ref.dtype)


def pair_sum(groups, rows):
    each = len(groups[0])
    count = groups[0][0].shape[0] // rows
    shape = (rows, sum(g[0].shape[1] for g in groups))
    return pl.pallas_call(
        functools.partial(pair_sum_kernel, len(groups), each),
        out_shape=[jax.ShapeDtypeStruct(shape, jnp.float32 if i < EXPERTS else jnp.bfloat16) for i in range(count)],
        compiler_params=params(16),
        name="pair_sum",
    )(*[a for g in groups for a in g])


def span_sum_kernel(*refs):
    value = refs[0][...]
    for ref in refs[1:-1]:
        value += ref[...].astype(jnp.float32)
    refs[-1][...] = value.astype(refs[-1].dtype)


def span_sum(arrays):
    return pl.pallas_call(
        span_sum_kernel,
        out_shape=jax.ShapeDtypeStruct(arrays[0].shape, jnp.bfloat16),
        compiler_params=params(),
        name="span_sum",
    )(*arrays)


def pack_kernel(own_expert, tokens_ref, ids_ref, weights_ref, sides_ref, *packed_refs):
    ids, weights = ids_ref[...], weights_ref[...]
    rows, width = tokens_ref.shape
    tail = width // rows
    square = (rows, rows)
    row, column = lax.broadcasted_iota(jnp.int32, square, 0), lax.broadcasted_iota(jnp.int32, square, 1)
    last = lax.broadcasted_iota(jnp.int32, (rows, tail), 0) == rows - 1
    here = tokens_ref[...].astype(jnp.float32)
    below = pltpu.roll(here, rows - 1, 0)
    for s, packed_ref in enumerate(packed_refs):
        expert = lax.bitwise_xor(own_expert[0], s)
        named = ids == expert
        chosen = jnp.sum(jnp.where(named, weights, 0.0), axis=0, keepdims=True)
        coeff = jnp.sum(jnp.where(row == column, jnp.broadcast_to(chosen, square), 0.0), axis=1, keepdims=True)
        unnamed = 1.0 - jnp.sum(jnp.where(named, 1.0, 0.0), axis=0, keepdims=True)
        shift = jnp.max(jnp.where(column <= row, jnp.broadcast_to(unnamed, square), 0.0), axis=1, keepdims=True)
        sides_ref[:, s * LANES:(s + 1) * LANES] = jnp.broadcast_to(coeff, (rows, LANES))
        sides_ref[:, (EXPERTS + s) * LANES:(EXPERTS + s + 1) * LANES] = jnp.broadcast_to(shift, (rows, LANES))
        kept = jnp.where(shift > 0.5, below, here)
        for i in range(rows - 1):
            moved = jnp.broadcast_to(kept[i:i + 1, width - tail:], (rows, tail))
            piece = jnp.where(last, moved, kept[:, i * tail:(i + 1) * tail])
            packed_ref[:, i * tail:(i + 1) * tail] = piece.astype(jnp.bfloat16)


def pack(own_expert, tokens, ids, weights):
    rows, width = tokens.shape
    packed = jax.ShapeDtypeStruct((rows, width - width // rows), jnp.bfloat16)
    return pl.pallas_call(
        pack_kernel,
        in_specs=[pl.BlockSpec(memory_space=pltpu.SMEM)] + [pl.BlockSpec(memory_space=pltpu.VMEM)] * 3,
        out_shape=[jax.ShapeDtypeStruct((rows, 2 * EXPERTS * LANES), jnp.float32)] + [packed] * EXPERTS,
        compiler_params=params(),
        cost_estimate=cost(EXCHANGE_FLOPS),
        name="pack",
    )(own_expert, tokens, ids.T, weights.T)


def combine_kernel(own_count, sides_ref, *refs):
    out_ref = refs[-1]
    rows, width = out_ref.shape
    tail = width // rows
    own = refs[0][...]
    for ref in refs[1:own_count]:
        own += ref[...].astype(jnp.float32)
    row = lax.broadcasted_iota(jnp.int32, (rows, tail), 0)
    parts = []
    others = [ref[...].astype(jnp.float32) for ref in refs[own_count:-1]]
    for s, packed in zip((0,) + RETURN_ORDER, [own] + others):
        coeff = sides_ref[:, s * LANES:s * LANES + 1]
        shifted = sides_ref[:, (EXPERTS + s) * LANES:(EXPERTS + s) * LANES + 1] > 0.5
        ends = jnp.zeros((rows, tail), jnp.float32)
        for i in range(rows - 1):
            ends = jnp.where(row == i, jnp.broadcast_to(packed[rows - 1:, i * tail:(i + 1) * tail], (rows, tail)), ends)
        whole = jnp.concatenate([packed, ends], axis=1)
        parts.append(coeff * jnp.where(shifted, pltpu.roll(whole, 1, 0), whole))
    out_ref[...] = sum(parts[1:], parts[0]).astype(jnp.bfloat16)


def combine(sides, own, others, width):
    return pl.pallas_call(
        functools.partial(combine_kernel, len(own)),
        out_shape=jax.ShapeDtypeStruct((own[0].shape[0], width), jnp.bfloat16),
        compiler_params=params(),
        name="combine",
    )(sides, *own, *others)


def local(tokens, expert_ids, route_weights, gate_weight, up_weight, down_weight):
    rows, width = tokens.shape
    attn = lax.axis_size("attn")
    pair = lax.axis_size("ffn")
    span = attn // EXPERTS

    def over_experts(value, other):
        return lax.ppermute(value, "attn", [(i, (i // span ^ other) * span + i % span) for i in range(attn)])

    def over_span(value, shift):
        return lax.ppermute(value, "attn", [(i, i // span * span + (i + shift) % span) for i in range(attn)])

    def over_pair(value, shift):
        return lax.ppermute(value, "ffn", [(i, (i + shift) % pair) for i in range(pair)])

    own_expert = (lax.axis_index("attn") // span).astype(jnp.int32).reshape(1)
    sides, *packed = pack(own_expert, tokens, expert_ids, route_weights)
    column = packed[:1] + [over_experts(packed[s], s) for s in range(1, EXPERTS)]
    plane, groups = list(column), [stack(column)]
    for t in range(1, span):
        blocks = [over_span(b, t) for b in column]
        plane += blocks
        groups.append(stack(blocks))
    others = [over_pair(g, p) for p in range(1, pair) for g in groups]
    hidden = gate_up(unpack(plane, rows, width), others, gate_weight, up_weight, rows)

    halves, ends = [], []
    for _ in range(2):
        keep, *sends = down(hidden, down_weight, ends, pair, rows)
        if not ends:
            ends = [sends.pop()]
        halves.append([keep] + [over_pair(b, -p) for p, b in enumerate(sends, 1)])
    blocks = pair_sum(halves, rows)
    sums = [[blocks[s]] + [over_span(blocks[t * EXPERTS + s], -t) for t in range(1, span)] for s in range(EXPERTS)]
    returned = [over_experts(span_sum(sums[s]), s) for s in RETURN_ORDER]
    return combine(sides, sums[0], returned, width)


def solution(mesh):
    return jax.shard_map(
        local,
        mesh=mesh,
        in_specs=(
            P(("groups", "attn", "ffn"), None),
            P(("groups", "attn", "ffn"), None),
            P(("groups", "attn", "ffn"), None),
            P(None, ("attn", "ffn")),
            P(None, ("attn", "ffn")),
            P(("attn", "ffn"), None),
        ),
        out_specs=P(("groups", "attn", "ffn"), None),
        check_vma=False,
    )
```

```python
import functools

import jax
import jax.numpy as jnp
from jax import lax
from jax.experimental import pallas as pl
from jax.experimental.pallas import tpu as pltpu
from jax.sharding import PartitionSpec as P

EXPERTS = 4
LANES = 128
RETURN_ORDER = (1, 3, 2)
N_BLOCK = 256
EXCHANGE_FLOPS = 20_000_000_000


def params(mib=4):
    return pltpu.CompilerParams(vmem_limit_bytes=mib * 1024 * 1024)


def cost(flops):
    return pl.CostEstimate(flops=flops, bytes_accessed=0, transcendentals=0)


def block_of(width, most):
    size = most
    while width % size:
        size -= 128
    return size


def in_vmem(value):
    return pltpu.with_memory_space_constraint(value, pltpu.VMEM)


def joined(refs):
    return jnp.concatenate([ref[...].astype(jnp.float32) for ref in refs], axis=0)


def stack_kernel(count, *refs):
    refs[-1][...] = joined(refs[:count]).astype(jnp.bfloat16)


def stack(values, after):
    rows = sum(v.shape[0] for v in values)
    return pl.pallas_call(
        functools.partial(stack_kernel, len(values)),
        in_specs=[pl.BlockSpec(memory_space=pltpu.VMEM)] * len(values) + [pl.BlockSpec(memory_space=pl.ANY)] * len(after),
        out_shape=jax.ShapeDtypeStruct((rows, values[0].shape[1]), jnp.bfloat16),
        compiler_params=params(),
        cost_estimate=cost(0),
        name="stack",
    )(*values, *after)


def unpacked(refs, out_ref, rows):
    total, width = out_ref.shape
    tail = width // rows
    blocks = (total // rows, rows, tail)
    row = lax.broadcasted_iota(jnp.int32, blocks, 1)
    ends = jnp.zeros(blocks, jnp.float32)
    for i in range(rows - 1):
        piece = joined([ref.at[:, i * tail:(i + 1) * tail] for ref in refs])
        out_ref[:, i * tail:(i + 1) * tail] = piece.astype(jnp.bfloat16)
        ends = jnp.where(row == i, jnp.broadcast_to(piece.reshape(blocks)[:, rows - 1:, :], blocks), ends)
    out_ref[:, width - tail:] = ends.reshape(total, tail).astype(jnp.bfloat16)


def gate_up_kernel(n_block, rows, *refs):
    rows_in, (gate_ref, up_ref, hidden_ref, rows_ref) = refs[:-4], refs[-4:]
    unpacked(rows_in, rows_ref, rows)
    for n in range(0, gate_ref.shape[1], n_block):
        columns = slice(n, n + n_block)
        gate = jnp.dot(rows_ref[...], gate_ref[:, columns], preferred_element_type=jnp.float32)
        up = jnp.dot(rows_ref[...], up_ref[:, columns], preferred_element_type=jnp.float32)
        hidden_ref[:, columns] = (gate / (1.0 + jnp.exp(-gate)) * up).astype(jnp.bfloat16)


def gate_up(blocks, gate_weight, up_weight, rows):
    total = sum(r.shape[0] for r in blocks)
    width, units = gate_weight.shape
    return pl.pallas_call(
        functools.partial(gate_up_kernel, block_of(units, N_BLOCK), rows),
        in_specs=[pl.BlockSpec(memory_space=pltpu.VMEM)] * (len(blocks) + 2),
        out_shape=jax.ShapeDtypeStruct((total, units), jnp.bfloat16),
        scratch_shapes=[pltpu.VMEM((total, width), jnp.bfloat16)],
        compiler_params=params(),
        cost_estimate=cost(4 * total * width * units),
        name="gate_up",
    )(*blocks, in_vmem(gate_weight), in_vmem(up_weight))


def down_kernel(rows, parts, *refs):
    hidden_refs, down_ref, outs = refs[:parts], refs[parts], refs[parts + 1:]
    count, width = outs[0].shape
    hidden = jnp.concatenate([ref[...] for ref in hidden_refs], axis=0)
    tail = down_ref.shape[1] // rows
    blocks = (hidden.shape[0] // rows, rows, tail)
    last = lax.broadcasted_iota(jnp.int32, blocks, 1) == rows - 1
    ends = jnp.dot(hidden, down_ref[:, width:], preferred_element_type=jnp.float32).reshape(blocks)
    for i in range(rows - 1):
        columns = slice(i * tail, (i + 1) * tail)
        value = jnp.dot(hidden, down_ref[:, columns], preferred_element_type=jnp.float32).reshape(blocks)
        value = jnp.where(last, jnp.broadcast_to(ends[:, i:i + 1, :], blocks), value).reshape(blocks[0] * rows, tail)
        for j, ref in enumerate(outs):
            ref[:, columns] = value[j * count:(j + 1) * count].astype(ref.dtype)


def down(hiddens, down_weight, pair, rows):
    total, units = hiddens[0].shape
    width = down_weight.shape[1] // rows * (rows - 1)
    shape = (total // pair, width)
    out_shape = [jax.ShapeDtypeStruct(shape, jnp.bfloat16 if p else jnp.float32) for _ in hiddens for p in range(pair)]
    outs = pl.pallas_call(
        functools.partial(down_kernel, rows, len(hiddens)),
        in_specs=[pl.BlockSpec(memory_space=pltpu.VMEM)] * (len(hiddens) + 1),
        out_shape=out_shape,
        compiler_params=params(),
        cost_estimate=cost(2 * total * len(hiddens) * width * units),
        name="down",
    )(*hiddens, in_vmem(down_weight))
    return [outs[i:i + pair] for i in range(0, len(outs), pair)]


def pair_sum_kernel(count, *refs):
    outs = refs[count:]
    rows = outs[0].shape[0]
    for i, out_ref in enumerate(outs):
        part = slice(i * rows, (i + 1) * rows)
        value = refs[0][part, :]
        for ref in refs[1:count]:
            value += ref[part, :].astype(jnp.float32)
        out_ref[...] = value.astype(out_ref.dtype)


def pair_sum(arrays, rows, dtype):
    total, width = arrays[0].shape
    return pl.pallas_call(
        functools.partial(pair_sum_kernel, len(arrays)),
        out_shape=[jax.ShapeDtypeStruct((rows, width), dtype)] * (total // rows),
        compiler_params=params(),
        name="pair_sum",
    )(*arrays)


def span_sum_kernel(*refs):
    value = refs[0][...]
    for ref in refs[1:-1]:
        value += ref[...].astype(jnp.float32)
    refs[-1][...] = value.astype(refs[-1].dtype)


def span_sum(arrays):
    return pl.pallas_call(
        span_sum_kernel,
        out_shape=jax.ShapeDtypeStruct(arrays[0].shape, jnp.bfloat16),
        compiler_params=params(),
        name="span_sum",
    )(*arrays)


def pack_kernel(own_expert, tokens_hbm, ids_hbm, weights_hbm, sides_ref, *refs):
    packed_refs, (tokens_ref, ids_ref, weights_ref, semaphores) = refs[:EXPERTS], refs[EXPERTS:]
    pairs = [(tokens_hbm, tokens_ref), (ids_hbm, ids_ref), (weights_hbm, weights_ref)]
    copies = [pltpu.make_async_copy(src, dst, semaphores.at[i]) for i, (src, dst) in enumerate(pairs)]
    for copy in copies:
        copy.start()
    for copy in copies:
        copy.wait()
    ids, weights = ids_ref[...], weights_ref[...]
    rows, width = tokens_ref.shape
    tail = width // rows
    square = (rows, rows)
    row, column = lax.broadcasted_iota(jnp.int32, square, 0), lax.broadcasted_iota(jnp.int32, square, 1)
    last = lax.broadcasted_iota(jnp.int32, (rows, tail), 0) == rows - 1
    here = tokens_ref[...].astype(jnp.float32)
    below = pltpu.roll(here, rows - 1, 0)
    for s, packed_ref in enumerate(packed_refs):
        expert = lax.bitwise_xor(own_expert[0], s)
        named = ids == expert
        chosen = jnp.sum(jnp.where(named, weights, 0.0), axis=0, keepdims=True)
        coeff = jnp.sum(jnp.where(row == column, jnp.broadcast_to(chosen, square), 0.0), axis=1, keepdims=True)
        unnamed = 1.0 - jnp.sum(jnp.where(named, 1.0, 0.0), axis=0, keepdims=True)
        shift = jnp.max(jnp.where(column <= row, jnp.broadcast_to(unnamed, square), 0.0), axis=1, keepdims=True)
        sides_ref[:, s * LANES:(s + 1) * LANES] = jnp.broadcast_to(coeff, (rows, LANES))
        sides_ref[:, (EXPERTS + s) * LANES:(EXPERTS + s + 1) * LANES] = jnp.broadcast_to(shift, (rows, LANES))
        kept = jnp.where(shift > 0.5, below, here)
        for i in range(rows - 1):
            moved = jnp.broadcast_to(kept[i:i + 1, width - tail:], (rows, tail))
            piece = jnp.where(last, moved, kept[:, i * tail:(i + 1) * tail])
            packed_ref[:, i * tail:(i + 1) * tail] = piece.astype(jnp.bfloat16)


def pack(own_expert, tokens, ids, weights):
    rows, width = tokens.shape
    packed = jax.ShapeDtypeStruct((rows, width - width // rows), jnp.bfloat16)
    inputs = [tokens, ids.T, weights.T]
    return pl.pallas_call(
        pack_kernel,
        in_specs=[pl.BlockSpec(memory_space=pltpu.SMEM)] + [pl.BlockSpec(memory_space=pl.ANY)] * 3,
        out_shape=[jax.ShapeDtypeStruct((rows, 2 * EXPERTS * LANES), jnp.float32)] + [packed] * EXPERTS,
        scratch_shapes=[pltpu.VMEM(a.shape, a.dtype) for a in inputs] + [pltpu.SemaphoreType.DMA((len(inputs),))],
        compiler_params=params(),
        cost_estimate=cost(EXCHANGE_FLOPS),
        name="pack",
    )(own_expert, *[pltpu.with_memory_space_constraint(a, pltpu.HBM) for a in inputs])


def combine_kernel(own_count, sides_ref, *refs):
    out_ref = refs[-1]
    rows, width = out_ref.shape
    tail = width // rows
    own = refs[0][...]
    for ref in refs[1:own_count]:
        own += ref[...].astype(jnp.float32)
    row = lax.broadcasted_iota(jnp.int32, (rows, tail), 0)
    parts = []
    others = [ref[...].astype(jnp.float32) for ref in refs[own_count:-1]]
    for s, packed in zip((0,) + RETURN_ORDER, [own] + others):
        coeff = sides_ref[:, s * LANES:s * LANES + 1]
        shifted = sides_ref[:, (EXPERTS + s) * LANES:(EXPERTS + s) * LANES + 1] > 0.5
        ends = jnp.zeros((rows, tail), jnp.float32)
        for i in range(rows - 1):
            ends = jnp.where(row == i, jnp.broadcast_to(packed[rows - 1:, i * tail:(i + 1) * tail], (rows, tail)), ends)
        whole = jnp.concatenate([packed, ends], axis=1)
        parts.append(coeff * jnp.where(shifted, pltpu.roll(whole, 1, 0), whole))
    out_ref[...] = sum(parts[1:], parts[0]).astype(jnp.bfloat16)


def combine(sides, own, others, width):
    return pl.pallas_call(
        functools.partial(combine_kernel, len(own)),
        out_shape=jax.ShapeDtypeStruct((own[0].shape[0], width), jnp.bfloat16),
        compiler_params=params(),
        name="combine",
    )(sides, *own, *others)


def local(tokens, expert_ids, route_weights, gate_weight, up_weight, down_weight):
    rows, width = tokens.shape
    attn = lax.axis_size("attn")
    pair = lax.axis_size("ffn")
    span = attn // EXPERTS

    def over_experts(value, other):
        return lax.ppermute(value, "attn", [(i, (i // span ^ other) * span + i % span) for i in range(attn)])

    def over_span(value, shift):
        return lax.ppermute(value, "attn", [(i, i // span * span + (i + shift) % span) for i in range(attn)])

    def over_pair(value, shift):
        return lax.ppermute(value, "ffn", [(i, (i + shift) % pair) for i in range(pair)])

    own_expert = (lax.axis_index("attn") // span).astype(jnp.int32).reshape(1)
    sides, *packed = pack(own_expert, tokens, expert_ids, route_weights)
    column = packed[:1] + [over_experts(packed[s], s) for s in range(1, EXPERTS)]
    parts = [column] + [[over_span(b, t) for b in column] for t in range(1, span)]
    hiddens, after = [], [b for part in parts[1:2] for b in part[:2]]
    for part in parts:
        group = stack(part, after)
        group = [group] + [over_pair(group, p) for p in range(1, pair)]
        after = [gate_up(group, gate_weight, up_weight, rows)]
        hiddens += after

    sums = [[] for _ in range(EXPERTS)]
    for t, (keep, *sends) in enumerate(down(hiddens, down_weight, pair, rows)):
        arrays = [keep] + [over_pair(b, -p) for p, b in enumerate(sends, 1)]
        blocks = pair_sum(arrays, rows, jnp.bfloat16 if t else jnp.float32)
        for s in range(EXPERTS):
            sums[s].append(over_span(blocks[s], -t) if t else blocks[s])

    returned = [over_experts(span_sum(sums[s]), s) for s in RETURN_ORDER]
    return combine(sides, sums[0], returned, width)


def solution(mesh):
    return jax.shard_map(
        local,
        mesh=mesh,
        in_specs=(
            P(("groups", "attn", "ffn"), None),
            P(("groups", "attn", "ffn"), None),
            P(("groups", "attn", "ffn"), None),
            P(None, ("attn", "ffn")),
            P(None, ("attn", "ffn")),
            P(("attn", "ffn"), None),
        ),
        out_specs=P(("groups", "attn", "ffn"), None),
        check_vma=False,
    )
```

```python
import functools

import jax
import jax.numpy as jnp
from jax import lax
from jax.experimental import pallas as pl
from jax.experimental.pallas import tpu as pltpu
from jax.sharding import PartitionSpec as P

EXPERTS = 4
LANES = 128
RETURN_ORDER = (1, 3, 2)
BLOCK_ORDER = (0, 2, 1, 3)
N_BLOCK = 256
EXCHANGE_FLOPS = 20_000_000_000


def params(mib=4):
    return pltpu.CompilerParams(vmem_limit_bytes=mib * 1024 * 1024)


def cost(flops):
    return pl.CostEstimate(flops=flops, bytes_accessed=0, transcendentals=0)


def block_of(width, most):
    size = most
    while width % size:
        size -= 128
    return size


def in_vmem(value):
    return pltpu.with_memory_space_constraint(value, pltpu.VMEM)


def joined(refs):
    return jnp.concatenate([ref[...].astype(jnp.float32) for ref in refs], axis=0)


def stack_kernel(*refs):
    refs[-1][...] = joined(refs[:-1]).astype(jnp.bfloat16)


def stack(values):
    rows = sum(v.shape[0] for v in values)
    return pl.pallas_call(
        stack_kernel,
        out_shape=jax.ShapeDtypeStruct((rows, values[0].shape[1]), jnp.bfloat16),
        compiler_params=params(),
        cost_estimate=cost(0),
        name="stack",
    )(*values)


def unpacked(refs, out_ref, rows):
    total, width = out_ref.shape
    tail = width // rows
    blocks = (total // rows, rows, tail)
    row = lax.broadcasted_iota(jnp.int32, blocks, 1)
    ends = jnp.zeros(blocks, jnp.float32)
    for i in range(rows - 1):
        piece = joined([ref.at[:, i * tail:(i + 1) * tail] for ref in refs])
        out_ref[:, i * tail:(i + 1) * tail] = piece.astype(jnp.bfloat16)
        ends = jnp.where(row == i, jnp.broadcast_to(piece.reshape(blocks)[:, rows - 1:, :], blocks), ends)
    out_ref[:, width - tail:] = ends.reshape(total, tail).astype(jnp.bfloat16)


def unpack_kernel(rows, *refs):
    unpacked(refs[:-1], refs[-1], rows)


def unpack(values, rows, width):
    total = sum(v.shape[0] for v in values)
    return pl.pallas_call(
        functools.partial(unpack_kernel, rows),
        out_shape=jax.ShapeDtypeStruct((total, width), jnp.bfloat16),
        compiler_params=params(),
        cost_estimate=cost(1_000_000_000),
        name="unpack",
    )(*values)


def gate_up_kernel(n_block, rows, first_ref, *refs):
    rows_in, (gate_ref, up_ref, hidden_ref, rows_ref) = refs[:-4], refs[-4:]
    count = first_ref.shape[0]
    rows_ref[:count, :] = first_ref[...]
    if rows_in:
        unpacked(rows_in, rows_ref.at[count:, :], rows)
    for n in range(0, gate_ref.shape[1], n_block):
        columns = slice(n, n + n_block)
        gate = jnp.dot(rows_ref[...], gate_ref[:, columns], preferred_element_type=jnp.float32)
        up = jnp.dot(rows_ref[...], up_ref[:, columns], preferred_element_type=jnp.float32)
        hidden_ref[:, columns] = (gate / (1.0 + jnp.exp(-gate)) * up).astype(jnp.bfloat16)


def gate_up(first, blocks, gate_weight, up_weight, rows):
    total = sum(r.shape[0] for r in [first] + blocks)
    width, units = gate_weight.shape
    return pl.pallas_call(
        functools.partial(gate_up_kernel, block_of(units, N_BLOCK), rows),
        in_specs=[pl.BlockSpec(memory_space=pltpu.VMEM)] * (len(blocks) + 3),
        out_shape=jax.ShapeDtypeStruct((total, units), jnp.bfloat16),
        scratch_shapes=[pltpu.VMEM((total, width), jnp.bfloat16)],
        compiler_params=params(8),
        cost_estimate=cost(4 * total * width * units),
        name="gate_up",
    )(first, *blocks, in_vmem(gate_weight), in_vmem(up_weight))


def down_kernel(rows, hidden_ref, down_ref, *outs):
    count, width = outs[0].shape
    tail = down_ref.shape[1] // rows
    blocks = (hidden_ref.shape[0] // rows, rows, tail)
    last = lax.broadcasted_iota(jnp.int32, blocks, 1) == rows - 1
    hidden = hidden_ref[...]
    ends = jnp.dot(hidden, down_ref[:, width:], preferred_element_type=jnp.float32).reshape(blocks)
    for i in range(rows - 1):
        columns = slice(i * tail, (i + 1) * tail)
        value = jnp.dot(hidden, down_ref[:, columns], preferred_element_type=jnp.float32).reshape(blocks)
        value = jnp.where(last, jnp.broadcast_to(ends[:, i:i + 1, :], blocks), value).reshape(blocks[0] * rows, tail)
        for j, ref in enumerate(outs):
            ref[:, columns] = value[j * count:(j + 1) * count].astype(ref.dtype)


def down(hidden, down_weight, span, pair, rows):
    total, units = hidden.shape
    width = down_weight.shape[1] // rows * (rows - 1)
    shape = (total // (span * pair), width)
    outs = pl.pallas_call(
        functools.partial(down_kernel, rows),
        in_specs=[pl.BlockSpec(memory_space=pltpu.VMEM)] * 2,
        out_shape=[jax.ShapeDtypeStruct(shape, jnp.bfloat16 if p else jnp.float32) for p in range(pair) for _ in range(span)],
        compiler_params=params(),
        cost_estimate=cost(2 * total * width * units),
        name="down",
    )(hidden, in_vmem(down_weight))
    return [outs[t::span] for t in range(span)]


def pair_sum_kernel(count, *refs):
    outs = refs[count:]
    rows = outs[0].shape[0]
    for i, out_ref in enumerate(outs):
        part = slice(i * rows, (i + 1) * rows)
        value = refs[0][part, :]
        for ref in refs[1:count]:
            value += ref[part, :].astype(jnp.float32)
        out_ref[...] = value.astype(out_ref.dtype)


def pair_sum(arrays, rows, dtype):
    total, width = arrays[0].shape
    return pl.pallas_call(
        functools.partial(pair_sum_kernel, len(arrays)),
        out_shape=[jax.ShapeDtypeStruct((rows, width), dtype)] * (total // rows),
        compiler_params=params(),
        name="pair_sum",
    )(*arrays)


def span_sum_kernel(*refs):
    value = refs[0][...]
    for ref in refs[1:-1]:
        value += ref[...].astype(jnp.float32)
    refs[-1][...] = value.astype(refs[-1].dtype)


def span_sum(arrays):
    return pl.pallas_call(
        span_sum_kernel,
        out_shape=jax.ShapeDtypeStruct(arrays[0].shape, jnp.bfloat16),
        compiler_params=params(),
        name="span_sum",
    )(*arrays)


def pack_kernel(own_expert, tokens_hbm, ids_hbm, weights_hbm, sides_ref, *refs):
    packed_refs, (tokens_ref, ids_ref, weights_ref, semaphores) = refs[:EXPERTS], refs[EXPERTS:]
    pairs = [(tokens_hbm, tokens_ref), (ids_hbm, ids_ref), (weights_hbm, weights_ref)]
    copies = [pltpu.make_async_copy(src, dst, semaphores.at[i]) for i, (src, dst) in enumerate(pairs)]
    for copy in copies:
        copy.start()
    for copy in copies:
        copy.wait()
    ids, weights = ids_ref[...], weights_ref[...]
    rows, width = tokens_ref.shape
    tail = width // rows
    square = (rows, rows)
    row, column = lax.broadcasted_iota(jnp.int32, square, 0), lax.broadcasted_iota(jnp.int32, square, 1)
    last = lax.broadcasted_iota(jnp.int32, (rows, tail), 0) == rows - 1
    here = tokens_ref[...].astype(jnp.float32)
    below = pltpu.roll(here, rows - 1, 0)
    for s, packed_ref in enumerate(packed_refs):
        expert = lax.bitwise_xor(own_expert[0], s)
        named = ids == expert
        chosen = jnp.sum(jnp.where(named, weights, 0.0), axis=0, keepdims=True)
        coeff = jnp.sum(jnp.where(row == column, jnp.broadcast_to(chosen, square), 0.0), axis=1, keepdims=True)
        unnamed = 1.0 - jnp.sum(jnp.where(named, 1.0, 0.0), axis=0, keepdims=True)
        shift = jnp.max(jnp.where(column <= row, jnp.broadcast_to(unnamed, square), 0.0), axis=1, keepdims=True)
        sides_ref[:, s * LANES:(s + 1) * LANES] = jnp.broadcast_to(coeff, (rows, LANES))
        sides_ref[:, (EXPERTS + s) * LANES:(EXPERTS + s + 1) * LANES] = jnp.broadcast_to(shift, (rows, LANES))
        kept = jnp.where(shift > 0.5, below, here)
        for i in range(rows - 1):
            moved = jnp.broadcast_to(kept[i:i + 1, width - tail:], (rows, tail))
            piece = jnp.where(last, moved, kept[:, i * tail:(i + 1) * tail])
            packed_ref[:, i * tail:(i + 1) * tail] = piece.astype(jnp.bfloat16)


def pack(own_expert, tokens, ids, weights):
    rows, width = tokens.shape
    packed = jax.ShapeDtypeStruct((rows, width - width // rows), jnp.bfloat16)
    inputs = [tokens, ids.T, weights.T]
    return pl.pallas_call(
        pack_kernel,
        in_specs=[pl.BlockSpec(memory_space=pltpu.SMEM)] + [pl.BlockSpec(memory_space=pl.ANY)] * 3,
        out_shape=[jax.ShapeDtypeStruct((rows, 2 * EXPERTS * LANES), jnp.float32)] + [packed] * EXPERTS,
        scratch_shapes=[pltpu.VMEM(a.shape, a.dtype) for a in inputs] + [pltpu.SemaphoreType.DMA((len(inputs),))],
        compiler_params=params(),
        cost_estimate=cost(EXCHANGE_FLOPS),
        name="pack",
    )(own_expert, *[pltpu.with_memory_space_constraint(a, pltpu.HBM) for a in inputs])


def combine_kernel(own_count, sides_ref, *refs):
    out_ref = refs[-1]
    rows, width = out_ref.shape
    tail = width // rows
    own = refs[0][...]
    for ref in refs[1:own_count]:
        own += ref[...].astype(jnp.float32)
    row = lax.broadcasted_iota(jnp.int32, (rows, tail), 0)
    parts = []
    others = [ref[...].astype(jnp.float32) for ref in refs[own_count:-1]]
    for s, packed in zip((0,) + RETURN_ORDER, [own] + others):
        coeff = sides_ref[:, s * LANES:s * LANES + 1]
        shifted = sides_ref[:, (EXPERTS + s) * LANES:(EXPERTS + s) * LANES + 1] > 0.5
        ends = jnp.zeros((rows, tail), jnp.float32)
        for i in range(rows - 1):
            ends = jnp.where(row == i, jnp.broadcast_to(packed[rows - 1:, i * tail:(i + 1) * tail], (rows, tail)), ends)
        whole = jnp.concatenate([packed, ends], axis=1)
        parts.append(coeff * jnp.where(shifted, pltpu.roll(whole, 1, 0), whole))
    out_ref[...] = sum(parts[1:], parts[0]).astype(jnp.bfloat16)


def combine(sides, own, others, width):
    return pl.pallas_call(
        functools.partial(combine_kernel, len(own)),
        out_shape=jax.ShapeDtypeStruct((own[0].shape[0], width), jnp.bfloat16),
        compiler_params=params(),
        name="combine",
    )(sides, *own, *others)


def local(tokens, expert_ids, route_weights, gate_weight, up_weight, down_weight):
    rows, width = tokens.shape
    attn = lax.axis_size("attn")
    pair = lax.axis_size("ffn")
    span = attn // EXPERTS

    def over_experts(value, other):
        return lax.ppermute(value, "attn", [(i, (i // span ^ other) * span + i % span) for i in range(attn)])

    def over_span(value, shift):
        return lax.ppermute(value, "attn", [(i, i // span * span + (i + shift) % span) for i in range(attn)])

    def over_pair(value, shift):
        return lax.ppermute(value, "ffn", [(i, (i + shift) % pair) for i in range(pair)])

    own_expert = (lax.axis_index("attn") // span).astype(jnp.int32).reshape(1)
    sides, *packed = pack(own_expert, tokens, expert_ids, route_weights)
    column = {s: over_experts(packed[s], s) if s else packed[0] for s in range(EXPERTS)}
    column = [column[s] for s in BLOCK_ORDER]
    parts = [column] + [[over_span(b, t) for b in column] for t in range(1, span)]
    groups = [stack(part) for part in parts]
    others = [over_pair(g, p) for p in range(1, pair) for g in groups]
    plane = unpack([b for part in parts for b in part], rows, width)
    hidden = gate_up(plane, others, gate_weight, up_weight, rows)

    sums = [[] for _ in range(EXPERTS)]
    for t, (keep, *sends) in enumerate(down(hidden, down_weight, span, pair, rows)):
        arrays = [keep] + [over_pair(b, -p) for p, b in enumerate(sends, 1)]
        blocks = pair_sum(arrays, rows, jnp.bfloat16 if t else jnp.float32)
        for s, block in zip(BLOCK_ORDER, blocks):
            sums[s].append(over_span(block, -t) if t else block)

    returned = [over_experts(span_sum(sums[s]), s) for s in RETURN_ORDER]
    return combine(sides, sums[0], returned, width)


def solution(mesh):
    return jax.shard_map(
        local,
        mesh=mesh,
        in_specs=(
            P(("groups", "attn", "ffn"), None),
            P(("groups", "attn", "ffn"), None),
            P(("groups", "attn", "ffn"), None),
            P(None, ("attn", "ffn")),
            P(None, ("attn", "ffn")),
            P(("attn", "ffn"), None),
        ),
        out_specs=P(("groups", "attn", "ffn"), None),
        check_vma=False,
    )
```

```python
import functools

import jax
import jax.numpy as jnp
from jax import lax
from jax.experimental import pallas as pl
from jax.experimental.pallas import tpu as pltpu
from jax.sharding import PartitionSpec as P

EXPERTS = 4
LANES = 128
RETURN_ORDER = (1, 3, 2)
BLOCK_ORDER = (0, 2, 1, 3)
N_BLOCK = 256
LAST_FLOPS = 5_000_000_000
EXCHANGE_FLOPS = 20_000_000_000


def params(mib=4):
    return pltpu.CompilerParams(vmem_limit_bytes=mib * 1024 * 1024)


def cost(flops):
    return pl.CostEstimate(flops=flops, bytes_accessed=0, transcendentals=0)


def block_of(width, most):
    size = most
    while width % size:
        size -= 128
    return size


def in_vmem(value):
    return pltpu.with_memory_space_constraint(value, pltpu.VMEM)


def joined(refs):
    return jnp.concatenate([ref[...].astype(jnp.float32) for ref in refs], axis=0)


def stack_kernel(count, *refs):
    refs[-1][...] = joined(refs[:count]).astype(jnp.bfloat16)


def stack(values, after=(), flops=0):
    rows = sum(v.shape[0] for v in values)
    return pl.pallas_call(
        functools.partial(stack_kernel, len(values)),
        in_specs=[pl.BlockSpec(memory_space=pltpu.VMEM)] * len(values) + [pl.BlockSpec(memory_space=pl.ANY)] * len(after),
        out_shape=jax.ShapeDtypeStruct((rows, values[0].shape[1]), jnp.bfloat16),
        compiler_params=params(),
        cost_estimate=cost(flops),
        name="stack",
    )(*values, *after)


def unpacked(refs, out_ref, rows):
    total, width = out_ref.shape
    tail = width // rows
    blocks = (total // rows, rows, tail)
    row = lax.broadcasted_iota(jnp.int32, blocks, 1)
    ends = jnp.zeros(blocks, jnp.float32)
    for i in range(rows - 1):
        piece = joined([ref.at[:, i * tail:(i + 1) * tail] for ref in refs])
        out_ref[:, i * tail:(i + 1) * tail] = piece.astype(jnp.bfloat16)
        ends = jnp.where(row == i, jnp.broadcast_to(piece.reshape(blocks)[:, rows - 1:, :], blocks), ends)
    out_ref[:, width - tail:] = ends.reshape(total, tail).astype(jnp.bfloat16)


def unpack_kernel(rows, *refs):
    unpacked(refs[:-1], refs[-1], rows)


def unpack(values, rows, width):
    total = sum(v.shape[0] for v in values)
    return pl.pallas_call(
        functools.partial(unpack_kernel, rows),
        out_shape=jax.ShapeDtypeStruct((total, width), jnp.bfloat16),
        compiler_params=params(),
        cost_estimate=cost(1_000_000_000),
        name="unpack",
    )(*values)


def gate_up_kernel(n_block, rows, first_ref, *refs):
    rows_in, (gate_ref, up_ref, hidden_ref, rows_ref) = refs[:-4], refs[-4:]
    count = first_ref.shape[0]
    rows_ref[:count, :] = first_ref[...]
    if rows_in:
        unpacked(rows_in, rows_ref.at[count:, :], rows)
    for n in range(0, gate_ref.shape[1], n_block):
        columns = slice(n, n + n_block)
        gate = jnp.dot(rows_ref[...], gate_ref[:, columns], preferred_element_type=jnp.float32)
        up = jnp.dot(rows_ref[...], up_ref[:, columns], preferred_element_type=jnp.float32)
        hidden_ref[:, columns] = (gate / (1.0 + jnp.exp(-gate)) * up).astype(jnp.bfloat16)


def gate_up(first, blocks, gate_weight, up_weight, rows):
    total = sum(r.shape[0] for r in [first] + blocks)
    width, units = gate_weight.shape
    return pl.pallas_call(
        functools.partial(gate_up_kernel, block_of(units, N_BLOCK), rows),
        in_specs=[pl.BlockSpec(memory_space=pltpu.VMEM)] * (len(blocks) + 3),
        out_shape=jax.ShapeDtypeStruct((total, units), jnp.bfloat16),
        scratch_shapes=[pltpu.VMEM((total, width), jnp.bfloat16)],
        compiler_params=params(8),
        cost_estimate=cost(4 * total * width * units),
        name="gate_up",
    )(first, *blocks, in_vmem(gate_weight), in_vmem(up_weight))


def down_kernel(rows, hidden_ref, down_ref, *outs):
    count, width = outs[0].shape
    tail = down_ref.shape[1] // rows
    blocks = (hidden_ref.shape[0] // rows, rows, tail)
    last = lax.broadcasted_iota(jnp.int32, blocks, 1) == rows - 1
    hidden = hidden_ref[...]
    ends = jnp.dot(hidden, down_ref[:, width:], preferred_element_type=jnp.float32).reshape(blocks)
    for i in range(rows - 1):
        columns = slice(i * tail, (i + 1) * tail)
        value = jnp.dot(hidden, down_ref[:, columns], preferred_element_type=jnp.float32).reshape(blocks)
        value = jnp.where(last, jnp.broadcast_to(ends[:, i:i + 1, :], blocks), value).reshape(blocks[0] * rows, tail)
        for j, ref in enumerate(outs):
            ref[:, columns] = value[j * count:(j + 1) * count].astype(ref.dtype)


def down(hidden, down_weight, span, pair, rows):
    total, units = hidden.shape
    width = down_weight.shape[1] // rows * (rows - 1)
    shape = (total // (span * pair), width)
    outs = pl.pallas_call(
        functools.partial(down_kernel, rows),
        in_specs=[pl.BlockSpec(memory_space=pltpu.VMEM)] * 2,
        out_shape=[jax.ShapeDtypeStruct(shape, jnp.bfloat16 if p else jnp.float32) for p in range(pair) for _ in range(span)],
        compiler_params=params(),
        cost_estimate=cost(2 * total * width * units),
        name="down",
    )(hidden, in_vmem(down_weight))
    return [outs[t::span] for t in range(span)]


def pair_sum_kernel(count, places, *refs):
    outs = refs[-len(places):]
    rows = outs[0].shape[0]
    for place, out_ref in zip(places, outs):
        part = slice(place * rows, (place + 1) * rows)
        value = refs[0][part, :]
        for ref in refs[1:count]:
            value += ref[part, :].astype(jnp.float32)
        out_ref[...] = value.astype(out_ref.dtype)


def pair_sum(arrays, rows, dtype, places, after=()):
    width = arrays[0].shape[1]
    return pl.pallas_call(
        functools.partial(pair_sum_kernel, len(arrays), places),
        in_specs=[pl.BlockSpec(memory_space=pltpu.VMEM)] * len(arrays) + [pl.BlockSpec(memory_space=pl.ANY)] * len(after),
        out_shape=[jax.ShapeDtypeStruct((rows, width), dtype)] * len(places),
        compiler_params=params(),
        name="pair_sum",
    )(*arrays, *after)


def span_sum_kernel(*refs):
    value = refs[0][...]
    for ref in refs[1:-1]:
        value += ref[...].astype(jnp.float32)
    refs[-1][...] = value.astype(refs[-1].dtype)


def span_sum(arrays):
    return pl.pallas_call(
        span_sum_kernel,
        out_shape=jax.ShapeDtypeStruct(arrays[0].shape, jnp.bfloat16),
        compiler_params=params(),
        name="span_sum",
    )(*arrays)


def pack_kernel(own_expert, tokens_hbm, ids_hbm, weights_hbm, sides_ref, *refs):
    packed_refs, (tokens_ref, ids_ref, weights_ref, semaphores) = refs[:EXPERTS], refs[EXPERTS:]
    pairs = [(tokens_hbm, tokens_ref), (ids_hbm, ids_ref), (weights_hbm, weights_ref)]
    copies = [pltpu.make_async_copy(src, dst, semaphores.at[i]) for i, (src, dst) in enumerate(pairs)]
    for copy in copies:
        copy.start()
    for copy in copies:
        copy.wait()
    ids, weights = ids_ref[...], weights_ref[...]
    rows, width = tokens_ref.shape
    tail = width // rows
    square = (rows, rows)
    row, column = lax.broadcasted_iota(jnp.int32, square, 0), lax.broadcasted_iota(jnp.int32, square, 1)
    last = lax.broadcasted_iota(jnp.int32, (rows, tail), 0) == rows - 1
    here = tokens_ref[...].astype(jnp.float32)
    below = pltpu.roll(here, rows - 1, 0)
    for s, packed_ref in enumerate(packed_refs):
        expert = lax.bitwise_xor(own_expert[0], s)
        named = ids == expert
        chosen = jnp.sum(jnp.where(named, weights, 0.0), axis=0, keepdims=True)
        coeff = jnp.sum(jnp.where(row == column, jnp.broadcast_to(chosen, square), 0.0), axis=1, keepdims=True)
        unnamed = 1.0 - jnp.sum(jnp.where(named, 1.0, 0.0), axis=0, keepdims=True)
        shift = jnp.max(jnp.where(column <= row, jnp.broadcast_to(unnamed, square), 0.0), axis=1, keepdims=True)
        sides_ref[:, s * LANES:(s + 1) * LANES] = jnp.broadcast_to(coeff, (rows, LANES))
        sides_ref[:, (EXPERTS + s) * LANES:(EXPERTS + s + 1) * LANES] = jnp.broadcast_to(shift, (rows, LANES))
        kept = jnp.where(shift > 0.5, below, here)
        for i in range(rows - 1):
            moved = jnp.broadcast_to(kept[i:i + 1, width - tail:], (rows, tail))
            piece = jnp.where(last, moved, kept[:, i * tail:(i + 1) * tail])
            packed_ref[:, i * tail:(i + 1) * tail] = piece.astype(jnp.bfloat16)


def pack(own_expert, tokens, ids, weights):
    rows, width = tokens.shape
    packed = jax.ShapeDtypeStruct((rows, width - width // rows), jnp.bfloat16)
    inputs = [tokens, ids.T, weights.T]
    return pl.pallas_call(
        pack_kernel,
        in_specs=[pl.BlockSpec(memory_space=pltpu.SMEM)] + [pl.BlockSpec(memory_space=pl.ANY)] * 3,
        out_shape=[jax.ShapeDtypeStruct((rows, 2 * EXPERTS * LANES), jnp.float32)] + [packed] * EXPERTS,
        scratch_shapes=[pltpu.VMEM(a.shape, a.dtype) for a in inputs] + [pltpu.SemaphoreType.DMA((len(inputs),))],
        compiler_params=params(),
        cost_estimate=cost(EXCHANGE_FLOPS),
        name="pack",
    )(own_expert, *[pltpu.with_memory_space_constraint(a, pltpu.HBM) for a in inputs])


def combine_kernel(own_count, sides_ref, *refs):
    out_ref = refs[-1]
    rows, width = out_ref.shape
    tail = width // rows
    own = refs[0][...]
    for ref in refs[1:own_count]:
        own += ref[...].astype(jnp.float32)
    row = lax.broadcasted_iota(jnp.int32, (rows, tail), 0)
    parts = []
    others = [ref[...].astype(jnp.float32) for ref in refs[own_count:-1]]
    for s, packed in zip((0,) + RETURN_ORDER, [own] + others):
        coeff = sides_ref[:, s * LANES:s * LANES + 1]
        shifted = sides_ref[:, (EXPERTS + s) * LANES:(EXPERTS + s) * LANES + 1] > 0.5
        ends = jnp.zeros((rows, tail), jnp.float32)
        for i in range(rows - 1):
            ends = jnp.where(row == i, jnp.broadcast_to(packed[rows - 1:, i * tail:(i + 1) * tail], (rows, tail)), ends)
        whole = jnp.concatenate([packed, ends], axis=1)
        parts.append(coeff * jnp.where(shifted, pltpu.roll(whole, 1, 0), whole))
    out_ref[...] = sum(parts[1:], parts[0]).astype(jnp.bfloat16)


def combine(sides, own, others, width):
    return pl.pallas_call(
        functools.partial(combine_kernel, len(own)),
        out_shape=jax.ShapeDtypeStruct((own[0].shape[0], width), jnp.bfloat16),
        compiler_params=params(),
        name="combine",
    )(sides, *own, *others)


def local(tokens, expert_ids, route_weights, gate_weight, up_weight, down_weight):
    rows, width = tokens.shape
    attn = lax.axis_size("attn")
    pair = lax.axis_size("ffn")
    span = attn // EXPERTS

    def over_experts(value, other):
        return lax.ppermute(value, "attn", [(i, (i // span ^ other) * span + i % span) for i in range(attn)])

    def over_span(value, shift):
        return lax.ppermute(value, "attn", [(i, i // span * span + (i + shift) % span) for i in range(attn)])

    def over_pair(value, shift):
        return lax.ppermute(value, "ffn", [(i, (i + shift) % pair) for i in range(pair)])

    own_expert = (lax.axis_index("attn") // span).astype(jnp.int32).reshape(1)
    sides, *packed = pack(own_expert, tokens, expert_ids, route_weights)
    column = {s: over_experts(packed[s], s) if s else packed[0] for s in range(EXPERTS)}
    column = [column[s] for s in BLOCK_ORDER]
    parts = [column] + [[over_span(b, t) for b in column] for t in range(1, span)]
    groups = [stack(column)]
    for part in parts[1:]:
        groups += [stack(part[:-1]), stack(part[-1:], (), LAST_FLOPS)]
    others = [over_pair(g, p) for p in range(1, pair) for g in groups]
    plane = unpack([b for part in parts for b in part], rows, width)
    hidden = gate_up(plane, others, gate_weight, up_weight, rows)

    def paired(keep, sends):
        return [keep] + [over_pair(b, -p) for p, b in enumerate(sends, 1)]

    (own_keep, *own_sends), *far = down(hidden, down_weight, span, pair, rows)
    far = [paired(keep, sends) for keep, *sends in far]
    order = (2, 3, 1, 0)
    blocks = [{} for _ in far]
    sums, returned, after = {}, {}, []
    for wave in (order[:2], order[2:]):
        places = [BLOCK_ORDER.index(s) for s in wave]
        for t, arrays in enumerate(far):
            blocks[t].update(zip(wave, pair_sum(arrays, rows, jnp.bfloat16, places, after)))
        if not sums:
            first = [blocks[t][s] for t in range(len(far)) for s in wave][:1]
            own_sends = [stack([b], first) for b in own_sends]
            own = pair_sum(paired(own_keep, own_sends), rows, jnp.float32, range(EXPERTS))
            own = dict(zip(BLOCK_ORDER, own))
        for s in wave:
            sums[s] = [own[s]] + [over_span(b[s], -t) for t, b in enumerate(blocks, 1)]
            if s:
                total = span_sum(sums[s])
                returned[s] = over_experts(total, s)
                after = [total]
    return combine(sides, sums[0], [returned[s] for s in RETURN_ORDER], width)


def solution(mesh):
    return jax.shard_map(
        local,
        mesh=mesh,
        in_specs=(
            P(("groups", "attn", "ffn"), None),
            P(("groups", "attn", "ffn"), None),
            P(("groups", "attn", "ffn"), None),
            P(None, ("attn", "ffn")),
            P(None, ("attn", "ffn")),
            P(("attn", "ffn"), None),
        ),
        out_specs=P(("groups", "attn", "ffn"), None),
        check_vma=False,
    )
```

```python
import functools

import jax
import jax.numpy as jnp
from jax import lax
from jax.experimental import pallas as pl
from jax.experimental.pallas import tpu as pltpu
from jax.sharding import PartitionSpec as P

EXPERTS = 4
LANES = 128
RETURN_ORDER = (1, 3, 2)
BLOCK_ORDER = (0, 2, 1, 3)
N_BLOCK = 256
LAST_FLOPS = 5_000_000_000
EXCHANGE_FLOPS = 20_000_000_000


def params(mib=4):
    return pltpu.CompilerParams(vmem_limit_bytes=mib * 1024 * 1024)


def cost(flops):
    return pl.CostEstimate(flops=flops, bytes_accessed=0, transcendentals=0)


def block_of(width, most):
    size = most
    while width % size:
        size -= 128
    return size


def in_vmem(value):
    return pltpu.with_memory_space_constraint(value, pltpu.VMEM)


def joined(refs):
    return jnp.concatenate([ref[...].astype(jnp.float32) for ref in refs], axis=0)


def stack_kernel(count, *refs):
    refs[-1][...] = joined(refs[:count]).astype(jnp.bfloat16)


def stack(values, after=(), flops=0):
    rows = sum(v.shape[0] for v in values)
    return pl.pallas_call(
        functools.partial(stack_kernel, len(values)),
        in_specs=[pl.BlockSpec(memory_space=pltpu.VMEM)] * len(values) + [pl.BlockSpec(memory_space=pl.ANY)] * len(after),
        out_shape=jax.ShapeDtypeStruct((rows, values[0].shape[1]), jnp.bfloat16),
        compiler_params=params(),
        cost_estimate=cost(flops),
        name="stack",
    )(*values, *after)


def gate_up_kernel(n_block, *refs):
    rows_in, (gate_ref, up_ref, hidden_ref, rows_ref) = refs[:-4], refs[-4:]
    start, run = 0, []
    for ref in rows_in:
        run.append(ref)
        count = sum(r.shape[0] for r in run)
        if count % 16 == 0:
            rows_ref[start:start + count, :] = ref[...] if len(run) == 1 else joined(run).astype(jnp.bfloat16)
            start, run = start + count, []
    for n in range(0, gate_ref.shape[1], n_block):
        columns = slice(n, n + n_block)
        gate = jnp.dot(rows_ref[...], gate_ref[:, columns], preferred_element_type=jnp.float32)
        up = jnp.dot(rows_ref[...], up_ref[:, columns], preferred_element_type=jnp.float32)
        hidden_ref[:, columns] = (gate / (1.0 + jnp.exp(-gate)) * up).astype(jnp.bfloat16)


def gate_up(blocks, gate_weight, up_weight):
    total = sum(r.shape[0] for r in blocks)
    width, units = gate_weight.shape
    return pl.pallas_call(
        functools.partial(gate_up_kernel, block_of(units, N_BLOCK)),
        in_specs=[pl.BlockSpec(memory_space=pltpu.VMEM)] * (len(blocks) + 2),
        out_shape=jax.ShapeDtypeStruct((total, units), jnp.bfloat16),
        scratch_shapes=[pltpu.VMEM((total, width), jnp.bfloat16)],
        compiler_params=params(),
        cost_estimate=cost(4 * total * width * units),
        name="gate_up",
    )(*blocks, in_vmem(gate_weight), in_vmem(up_weight))


def down_kernel(c_block, hidden_ref, down_ref, *outs):
    count, width = outs[0].shape
    hidden = hidden_ref[...]
    for c in range(0, width, c_block):
        columns = slice(c, c + c_block)
        value = jnp.dot(hidden, down_ref[:, columns], preferred_element_type=jnp.float32)
        for j, ref in enumerate(outs):
            ref[:, columns] = value[j * count:(j + 1) * count].astype(ref.dtype)


def down(hidden, down_weight, span, pair):
    total, units = hidden.shape
    width = down_weight.shape[1]
    shape = (total // (span * pair), width)
    outs = pl.pallas_call(
        functools.partial(down_kernel, block_of(width, N_BLOCK)),
        in_specs=[pl.BlockSpec(memory_space=pltpu.VMEM)] * 2,
        out_shape=[jax.ShapeDtypeStruct(shape, jnp.bfloat16 if p else jnp.float32) for p in range(pair) for _ in range(span)],
        compiler_params=params(),
        cost_estimate=cost(2 * total * width * units),
        name="down",
    )(hidden, in_vmem(down_weight))
    return [outs[t::span] for t in range(span)]


def pair_sum_kernel(count, *refs):
    outs = refs[count:]
    rows = outs[0].shape[0]
    for i, out_ref in enumerate(outs):
        part = slice(i * rows, (i + 1) * rows)
        value = refs[0][part, :]
        for ref in refs[1:count]:
            value += ref[part, :].astype(jnp.float32)
        out_ref[...] = value.astype(out_ref.dtype)


def pair_sum(arrays, rows, dtype):
    total, width = arrays[0].shape
    return pl.pallas_call(
        functools.partial(pair_sum_kernel, len(arrays)),
        out_shape=[jax.ShapeDtypeStruct((rows, width), dtype)] * (total // rows),
        compiler_params=params(),
        name="pair_sum",
    )(*arrays)


def span_sum_kernel(*refs):
    value = refs[0][...]
    for ref in refs[1:-1]:
        value += ref[...].astype(jnp.float32)
    refs[-1][...] = value.astype(refs[-1].dtype)


def span_sum(arrays):
    return pl.pallas_call(
        span_sum_kernel,
        out_shape=jax.ShapeDtypeStruct(arrays[0].shape, jnp.bfloat16),
        compiler_params=params(),
        name="span_sum",
    )(*arrays)


def coefficients_kernel(own_expert, ids_ref, weights_ref, out_ref):
    ids, weights = ids_ref[...], weights_ref[...]
    rows = ids.shape[1]
    square = (rows, rows)
    diagonal = lax.broadcasted_iota(jnp.int32, square, 0) == lax.broadcasted_iota(jnp.int32, square, 1)
    for s in range(EXPERTS):
        expert = lax.bitwise_xor(own_expert[0], s)
        chosen = jnp.sum(jnp.where(ids == expert, weights, 0.0), axis=0, keepdims=True)
        column = jnp.sum(jnp.where(diagonal, jnp.broadcast_to(chosen, square), 0.0), axis=1, keepdims=True)
        out_ref[:, s * LANES:(s + 1) * LANES] = jnp.broadcast_to(column, (rows, LANES))


def coefficients(own_expert, ids, weights):
    return pl.pallas_call(
        coefficients_kernel,
        in_specs=[pl.BlockSpec(memory_space=pltpu.SMEM)] + [pl.BlockSpec(memory_space=pltpu.VMEM)] * 2,
        out_shape=jax.ShapeDtypeStruct((ids.shape[0], EXPERTS * LANES), jnp.float32),
        compiler_params=params(),
        cost_estimate=cost(0),
        name="coefficients",
    )(own_expert, ids.T, weights.T)


def combine_kernel(own_count, coeff_ref, *refs):
    out_ref = refs[-1]
    value = refs[0][...]
    for ref in refs[1:own_count]:
        value += ref[...].astype(jnp.float32)
    value *= coeff_ref[:, :1]
    for s, ref in zip(RETURN_ORDER, refs[own_count:-1]):
        value += coeff_ref[:, s * LANES:s * LANES + 1] * ref[...].astype(jnp.float32)
    out_ref[...] = value.astype(jnp.bfloat16)


def combine(coeffs, own, others):
    return pl.pallas_call(
        functools.partial(combine_kernel, len(own)),
        out_shape=jax.ShapeDtypeStruct(own[0].shape, jnp.bfloat16),
        compiler_params=params(),
        name="combine",
    )(coeffs, *own, *others)


def local(tokens, expert_ids, route_weights, gate_weight, up_weight, down_weight):
    rows = tokens.shape[0]
    attn = lax.axis_size("attn")
    pair = lax.axis_size("ffn")
    span = attn // EXPERTS

    def over_experts(value, other):
        return lax.ppermute(value, "attn", [(i, (i // span ^ other) * span + i % span) for i in range(attn)])

    def over_span(value, shift):
        return lax.ppermute(value, "attn", [(i, i // span * span + (i + shift) % span) for i in range(attn)])

    def over_pair(value, shift):
        return lax.ppermute(value, "ffn", [(i, (i + shift) % pair) for i in range(pair)])

    own_expert = (lax.axis_index("attn") // span).astype(jnp.int32).reshape(1)
    coeffs = coefficients(own_expert, expert_ids, route_weights)
    own = stack([tokens], (), EXCHANGE_FLOPS)
    far = over_experts(tokens, 2)
    near = over_experts(own, 1)
    column = {0: own, 2: far, 1: near, 3: over_experts(far, 1)}
    column = [column[s] for s in BLOCK_ORDER]
    parts = [column] + [[over_span(b, t) for b in column] for t in range(1, span)]
    groups = [stack(column)]
    for part in parts[1:]:
        groups += [stack(part[:-1]), stack(part[-1:], (), LAST_FLOPS)]
    others = [over_pair(g, p) for p in range(1, pair) for g in groups]
    plane = stack([b for part in parts for b in part], (), 1_000_000_000)
    hidden = gate_up([plane] + others, gate_weight, up_weight)

    sums = [[] for _ in range(EXPERTS)]
    for t, (keep, *sends) in enumerate(down(hidden, down_weight, span, pair)):
        arrays = [keep] + [over_pair(b, -p) for p, b in enumerate(sends, 1)]
        blocks = pair_sum(arrays, rows, jnp.bfloat16 if t else jnp.float32)
        for s, block in zip(BLOCK_ORDER, blocks):
            sums[s].append(over_span(block, -t) if t else block)

    returned = [over_experts(span_sum(sums[s]), s) for s in RETURN_ORDER]
    return combine(coeffs, sums[0], returned)


def solution(mesh):
    return jax.shard_map(
        local,
        mesh=mesh,
        in_specs=(
            P(("groups", "attn", "ffn"), None),
            P(("groups", "attn", "ffn"), None),
            P(("groups", "attn", "ffn"), None),
            P(None, ("attn", "ffn")),
            P(None, ("attn", "ffn")),
            P(("attn", "ffn"), None),
        ),
        out_specs=P(("groups", "attn", "ffn"), None),
        check_vma=False,
    )
```

```python
import functools

import jax
import jax.numpy as jnp
from jax import lax
from jax.experimental import pallas as pl
from jax.experimental.pallas import tpu as pltpu
from jax.sharding import PartitionSpec as P

EXPERTS = 4
LANES = 128
RETURN_ORDER = (2, 3, 1)
SEND_ORDER = (2, 3, 1, 0)
BLOCK_ORDER = (0, 2, 1, 3)
N_BLOCK = 256
LAST_FLOPS = 5_000_000_000
EXCHANGE_FLOPS = 20_000_000_000


def params(mib=4):
    return pltpu.CompilerParams(vmem_limit_bytes=mib * 1024 * 1024)


def cost(flops):
    return pl.CostEstimate(flops=flops, bytes_accessed=0, transcendentals=0)


def block_of(width, most):
    size = most
    while width % size:
        size -= 128
    return size


def in_vmem(value):
    return pltpu.with_memory_space_constraint(value, pltpu.VMEM)


def joined(refs):
    return jnp.concatenate([ref[...].astype(jnp.float32) for ref in refs], axis=0)


def stack_kernel(count, *refs):
    refs[-1][...] = joined(refs[:count]).astype(jnp.bfloat16)


def stack(values, after=(), flops=0):
    rows = sum(v.shape[0] for v in values)
    return pl.pallas_call(
        functools.partial(stack_kernel, len(values)),
        in_specs=[pl.BlockSpec(memory_space=pltpu.VMEM)] * len(values) + [pl.BlockSpec(memory_space=pl.ANY)] * len(after),
        out_shape=jax.ShapeDtypeStruct((rows, values[0].shape[1]), jnp.bfloat16),
        compiler_params=params(),
        cost_estimate=cost(flops),
        name="stack",
    )(*values, *after)


def unpacked(refs, out_ref, rows):
    total, width = out_ref.shape
    tail = width // rows
    blocks = (total // rows, rows, tail)
    row = lax.broadcasted_iota(jnp.int32, blocks, 1)
    ends = jnp.zeros(blocks, jnp.float32)
    for i in range(rows - 1):
        piece = joined([ref.at[:, i * tail:(i + 1) * tail] for ref in refs])
        out_ref[:, i * tail:(i + 1) * tail] = piece.astype(jnp.bfloat16)
        ends = jnp.where(row == i, jnp.broadcast_to(piece.reshape(blocks)[:, rows - 1:, :], blocks), ends)
    out_ref[:, width - tail:] = ends.reshape(total, tail).astype(jnp.bfloat16)


def unpack_kernel(rows, *refs):
    unpacked(refs[:-1], refs[-1], rows)


def unpack(values, rows, width):
    total = sum(v.shape[0] for v in values)
    return pl.pallas_call(
        functools.partial(unpack_kernel, rows),
        out_shape=jax.ShapeDtypeStruct((total, width), jnp.bfloat16),
        compiler_params=params(),
        cost_estimate=cost(1_000_000_000),
        name="unpack",
    )(*values)


def gate_up_kernel(n_block, rows, first_ref, *refs):
    rows_in, (gate_ref, up_ref, hidden_ref, rows_ref) = refs[:-4], refs[-4:]
    count = first_ref.shape[0]
    rows_ref[:count, :] = first_ref[...]
    if rows_in:
        unpacked(rows_in, rows_ref.at[count:, :], rows)
    for n in range(0, gate_ref.shape[1], n_block):
        columns = slice(n, n + n_block)
        gate = jnp.dot(rows_ref[...], gate_ref[:, columns], preferred_element_type=jnp.float32)
        up = jnp.dot(rows_ref[...], up_ref[:, columns], preferred_element_type=jnp.float32)
        hidden_ref[:, columns] = (gate / (1.0 + jnp.exp(-gate)) * up).astype(jnp.bfloat16)


def gate_up(first, blocks, gate_weight, up_weight, rows):
    total = sum(r.shape[0] for r in [first] + blocks)
    width, units = gate_weight.shape
    return pl.pallas_call(
        functools.partial(gate_up_kernel, block_of(units, N_BLOCK), rows),
        in_specs=[pl.BlockSpec(memory_space=pltpu.VMEM)] * (len(blocks) + 3),
        out_shape=jax.ShapeDtypeStruct((total, units), jnp.bfloat16),
        scratch_shapes=[pltpu.VMEM((total, width), jnp.bfloat16)],
        compiler_params=params(8),
        cost_estimate=cost(4 * total * width * units),
        name="gate_up",
    )(first, *blocks, in_vmem(gate_weight), in_vmem(up_weight))


def down_kernel(rows, hidden_ref, down_ref, *outs):
    count, width = outs[0].shape
    tail = down_ref.shape[1] // rows
    blocks = (hidden_ref.shape[0] // rows, rows, tail)
    last = lax.broadcasted_iota(jnp.int32, blocks, 1) == rows - 1
    hidden = hidden_ref[...]
    ends = None
    for i in [rows - 2] + list(range(0, rows - 2, 2)):
        both = jnp.dot(hidden, down_ref[:, i * tail:(i + 2) * tail], preferred_element_type=jnp.float32)
        pieces = {i: both[:, :tail].reshape(blocks), i + 1: both[:, tail:].reshape(blocks)}
        if ends is None:
            ends = pieces.pop(i + 1)
        for j, value in pieces.items():
            value = jnp.where(last, jnp.broadcast_to(ends[:, j:j + 1, :], blocks), value).reshape(blocks[0] * rows, tail)
            for k, ref in enumerate(outs):
                ref[:, j * tail:(j + 1) * tail] = value[k * count:(k + 1) * count].astype(ref.dtype)


def down(hidden, down_weight, span, pair, rows):
    total, units = hidden.shape
    width = down_weight.shape[1] // rows * (rows - 1)
    shape = (total // (span * pair), width)
    outs = pl.pallas_call(
        functools.partial(down_kernel, rows),
        in_specs=[pl.BlockSpec(memory_space=pltpu.VMEM)] * 2,
        out_shape=[jax.ShapeDtypeStruct(shape, jnp.bfloat16 if p else jnp.float32) for p in range(pair) for _ in range(span)],
        compiler_params=params(),
        cost_estimate=cost(2 * total * width * units),
        name="down",
    )(hidden, in_vmem(down_weight))
    return [outs[t::span] for t in range(span)]


def pair_sum_kernel(count, places, *refs):
    outs = refs[-len(places):]
    rows = outs[0].shape[0]
    for place, out_ref in zip(places, outs):
        part = slice(place * rows, (place + 1) * rows)
        value = refs[0][part, :]
        for ref in refs[1:count]:
            value += ref[part, :].astype(jnp.float32)
        out_ref[...] = value.astype(out_ref.dtype)


def pair_sum(arrays, rows, dtype, places, after=()):
    width = arrays[0].shape[1]
    return pl.pallas_call(
        functools.partial(pair_sum_kernel, len(arrays), places),
        in_specs=[pl.BlockSpec(memory_space=pltpu.VMEM)] * len(arrays) + [pl.BlockSpec(memory_space=pl.ANY)] * len(after),
        out_shape=[jax.ShapeDtypeStruct((rows, width), dtype)] * len(places),
        compiler_params=params(),
        name="pair_sum",
    )(*arrays, *after)


def span_sum_kernel(*refs):
    value = refs[0][...]
    for ref in refs[1:-1]:
        value += ref[...].astype(jnp.float32)
    refs[-1][...] = value.astype(refs[-1].dtype)


def span_sum(arrays):
    return pl.pallas_call(
        span_sum_kernel,
        out_shape=jax.ShapeDtypeStruct(arrays[0].shape, jnp.bfloat16),
        compiler_params=params(),
        name="span_sum",
    )(*arrays)


def pack_kernel(own_expert, tokens_hbm, ids_hbm, weights_hbm, sides_ref, *refs):
    packed_refs, (tokens_ref, ids_ref, weights_ref, semaphores) = refs[:EXPERTS], refs[EXPERTS:]
    pairs = [(tokens_hbm, tokens_ref), (ids_hbm, ids_ref), (weights_hbm, weights_ref)]
    copies = [pltpu.make_async_copy(src, dst, semaphores.at[i]) for i, (src, dst) in enumerate(pairs)]
    for copy in copies:
        copy.start()
    for copy in copies:
        copy.wait()
    ids, weights = ids_ref[...], weights_ref[...]
    rows, width = tokens_ref.shape
    tail = width // rows
    square = (rows, rows)
    row, column = lax.broadcasted_iota(jnp.int32, square, 0), lax.broadcasted_iota(jnp.int32, square, 1)
    last = lax.broadcasted_iota(jnp.int32, (rows, tail), 0) == rows - 1
    here = tokens_ref[...].astype(jnp.float32)
    below = pltpu.roll(here, rows - 1, 0)
    for s, packed_ref in enumerate(packed_refs):
        expert = lax.bitwise_xor(own_expert[0], s)
        named = ids == expert
        chosen = jnp.sum(jnp.where(named, weights, 0.0), axis=0, keepdims=True)
        coeff = jnp.sum(jnp.where(row == column, jnp.broadcast_to(chosen, square), 0.0), axis=1, keepdims=True)
        unnamed = 1.0 - jnp.sum(jnp.where(named, 1.0, 0.0), axis=0, keepdims=True)
        shift = jnp.max(jnp.where(column <= row, jnp.broadcast_to(unnamed, square), 0.0), axis=1, keepdims=True)
        sides_ref[:, s * LANES:(s + 1) * LANES] = jnp.broadcast_to(coeff, (rows, LANES))
        sides_ref[:, (EXPERTS + s) * LANES:(EXPERTS + s + 1) * LANES] = jnp.broadcast_to(shift, (rows, LANES))
        kept = jnp.where(shift > 0.5, below, here)
        for i in range(rows - 1):
            moved = jnp.broadcast_to(kept[i:i + 1, width - tail:], (rows, tail))
            piece = jnp.where(last, moved, kept[:, i * tail:(i + 1) * tail])
            packed_ref[:, i * tail:(i + 1) * tail] = piece.astype(jnp.bfloat16)


def pack(own_expert, tokens, ids, weights):
    rows, width = tokens.shape
    packed = jax.ShapeDtypeStruct((rows, width - width // rows), jnp.bfloat16)
    inputs = [tokens, ids.T, weights.T]
    return pl.pallas_call(
        pack_kernel,
        in_specs=[pl.BlockSpec(memory_space=pltpu.SMEM)] + [pl.BlockSpec(memory_space=pl.ANY)] * 3,
        out_shape=[jax.ShapeDtypeStruct((rows, 2 * EXPERTS * LANES), jnp.float32)] + [packed] * EXPERTS,
        scratch_shapes=[pltpu.VMEM(a.shape, a.dtype) for a in inputs] + [pltpu.SemaphoreType.DMA((len(inputs),))],
        compiler_params=params(),
        cost_estimate=cost(EXCHANGE_FLOPS),
        name="pack",
    )(own_expert, *[pltpu.with_memory_space_constraint(a, pltpu.HBM) for a in inputs])


def combine_kernel(own_count, sides_ref, *refs):
    out_ref = refs[-1]
    rows, width = out_ref.shape
    tail = width // rows
    own = refs[0][...]
    for ref in refs[1:own_count]:
        own += ref[...].astype(jnp.float32)
    row = lax.broadcasted_iota(jnp.int32, (rows, tail), 0)
    parts = []
    others = [ref[...].astype(jnp.float32) for ref in refs[own_count:-1]]
    for s, packed in zip((0,) + RETURN_ORDER, [own] + others):
        coeff = sides_ref[:, s * LANES:s * LANES + 1]
        shifted = sides_ref[:, (EXPERTS + s) * LANES:(EXPERTS + s) * LANES + 1] > 0.5
        ends = jnp.zeros((rows, tail), jnp.float32)
        for i in range(rows - 1):
            ends = jnp.where(row == i, jnp.broadcast_to(packed[rows - 1:, i * tail:(i + 1) * tail], (rows, tail)), ends)
        whole = jnp.concatenate([packed, ends], axis=1)
        parts.append(coeff * jnp.where(shifted, pltpu.roll(whole, 1, 0), whole))
    out_ref[...] = sum(parts[1:], parts[0]).astype(jnp.bfloat16)


def combine(sides, own, others, width):
    return pl.pallas_call(
        functools.partial(combine_kernel, len(own)),
        out_shape=jax.ShapeDtypeStruct((own[0].shape[0], width), jnp.bfloat16),
        compiler_params=params(),
        name="combine",
    )(sides, *own, *others)


def local(tokens, expert_ids, route_weights, gate_weight, up_weight, down_weight):
    rows, width = tokens.shape
    attn = lax.axis_size("attn")
    pair = lax.axis_size("ffn")
    span = attn // EXPERTS

    def over_experts(value, other):
        return lax.ppermute(value, "attn", [(i, (i // span ^ other) * span + i % span) for i in range(attn)])

    def over_span(value, shift):
        return lax.ppermute(value, "attn", [(i, i // span * span + (i + shift) % span) for i in range(attn)])

    def over_pair(value, shift):
        return lax.ppermute(value, "ffn", [(i, (i + shift) % pair) for i in range(pair)])

    own_expert = (lax.axis_index("attn") // span).astype(jnp.int32).reshape(1)
    sides, *packed = pack(own_expert, tokens, expert_ids, route_weights)
    column = {s: over_experts(packed[s], s) if s else packed[0] for s in range(EXPERTS)}
    column = [column[s] for s in BLOCK_ORDER]
    parts = [column] + [[over_span(b, t) for b in column] for t in range(1, span)]
    groups = [stack(column)]
    for part in parts[1:]:
        groups += [stack(part[:-1]), stack(part[-1:], (), LAST_FLOPS)]
    others = [over_pair(g, p) for p in range(1, pair) for g in groups]
    plane = unpack([b for part in parts for b in part], rows, width)
    hidden = gate_up(plane, others, gate_weight, up_weight, rows)

    def paired(keep, sends):
        return [keep] + [over_pair(b, -p) for p, b in enumerate(sends, 1)]

    (own_keep, *own_sends), *far = down(hidden, down_weight, span, pair, rows)
    far = [paired(keep, sends) for keep, *sends in far]
    first, *later = SEND_ORDER
    blocks = [{first: pair_sum(a, rows, jnp.bfloat16, [BLOCK_ORDER.index(first)])[0]} for a in far]
    own_sends = [stack([b], [blocks[0][first]]) for b in own_sends]
    own = dict(zip(BLOCK_ORDER, pair_sum(paired(own_keep, own_sends), rows, jnp.float32, range(EXPERTS))))
    for block, arrays in zip(blocks, far):
        places = [BLOCK_ORDER.index(s) for s in later]
        block.update(zip(later, pair_sum(arrays, rows, jnp.bfloat16, places, [own[first]])))
    sums = {s: [own[s]] + [over_span(b[s], -t) for t, b in enumerate(blocks, 1)] for s in SEND_ORDER}
    returned = [over_experts(span_sum(sums[s]), s) for s in RETURN_ORDER]
    return combine(sides, sums[0], returned, width)


def solution(mesh):
    return jax.shard_map(
        local,
        mesh=mesh,
        in_specs=(
            P(("groups", "attn", "ffn"), None),
            P(("groups", "attn", "ffn"), None),
            P(("groups", "attn", "ffn"), None),
            P(None, ("attn", "ffn")),
            P(None, ("attn", "ffn")),
            P(("attn", "ffn"), None),
        ),
        out_specs=P(("groups", "attn", "ffn"), None),
        check_vma=False,
    )
```

```python
import functools

import jax
import jax.numpy as jnp
from jax import lax
from jax.experimental import pallas as pl
from jax.experimental.pallas import tpu as pltpu
from jax.sharding import PartitionSpec as P

EXPERTS = 4
LANES = 128
RETURN_ORDER = (2, 3, 1)
BLOCK_ORDER = (0, 2, 1, 3)
N_BLOCK = 256
LAST_FLOPS = 5_000_000_000
EXCHANGE_FLOPS = 20_000_000_000


def params(rows=0):
    return pltpu.CompilerParams(vmem_limit_bytes=4 * max(1, -(-rows // 128)) * 1024 * 1024)


def cost(flops):
    return pl.CostEstimate(flops=flops, bytes_accessed=0, transcendentals=0)


def block_of(width, most):
    size = most
    while width % size:
        size -= 128
    return size


def in_vmem(value):
    return pltpu.with_memory_space_constraint(value, pltpu.VMEM)


def joined(refs):
    return jnp.concatenate([ref[...].astype(jnp.float32) for ref in refs], axis=0)


def stack_kernel(count, *refs):
    refs[-1][...] = joined(refs[:count]).astype(jnp.bfloat16)


def stack(values, after=(), flops=0):
    rows = sum(v.shape[0] for v in values)
    return pl.pallas_call(
        functools.partial(stack_kernel, len(values)),
        in_specs=[pl.BlockSpec(memory_space=pltpu.VMEM)] * len(values) + [pl.BlockSpec(memory_space=pl.ANY)] * len(after),
        out_shape=jax.ShapeDtypeStruct((rows, values[0].shape[1]), jnp.bfloat16),
        compiler_params=params(),
        cost_estimate=cost(flops),
        name="stack",
    )(*values, *after)


def unpacked(refs, out_ref, rows):
    total, width = out_ref.shape
    tail = width // rows
    blocks = (total // rows, rows, tail)
    row = lax.broadcasted_iota(jnp.int32, blocks, 1)
    ends = jnp.zeros(blocks, jnp.float32)
    for i in range(rows - 1):
        piece = joined([ref.at[:, i * tail:(i + 1) * tail] for ref in refs])
        out_ref[:, i * tail:(i + 1) * tail] = piece.astype(jnp.bfloat16)
        ends = jnp.where(row == i, jnp.broadcast_to(piece.reshape(blocks)[:, rows - 1:, :], blocks), ends)
    out_ref[:, width - tail:] = ends.reshape(total, tail).astype(jnp.bfloat16)


def unpack_kernel(rows, *refs):
    unpacked(refs[:-1], refs[-1], rows)


def unpack(values, rows, width):
    total = sum(v.shape[0] for v in values)
    return pl.pallas_call(
        functools.partial(unpack_kernel, rows),
        out_shape=jax.ShapeDtypeStruct((total, width), jnp.bfloat16),
        compiler_params=params(total),
        cost_estimate=cost(1_000_000_000),
        name="unpack",
    )(*values)


def gate_up_kernel(n_block, first_ref, last_ref, gate_ref, up_ref, hidden_ref, rows_ref):
    rows = last_ref.shape[0]
    total, width = rows_ref.shape
    whole = total - 2 * rows
    rows_ref[:whole, :] = first_ref[:whole, :]
    tail = width // rows
    row = lax.broadcasted_iota(jnp.int32, (rows, tail), 0)
    ends = jnp.zeros((rows, tail), jnp.float32)
    for i in range(rows):
        columns = slice(i * tail, (i + 1) * tail)
        if i < rows - 1:
            piece = last_ref[:, columns].astype(jnp.float32)
            ends = jnp.where(row == i, jnp.broadcast_to(piece[rows - 1:, :], (rows, tail)), ends)
        else:
            piece = ends
        both = jnp.concatenate([first_ref[whole:, columns].astype(jnp.float32), piece], axis=0)
        rows_ref[whole:, columns] = both.astype(jnp.bfloat16)
    for n in range(0, gate_ref.shape[1], n_block):
        columns = slice(n, n + n_block)
        gate = jnp.dot(rows_ref[...], gate_ref[:, columns], preferred_element_type=jnp.float32)
        up = jnp.dot(rows_ref[...], up_ref[:, columns], preferred_element_type=jnp.float32)
        hidden_ref[:, columns] = (gate / (1.0 + jnp.exp(-gate)) * up).astype(jnp.bfloat16)


def gate_up(first, last, gate_weight, up_weight):
    total = first.shape[0] + last.shape[0]
    width, units = gate_weight.shape
    return pl.pallas_call(
        functools.partial(gate_up_kernel, block_of(units, N_BLOCK)),
        in_specs=[pl.BlockSpec(memory_space=pltpu.VMEM)] * 4,
        out_shape=jax.ShapeDtypeStruct((total, units), jnp.bfloat16),
        scratch_shapes=[pltpu.VMEM((total, width), jnp.bfloat16)],
        compiler_params=params(total),
        cost_estimate=cost(4 * total * width * units),
        name="gate_up",
    )(first, last, in_vmem(gate_weight), in_vmem(up_weight))


def down_kernel(rows, hidden_ref, down_ref, *outs):
    count, width = outs[0].shape
    tail = down_ref.shape[1] // rows
    blocks = (hidden_ref.shape[0] // rows, rows, tail)
    last = lax.broadcasted_iota(jnp.int32, blocks, 1) == rows - 1
    hidden = hidden_ref[...]
    ends = None
    for i in [rows - 2] + list(range(0, rows - 2, 2)):
        both = jnp.dot(hidden, down_ref[:, i * tail:(i + 2) * tail], preferred_element_type=jnp.float32)
        pieces = {i: both[:, :tail].reshape(blocks), i + 1: both[:, tail:].reshape(blocks)}
        if ends is None:
            ends = pieces.pop(i + 1)
        for j, value in pieces.items():
            value = jnp.where(last, jnp.broadcast_to(ends[:, j:j + 1, :], blocks), value).reshape(blocks[0] * rows, tail)
            for k, ref in enumerate(outs):
                ref[:, j * tail:(j + 1) * tail] = value[k * count:(k + 1) * count].astype(ref.dtype)


def down(hidden, down_weight, span, pair, rows):
    total, units = hidden.shape
    width = down_weight.shape[1] // rows * (rows - 1)
    shape = (total // (span * pair), width)
    outs = pl.pallas_call(
        functools.partial(down_kernel, rows),
        in_specs=[pl.BlockSpec(memory_space=pltpu.VMEM)] * 2,
        out_shape=[jax.ShapeDtypeStruct(shape, jnp.bfloat16 if p else jnp.float32) for p in range(pair) for _ in range(span)],
        compiler_params=params(total),
        cost_estimate=cost(2 * total * width * units),
        name="down",
    )(hidden, in_vmem(down_weight))
    return [outs[t::span] for t in range(span)]


def pair_sum_kernel(count, places, *refs):
    outs = refs[-len(places):]
    rows = outs[0].shape[0]
    for place, out_ref in zip(places, outs):
        part = slice(place * rows, (place + 1) * rows)
        value = refs[0][part, :]
        for ref in refs[1:count]:
            value += ref[part, :].astype(jnp.float32)
        out_ref[...] = value.astype(out_ref.dtype)


def pair_sum(arrays, rows, dtype, places, after=()):
    width = arrays[0].shape[1]
    return pl.pallas_call(
        functools.partial(pair_sum_kernel, len(arrays), places),
        in_specs=[pl.BlockSpec(memory_space=pltpu.VMEM)] * len(arrays) + [pl.BlockSpec(memory_space=pl.ANY)] * len(after),
        out_shape=[jax.ShapeDtypeStruct((rows, width), dtype)] * len(places),
        compiler_params=params(),
        name="pair_sum",
    )(*arrays, *after)


def span_sum_kernel(*refs):
    value = refs[0][...]
    for ref in refs[1:-1]:
        value += ref[...].astype(jnp.float32)
    refs[-1][...] = value.astype(refs[-1].dtype)


def span_sum(arrays):
    return pl.pallas_call(
        span_sum_kernel,
        out_shape=jax.ShapeDtypeStruct(arrays[0].shape, jnp.bfloat16),
        compiler_params=params(),
        name="span_sum",
    )(*arrays)


def pack_kernel(own_expert, tokens_hbm, ids_hbm, weights_hbm, sides_ref, *refs):
    packed_refs, (tokens_ref, ids_ref, weights_ref, semaphores) = refs[:EXPERTS], refs[EXPERTS:]
    pairs = [(tokens_hbm, tokens_ref), (ids_hbm, ids_ref), (weights_hbm, weights_ref)]
    copies = [pltpu.make_async_copy(src, dst, semaphores.at[i]) for i, (src, dst) in enumerate(pairs)]
    for copy in copies:
        copy.start()
    for copy in copies:
        copy.wait()
    ids, weights = ids_ref[...], weights_ref[...]
    rows, width = tokens_ref.shape
    tail = width // rows
    square = (rows, rows)
    row, column = lax.broadcasted_iota(jnp.int32, square, 0), lax.broadcasted_iota(jnp.int32, square, 1)
    last = lax.broadcasted_iota(jnp.int32, (rows, tail), 0) == rows - 1
    here = tokens_ref[...].astype(jnp.float32)
    below = pltpu.roll(here, rows - 1, 0)
    for s, packed_ref in enumerate(packed_refs):
        expert = lax.bitwise_xor(own_expert[0], s)
        named = ids == expert
        chosen = jnp.sum(jnp.where(named, weights, 0.0), axis=0, keepdims=True)
        coeff = jnp.sum(jnp.where(row == column, jnp.broadcast_to(chosen, square), 0.0), axis=1, keepdims=True)
        unnamed = 1.0 - jnp.sum(jnp.where(named, 1.0, 0.0), axis=0, keepdims=True)
        shift = jnp.max(jnp.where(column <= row, jnp.broadcast_to(unnamed, square), 0.0), axis=1, keepdims=True)
        sides_ref[:, s * LANES:(s + 1) * LANES] = jnp.broadcast_to(coeff, (rows, LANES))
        sides_ref[:, (EXPERTS + s) * LANES:(EXPERTS + s + 1) * LANES] = jnp.broadcast_to(shift, (rows, LANES))
        kept = jnp.where(shift > 0.5, below, here)
        for i in range(rows - 1):
            moved = jnp.broadcast_to(kept[i:i + 1, width - tail:], (rows, tail))
            piece = jnp.where(last, moved, kept[:, i * tail:(i + 1) * tail])
            packed_ref[:, i * tail:(i + 1) * tail] = piece.astype(jnp.bfloat16)


def pack(own_expert, tokens, ids, weights):
    rows, width = tokens.shape
    packed = jax.ShapeDtypeStruct((rows, width - width // rows), jnp.bfloat16)
    inputs = [tokens, ids.T, weights.T]
    return pl.pallas_call(
        pack_kernel,
        in_specs=[pl.BlockSpec(memory_space=pltpu.SMEM)] + [pl.BlockSpec(memory_space=pl.ANY)] * 3,
        out_shape=[jax.ShapeDtypeStruct((rows, 2 * EXPERTS * LANES), jnp.float32)] + [packed] * EXPERTS,
        scratch_shapes=[pltpu.VMEM(a.shape, a.dtype) for a in inputs] + [pltpu.SemaphoreType.DMA((len(inputs),))],
        compiler_params=params(),
        cost_estimate=cost(EXCHANGE_FLOPS),
        name="pack",
    )(own_expert, *[pltpu.with_memory_space_constraint(a, pltpu.HBM) for a in inputs])


def combine_kernel(base, places, counts, sides_ref, *refs):
    *refs, out_ref = refs
    rows, width = out_ref.shape
    tail = width // rows
    row = lax.broadcasted_iota(jnp.int32, (rows, tail), 0)
    value = None
    for ref in refs[:base]:
        value = ref[...]
    refs = refs[base:]
    for s, count in zip(places, counts):
        packed = sum([ref[...].astype(jnp.float32) for ref in refs[1:count]], refs[0][...].astype(jnp.float32))
        refs = refs[count:]
        coeff = sides_ref[:, s * LANES:s * LANES + 1]
        shifted = sides_ref[:, (EXPERTS + s) * LANES:(EXPERTS + s) * LANES + 1] > 0.5
        ends = jnp.zeros((rows, tail), jnp.float32)
        for i in range(rows - 1):
            ends = jnp.where(row == i, jnp.broadcast_to(packed[rows - 1:, i * tail:(i + 1) * tail], (rows, tail)), ends)
        whole = jnp.concatenate([packed, ends], axis=1)
        term = coeff * jnp.where(shifted, pltpu.roll(whole, 1, 0), whole)
        value = term if value is None else value + term
    out_ref[...] = value.astype(out_ref.dtype)


def combine(sides, base, places, groups, width, dtype):
    arrays = [a for group in groups for a in group]
    return pl.pallas_call(
        functools.partial(combine_kernel, len(base), tuple(places), tuple(len(g) for g in groups)),
        out_shape=jax.ShapeDtypeStruct((arrays[0].shape[0], width), dtype),
        compiler_params=params(),
        name="combine",
    )(sides, *base, *arrays)


def local(tokens, expert_ids, route_weights, gate_weight, up_weight, down_weight):
    rows, width = tokens.shape
    attn = lax.axis_size("attn")
    pair = lax.axis_size("ffn")
    span = attn // EXPERTS

    def over_experts(value, other):
        return lax.ppermute(value, "attn", [(i, (i // span ^ other) * span + i % span) for i in range(attn)])

    def over_span(value, shift):
        return lax.ppermute(value, "attn", [(i, i // span * span + (i + shift) % span) for i in range(attn)])

    def over_pair(value, shift):
        return lax.ppermute(value, "ffn", [(i, (i + shift) % pair) for i in range(pair)])

    own_expert = (lax.axis_index("attn") // span).astype(jnp.int32).reshape(1)
    sides, *packed = pack(own_expert, tokens, expert_ids, route_weights)
    column = {s: over_experts(packed[s], s) if s else packed[0] for s in range(EXPERTS)}
    column = [column[s] for s in BLOCK_ORDER]
    parts = [column] + [[over_span(b, t) for b in column] for t in range(1, span)]
    groups = [stack(column)]
    for part in parts[1:]:
        groups += [stack(part[:-1]), stack(part[-1:], (), LAST_FLOPS)]
    *others, last = [over_pair(g, p) for p in range(1, pair) for g in groups]
    first = unpack([b for part in parts for b in part] + others, rows, width)
    hidden = gate_up(first, last, gate_weight, up_weight)

    def paired(keep, sends):
        return [keep] + [over_pair(b, -p) for p, b in enumerate(sends, 1)]

    sums = [[] for _ in range(EXPERTS)]
    for t, (keep, *sends) in enumerate(down(hidden, down_weight, span, pair, rows)):
        arrays = paired(keep, sends)
        blocks = pair_sum(arrays, rows, jnp.bfloat16 if t else jnp.float32, range(EXPERTS))
        for s, block in zip(BLOCK_ORDER, blocks):
            sums[s].append(over_span(block, -t) if t else block)

    returned = {s: over_experts(span_sum(sums[s]), s) for s in RETURN_ORDER}
    first, *later = RETURN_ORDER
    early = combine(sides, [], [0, first], [sums[0], [returned[first]]], width, jnp.float32)
    return combine(sides, [early], later, [[returned[s]] for s in later], width, jnp.bfloat16)


def solution(mesh):
    return jax.shard_map(
        local,
        mesh=mesh,
        in_specs=(
            P(("groups", "attn", "ffn"), None),
            P(("groups", "attn", "ffn"), None),
            P(("groups", "attn", "ffn"), None),
            P(None, ("attn", "ffn")),
            P(None, ("attn", "ffn")),
            P(("attn", "ffn"), None),
        ),
        out_specs=P(("groups", "attn", "ffn"), None),
        check_vma=False,
    )
```

```python
import functools

import jax
import jax.numpy as jnp
from jax import lax
from jax.experimental import pallas as pl
from jax.experimental.pallas import tpu as pltpu
from jax.sharding import PartitionSpec as P

EXPERTS = 4
LANES = 128
RETURN_ORDER = (3, 2, 1)
BLOCK_ORDER = (0, 3, 1, 2)
N_BLOCK = 512
LAST_FLOPS = 5_000_000_000
EXCHANGE_FLOPS = 20_000_000_000


def params(rows=0):
    return pltpu.CompilerParams(vmem_limit_bytes=4 * max(1, -(-rows // 128)) * 1024 * 1024)


def cost(flops):
    return pl.CostEstimate(flops=flops, bytes_accessed=0, transcendentals=0)


def block_of(width, most):
    size = most
    while width % size:
        size -= 128
    return size


def in_vmem(value):
    return pltpu.with_memory_space_constraint(value, pltpu.VMEM)


def joined(refs):
    return jnp.concatenate([ref[...].astype(jnp.float32) for ref in refs], axis=0)


def stack_kernel(count, *refs):
    refs[-1][...] = joined(refs[:count]).astype(jnp.bfloat16)


def stack(values, after=(), flops=0):
    rows = sum(v.shape[0] for v in values)
    return pl.pallas_call(
        functools.partial(stack_kernel, len(values)),
        in_specs=[pl.BlockSpec(memory_space=pltpu.VMEM)] * len(values) + [pl.BlockSpec(memory_space=pl.ANY)] * len(after),
        out_shape=jax.ShapeDtypeStruct((rows, values[0].shape[1]), jnp.bfloat16),
        compiler_params=params(),
        cost_estimate=cost(flops),
        name="stack",
    )(*values, *after)


def unpacked(refs, out_ref, rows):
    total, width = out_ref.shape
    tail = width // rows
    blocks = (total // rows, rows, tail)
    row = lax.broadcasted_iota(jnp.int32, blocks, 1)
    ends = jnp.zeros(blocks, jnp.float32)
    for i in range(rows - 1):
        piece = joined([ref.at[:, i * tail:(i + 1) * tail] for ref in refs])
        out_ref[:, i * tail:(i + 1) * tail] = piece.astype(jnp.bfloat16)
        ends = jnp.where(row == i, jnp.broadcast_to(piece.reshape(blocks)[:, rows - 1:, :], blocks), ends)
    out_ref[:, width - tail:] = ends.reshape(total, tail).astype(jnp.bfloat16)


def unpack_kernel(rows, *refs):
    unpacked(refs[:-1], refs[-1], rows)


def unpack(values, rows, width):
    total = sum(v.shape[0] for v in values)
    return pl.pallas_call(
        functools.partial(unpack_kernel, rows),
        out_shape=jax.ShapeDtypeStruct((total, width), jnp.bfloat16),
        compiler_params=params(total),
        cost_estimate=cost(1_000_000_000),
        name="unpack",
    )(*values)


def gate_up_kernel(n_block, first_ref, last_ref, gate_ref, up_ref, hidden_ref, rows_ref):
    rows = last_ref.shape[0]
    total, width = rows_ref.shape
    whole = total - 2 * rows
    rows_ref[:whole, :] = first_ref[:whole, :]
    tail = width // rows
    row = lax.broadcasted_iota(jnp.int32, (rows, tail), 0)
    ends = jnp.zeros((rows, tail), jnp.float32)
    for i in range(rows):
        columns = slice(i * tail, (i + 1) * tail)
        if i < rows - 1:
            piece = last_ref[:, columns].astype(jnp.float32)
            ends = jnp.where(row == i, jnp.broadcast_to(piece[rows - 1:, :], (rows, tail)), ends)
        else:
            piece = ends
        both = jnp.concatenate([first_ref[whole:, columns].astype(jnp.float32), piece], axis=0)
        rows_ref[whole:, columns] = both.astype(jnp.bfloat16)
    for n in range(0, gate_ref.shape[1], n_block):
        columns = slice(n, n + n_block)
        gate = jnp.dot(rows_ref[...], gate_ref[:, columns], preferred_element_type=jnp.float32)
        up = jnp.dot(rows_ref[...], up_ref[:, columns], preferred_element_type=jnp.float32)
        hidden_ref[:, columns] = (gate / (1.0 + jnp.exp(-gate)) * up).astype(jnp.bfloat16)


def gate_up(first, last, gate_weight, up_weight):
    total = first.shape[0] + last.shape[0]
    width, units = gate_weight.shape
    return pl.pallas_call(
        functools.partial(gate_up_kernel, block_of(units, N_BLOCK)),
        in_specs=[pl.BlockSpec(memory_space=pltpu.VMEM)] * 4,
        out_shape=jax.ShapeDtypeStruct((total, units), jnp.bfloat16),
        scratch_shapes=[pltpu.VMEM((total, width), jnp.bfloat16)],
        compiler_params=params(total),
        cost_estimate=cost(4 * total * width * units),
        name="gate_up",
    )(first, last, in_vmem(gate_weight), in_vmem(up_weight))


def down_kernel(rows, hidden_ref, down_ref, *outs):
    count, width = outs[0].shape
    tail = down_ref.shape[1] // rows
    blocks = (hidden_ref.shape[0] // rows, rows, tail)
    last = lax.broadcasted_iota(jnp.int32, blocks, 1) == rows - 1
    hidden = hidden_ref[...]
    ends = None
    for i in [rows - 2] + list(range(0, rows - 2, 2)):
        both = jnp.dot(hidden, down_ref[:, i * tail:(i + 2) * tail], preferred_element_type=jnp.float32)
        pieces = {i: both[:, :tail].reshape(blocks), i + 1: both[:, tail:].reshape(blocks)}
        if ends is None:
            ends = pieces.pop(i + 1)
        for j, value in pieces.items():
            value = jnp.where(last, jnp.broadcast_to(ends[:, j:j + 1, :], blocks), value).reshape(blocks[0] * rows, tail)
            for k, ref in enumerate(outs):
                ref[:, j * tail:(j + 1) * tail] = value[k * count:(k + 1) * count].astype(ref.dtype)


def down(hidden, down_weight, span, pair, rows):
    total, units = hidden.shape
    width = down_weight.shape[1] // rows * (rows - 1)
    shape = (total // (span * pair), width)
    outs = pl.pallas_call(
        functools.partial(down_kernel, rows),
        in_specs=[pl.BlockSpec(memory_space=pltpu.VMEM)] * 2,
        out_shape=[jax.ShapeDtypeStruct(shape, jnp.bfloat16 if p else jnp.float32) for p in range(pair) for _ in range(span)],
        compiler_params=params(total),
        cost_estimate=cost(2 * total * width * units),
        name="down",
    )(hidden, in_vmem(down_weight))
    return [outs[t::span] for t in range(span)]


def pair_sum_kernel(count, places, *refs):
    outs = refs[-len(places):]
    rows = outs[0].shape[0]
    for place, out_ref in zip(places, outs):
        part = slice(place * rows, (place + 1) * rows)
        value = refs[0][part, :]
        for ref in refs[1:count]:
            value += ref[part, :].astype(jnp.float32)
        out_ref[...] = value.astype(out_ref.dtype)


def pair_sum(arrays, rows, dtype, places, after=()):
    width = arrays[0].shape[1]
    return pl.pallas_call(
        functools.partial(pair_sum_kernel, len(arrays), places),
        in_specs=[pl.BlockSpec(memory_space=pltpu.VMEM)] * len(arrays) + [pl.BlockSpec(memory_space=pl.ANY)] * len(after),
        out_shape=[jax.ShapeDtypeStruct((rows, width), dtype)] * len(places),
        compiler_params=params(),
        name="pair_sum",
    )(*arrays, *after)


def span_sum_kernel(*refs):
    value = refs[0][...]
    for ref in refs[1:-1]:
        value += ref[...].astype(jnp.float32)
    refs[-1][...] = value.astype(refs[-1].dtype)


def span_sum(arrays):
    return pl.pallas_call(
        span_sum_kernel,
        out_shape=jax.ShapeDtypeStruct(arrays[0].shape, jnp.bfloat16),
        compiler_params=params(),
        name="span_sum",
    )(*arrays)


def pack_kernel(own_expert, tokens_hbm, ids_hbm, weights_hbm, sides_ref, *refs):
    packed_refs, (tokens_ref, ids_ref, weights_ref, semaphores) = refs[:EXPERTS], refs[EXPERTS:]
    pairs = [(tokens_hbm, tokens_ref), (ids_hbm, ids_ref), (weights_hbm, weights_ref)]
    copies = [pltpu.make_async_copy(src, dst, semaphores.at[i]) for i, (src, dst) in enumerate(pairs)]
    for copy in copies:
        copy.start()
    for copy in copies:
        copy.wait()
    ids, weights = ids_ref[...], weights_ref[...]
    rows, width = tokens_ref.shape
    tail = width // rows
    square = (rows, rows)
    row, column = lax.broadcasted_iota(jnp.int32, square, 0), lax.broadcasted_iota(jnp.int32, square, 1)
    last = lax.broadcasted_iota(jnp.int32, (rows, tail), 0) == rows - 1
    here = tokens_ref[...].astype(jnp.float32)
    below = pltpu.roll(here, rows - 1, 0)
    for s, packed_ref in enumerate(packed_refs):
        expert = lax.bitwise_xor(own_expert[0], s)
        named = ids == expert
        chosen = jnp.sum(jnp.where(named, weights, 0.0), axis=0, keepdims=True)
        coeff = jnp.sum(jnp.where(row == column, jnp.broadcast_to(chosen, square), 0.0), axis=1, keepdims=True)
        unnamed = 1.0 - jnp.sum(jnp.where(named, 1.0, 0.0), axis=0, keepdims=True)
        shift = jnp.max(jnp.where(column <= row, jnp.broadcast_to(unnamed, square), 0.0), axis=1, keepdims=True)
        sides_ref[:, s * LANES:(s + 1) * LANES] = jnp.broadcast_to(coeff, (rows, LANES))
        sides_ref[:, (EXPERTS + s) * LANES:(EXPERTS + s + 1) * LANES] = jnp.broadcast_to(shift, (rows, LANES))
        kept = jnp.where(shift > 0.5, below, here)
        for i in range(rows - 1):
            moved = jnp.broadcast_to(kept[i:i + 1, width - tail:], (rows, tail))
            piece = jnp.where(last, moved, kept[:, i * tail:(i + 1) * tail])
            packed_ref[:, i * tail:(i + 1) * tail] = piece.astype(jnp.bfloat16)


def pack(own_expert, tokens, ids, weights):
    rows, width = tokens.shape
    packed = jax.ShapeDtypeStruct((rows, width - width // rows), jnp.bfloat16)
    inputs = [tokens, ids.T, weights.T]
    return pl.pallas_call(
        pack_kernel,
        in_specs=[pl.BlockSpec(memory_space=pltpu.SMEM)] + [pl.BlockSpec(memory_space=pl.ANY)] * 3,
        out_shape=[jax.ShapeDtypeStruct((rows, 2 * EXPERTS * LANES), jnp.float32)] + [packed] * EXPERTS,
        scratch_shapes=[pltpu.VMEM(a.shape, a.dtype) for a in inputs] + [pltpu.SemaphoreType.DMA((len(inputs),))],
        compiler_params=params(),
        cost_estimate=cost(EXCHANGE_FLOPS),
        name="pack",
    )(own_expert, *[pltpu.with_memory_space_constraint(a, pltpu.HBM) for a in inputs])


def combine_kernel(base, places, counts, sides_ref, *refs):
    *refs, out_ref = refs
    rows, width = out_ref.shape
    tail = width // rows
    row = lax.broadcasted_iota(jnp.int32, (rows, tail), 0)
    value = None
    for ref in refs[:base]:
        value = ref[...]
    refs = refs[base:]
    for s, count in zip(places, counts):
        packed = sum([ref[...].astype(jnp.float32) for ref in refs[1:count]], refs[0][...].astype(jnp.float32))
        refs = refs[count:]
        coeff = sides_ref[:, s * LANES:s * LANES + 1]
        shifted = sides_ref[:, (EXPERTS + s) * LANES:(EXPERTS + s) * LANES + 1] > 0.5
        ends = jnp.zeros((rows, tail), jnp.float32)
        for i in range(rows - 1):
            ends = jnp.where(row == i, jnp.broadcast_to(packed[rows - 1:, i * tail:(i + 1) * tail], (rows, tail)), ends)
        whole = jnp.concatenate([packed, ends], axis=1)
        term = coeff * jnp.where(shifted, pltpu.roll(whole, 1, 0), whole)
        value = term if value is None else value + term
    out_ref[...] = value.astype(out_ref.dtype)


def combine(sides, base, places, groups, width, dtype):
    arrays = [a for group in groups for a in group]
    return pl.pallas_call(
        functools.partial(combine_kernel, len(base), tuple(places), tuple(len(g) for g in groups)),
        out_shape=jax.ShapeDtypeStruct((arrays[0].shape[0], width), dtype),
        compiler_params=params(),
        name="combine",
    )(sides, *base, *arrays)


def local(tokens, expert_ids, route_weights, gate_weight, up_weight, down_weight):
    rows, width = tokens.shape
    attn = lax.axis_size("attn")
    pair = lax.axis_size("ffn")
    span = attn // EXPERTS

    def over_experts(value, other):
        return lax.ppermute(value, "attn", [(i, (i // span ^ other) * span + i % span) for i in range(attn)])

    def over_span(value, shift):
        return lax.ppermute(value, "attn", [(i, i // span * span + (i + shift) % span) for i in range(attn)])

    def over_pair(value, shift):
        return lax.ppermute(value, "ffn", [(i, (i + shift) % pair) for i in range(pair)])

    own_expert = (lax.axis_index("attn") // span).astype(jnp.int32).reshape(1)
    sides, *packed = pack(own_expert, tokens, expert_ids, route_weights)
    column = {s: over_experts(packed[s], s) if s else packed[0] for s in range(EXPERTS)}
    column = [column[s] for s in BLOCK_ORDER]
    parts = [column] + [[over_span(b, t) for b in column] for t in range(1, span)]
    groups = [stack(column)]
    for part in parts[1:]:
        groups += [stack(part[:-1]), stack(part[-1:], (), LAST_FLOPS)]
    *others, last = [over_pair(g, p) for p in range(1, pair) for g in groups]
    first = unpack([b for part in parts for b in part] + others, rows, width)
    hidden = gate_up(first, last, gate_weight, up_weight)

    def paired(keep, sends):
        return [keep] + [over_pair(b, -p) for p, b in enumerate(sends, 1)]

    sums = [[] for _ in range(EXPERTS)]
    for t, (keep, *sends) in enumerate(down(hidden, down_weight, span, pair, rows)):
        arrays = paired(keep, sends)
        blocks = pair_sum(arrays, rows, jnp.bfloat16 if t else jnp.float32, range(EXPERTS))
        for s, block in zip(BLOCK_ORDER, blocks):
            sums[s].append(over_span(block, -t) if t else block)

    returned = {s: over_experts(span_sum(sums[s]), s) for s in RETURN_ORDER}
    first, *later = RETURN_ORDER
    early = combine(sides, [], [0, first], [sums[0], [returned[first]]], width, jnp.float32)
    return combine(sides, [early], later, [[returned[s]] for s in later], width, jnp.bfloat16)


def solution(mesh):
    return jax.shard_map(
        local,
        mesh=mesh,
        in_specs=(
            P(("groups", "attn", "ffn"), None),
            P(("groups", "attn", "ffn"), None),
            P(("groups", "attn", "ffn"), None),
            P(None, ("attn", "ffn")),
            P(None, ("attn", "ffn")),
            P(("attn", "ffn"), None),
        ),
        out_specs=P(("groups", "attn", "ffn"), None),
        check_vma=False,
    )
```

```python
import functools

import jax
import jax.numpy as jnp
from jax import lax
from jax.experimental import pallas as pl
from jax.experimental.pallas import tpu as pltpu
from jax.sharding import PartitionSpec as P

EXPERTS = 4
LANES = 128
RETURN_ORDER = (3, 2, 1)
BLOCK_ORDER = (0, 3, 1, 2)
N_BLOCK = 1024
LAST_FLOPS = 5_000_000_000
EXCHANGE_FLOPS = 20_000_000_000


def params(rows=0):
    return pltpu.CompilerParams(vmem_limit_bytes=4 * max(1, -(-rows // 128)) * 1024 * 1024)


def cost(flops):
    return pl.CostEstimate(flops=flops, bytes_accessed=0, transcendentals=0)


def block_of(width, most):
    size = most
    while width % size:
        size -= 128
    return size


def in_vmem(value):
    return pltpu.with_memory_space_constraint(value, pltpu.VMEM)


def joined(refs):
    return jnp.concatenate([ref[...].astype(jnp.float32) for ref in refs], axis=0)


def stack_kernel(count, *refs):
    refs[-1][...] = joined(refs[:count]).astype(jnp.bfloat16)


def stack(values, after=(), flops=0):
    rows = sum(v.shape[0] for v in values)
    return pl.pallas_call(
        functools.partial(stack_kernel, len(values)),
        in_specs=[pl.BlockSpec(memory_space=pltpu.VMEM)] * len(values) + [pl.BlockSpec(memory_space=pl.ANY)] * len(after),
        out_shape=jax.ShapeDtypeStruct((rows, values[0].shape[1]), jnp.bfloat16),
        compiler_params=params(),
        cost_estimate=cost(flops),
        name="stack",
    )(*values, *after)


def unpacked(refs, out_ref, rows):
    total, width = out_ref.shape
    tail = width // rows
    blocks = (total // rows, rows, tail)
    row = lax.broadcasted_iota(jnp.int32, blocks, 1)
    ends = jnp.zeros(blocks, jnp.float32)
    for i in range(rows - 1):
        piece = joined([ref.at[:, i * tail:(i + 1) * tail] for ref in refs])
        out_ref[:, i * tail:(i + 1) * tail] = piece.astype(jnp.bfloat16)
        ends = jnp.where(row == i, jnp.broadcast_to(piece.reshape(blocks)[:, rows - 1:, :], blocks), ends)
    out_ref[:, width - tail:] = ends.reshape(total, tail).astype(jnp.bfloat16)


def unpack_kernel(rows, *refs):
    unpacked(refs[:-1], refs[-1], rows)


def unpack(values, rows, width):
    total = sum(v.shape[0] for v in values)
    return pl.pallas_call(
        functools.partial(unpack_kernel, rows),
        out_shape=jax.ShapeDtypeStruct((total, width), jnp.bfloat16),
        compiler_params=params(total),
        cost_estimate=cost(1_000_000_000),
        name="unpack",
    )(*values)


def gate_up_kernel(n_block, first_ref, last_ref, gate_ref, up_ref, hidden_ref, rows_ref):
    rows = last_ref.shape[0]
    total, width = rows_ref.shape
    whole = total - 2 * rows
    rows_ref[:whole, :] = first_ref[:whole, :]
    tail = width // rows
    row = lax.broadcasted_iota(jnp.int32, (rows, tail), 0)
    ends = jnp.zeros((rows, tail), jnp.float32)
    for i in range(rows):
        columns = slice(i * tail, (i + 1) * tail)
        if i < rows - 1:
            piece = last_ref[:, columns].astype(jnp.float32)
            ends = jnp.where(row == i, jnp.broadcast_to(piece[rows - 1:, :], (rows, tail)), ends)
        else:
            piece = ends
        both = jnp.concatenate([first_ref[whole:, columns].astype(jnp.float32), piece], axis=0)
        rows_ref[whole:, columns] = both.astype(jnp.bfloat16)
    for n in range(0, gate_ref.shape[1], n_block):
        columns = slice(n, n + n_block)
        gate = jnp.dot(rows_ref[...], gate_ref[:, columns], preferred_element_type=jnp.float32)
        up = jnp.dot(rows_ref[...], up_ref[:, columns], preferred_element_type=jnp.float32)
        hidden_ref[:, columns] = (gate / (1.0 + jnp.exp(-gate)) * up).astype(jnp.bfloat16)


def gate_up(first, last, gate_weight, up_weight):
    total = first.shape[0] + last.shape[0]
    width, units = gate_weight.shape
    return pl.pallas_call(
        functools.partial(gate_up_kernel, block_of(units, N_BLOCK)),
        in_specs=[pl.BlockSpec(memory_space=pltpu.VMEM)] * 4,
        out_shape=jax.ShapeDtypeStruct((total, units), jnp.bfloat16),
        scratch_shapes=[pltpu.VMEM((total, width), jnp.bfloat16)],
        compiler_params=params(total),
        cost_estimate=cost(4 * total * width * units),
        name="gate_up",
    )(first, last, in_vmem(gate_weight), in_vmem(up_weight))


def down_kernel(rows, hidden_ref, down_ref, *outs):
    count, width = outs[0].shape
    tail = down_ref.shape[1] // rows
    blocks = (hidden_ref.shape[0] // rows, rows, tail)
    last = lax.broadcasted_iota(jnp.int32, blocks, 1) == rows - 1
    hidden = hidden_ref[...]
    ends = None
    for first in (rows // 2, 0):
        wide = jnp.dot(hidden, down_ref[:, first * tail:(first + rows // 2) * tail], preferred_element_type=jnp.float32)
        if ends is None:
            ends = wide[:, -tail:].reshape(blocks)
        for i in range(first, min(first + rows // 2, rows - 1)):
            value = wide[:, (i - first) * tail:(i - first + 1) * tail].reshape(blocks)
            value = jnp.where(last, jnp.broadcast_to(ends[:, i:i + 1, :], blocks), value).reshape(blocks[0] * rows, tail)
            for k, ref in enumerate(outs):
                ref[:, i * tail:(i + 1) * tail] = value[k * count:(k + 1) * count].astype(ref.dtype)


def down(hidden, down_weight, span, pair, rows):
    total, units = hidden.shape
    width = down_weight.shape[1] // rows * (rows - 1)
    shape = (total // (span * pair), width)
    outs = pl.pallas_call(
        functools.partial(down_kernel, rows),
        in_specs=[pl.BlockSpec(memory_space=pltpu.VMEM)] * 2,
        out_shape=[jax.ShapeDtypeStruct(shape, jnp.bfloat16 if p else jnp.float32) for p in range(pair) for _ in range(span)],
        compiler_params=params(total),
        cost_estimate=cost(2 * total * width * units),
        name="down",
    )(hidden, in_vmem(down_weight))
    return [outs[t::span] for t in range(span)]


def pair_sum_kernel(count, places, *refs):
    outs = refs[-len(places):]
    rows = outs[0].shape[0]
    for place, out_ref in zip(places, outs):
        part = slice(place * rows, (place + 1) * rows)
        value = refs[0][part, :]
        for ref in refs[1:count]:
            value += ref[part, :].astype(jnp.float32)
        out_ref[...] = value.astype(out_ref.dtype)


def pair_sum(arrays, rows, dtype, places, after=()):
    width = arrays[0].shape[1]
    return pl.pallas_call(
        functools.partial(pair_sum_kernel, len(arrays), places),
        in_specs=[pl.BlockSpec(memory_space=pltpu.VMEM)] * len(arrays) + [pl.BlockSpec(memory_space=pl.ANY)] * len(after),
        out_shape=[jax.ShapeDtypeStruct((rows, width), dtype)] * len(places),
        compiler_params=params(),
        name="pair_sum",
    )(*arrays, *after)


def span_sum_kernel(*refs):
    value = refs[0][...]
    for ref in refs[1:-1]:
        value += ref[...].astype(jnp.float32)
    refs[-1][...] = value.astype(refs[-1].dtype)


def span_sum(arrays):
    return pl.pallas_call(
        span_sum_kernel,
        out_shape=jax.ShapeDtypeStruct(arrays[0].shape, jnp.bfloat16),
        compiler_params=params(),
        name="span_sum",
    )(*arrays)


def pack_kernel(own_expert, tokens_hbm, ids_hbm, weights_hbm, sides_ref, *refs):
    packed_refs, (tokens_ref, ids_ref, weights_ref, semaphores) = refs[:EXPERTS], refs[EXPERTS:]
    pairs = [(tokens_hbm, tokens_ref), (ids_hbm, ids_ref), (weights_hbm, weights_ref)]
    copies = [pltpu.make_async_copy(src, dst, semaphores.at[i]) for i, (src, dst) in enumerate(pairs)]
    for copy in copies:
        copy.start()
    for copy in copies:
        copy.wait()
    ids, weights = ids_ref[...], weights_ref[...]
    rows, width = tokens_ref.shape
    tail = width // rows
    square = (rows, rows)
    row, column = lax.broadcasted_iota(jnp.int32, square, 0), lax.broadcasted_iota(jnp.int32, square, 1)
    last = lax.broadcasted_iota(jnp.int32, (rows, tail), 0) == rows - 1
    here = tokens_ref[...].astype(jnp.float32)
    below = pltpu.roll(here, rows - 1, 0)
    for s, packed_ref in enumerate(packed_refs):
        expert = lax.bitwise_xor(own_expert[0], s)
        named = ids == expert
        chosen = jnp.sum(jnp.where(named, weights, 0.0), axis=0, keepdims=True)
        coeff = jnp.sum(jnp.where(row == column, jnp.broadcast_to(chosen, square), 0.0), axis=1, keepdims=True)
        unnamed = 1.0 - jnp.sum(jnp.where(named, 1.0, 0.0), axis=0, keepdims=True)
        shift = jnp.max(jnp.where(column <= row, jnp.broadcast_to(unnamed, square), 0.0), axis=1, keepdims=True)
        sides_ref[:, s * LANES:(s + 1) * LANES] = jnp.broadcast_to(coeff, (rows, LANES))
        sides_ref[:, (EXPERTS + s) * LANES:(EXPERTS + s + 1) * LANES] = jnp.broadcast_to(shift, (rows, LANES))
        kept = jnp.where(shift > 0.5, below, here)
        for i in range(rows - 1):
            moved = jnp.broadcast_to(kept[i:i + 1, width - tail:], (rows, tail))
            piece = jnp.where(last, moved, kept[:, i * tail:(i + 1) * tail])
            packed_ref[:, i * tail:(i + 1) * tail] = piece.astype(jnp.bfloat16)


def pack(own_expert, tokens, ids, weights):
    rows, width = tokens.shape
    packed = jax.ShapeDtypeStruct((rows, width - width // rows), jnp.bfloat16)
    inputs = [tokens, ids.T, weights.T]
    return pl.pallas_call(
        pack_kernel,
        in_specs=[pl.BlockSpec(memory_space=pltpu.SMEM)] + [pl.BlockSpec(memory_space=pl.ANY)] * 3,
        out_shape=[jax.ShapeDtypeStruct((rows, 2 * EXPERTS * LANES), jnp.float32)] + [packed] * EXPERTS,
        scratch_shapes=[pltpu.VMEM(a.shape, a.dtype) for a in inputs] + [pltpu.SemaphoreType.DMA((len(inputs),))],
        compiler_params=params(),
        cost_estimate=cost(EXCHANGE_FLOPS),
        name="pack",
    )(own_expert, *[pltpu.with_memory_space_constraint(a, pltpu.HBM) for a in inputs])


def combine_kernel(base, places, counts, sides_ref, *refs):
    *refs, out_ref = refs
    rows, width = out_ref.shape
    tail = width // rows
    row = lax.broadcasted_iota(jnp.int32, (rows, tail), 0)
    value = None
    for ref in refs[:base]:
        value = ref[...]
    refs = refs[base:]
    for s, count in zip(places, counts):
        packed = sum([ref[...].astype(jnp.float32) for ref in refs[1:count]], refs[0][...].astype(jnp.float32))
        refs = refs[count:]
        coeff = sides_ref[:, s * LANES:s * LANES + 1]
        shifted = sides_ref[:, (EXPERTS + s) * LANES:(EXPERTS + s) * LANES + 1] > 0.5
        ends = jnp.zeros((rows, tail), jnp.float32)
        for i in range(rows - 1):
            ends = jnp.where(row == i, jnp.broadcast_to(packed[rows - 1:, i * tail:(i + 1) * tail], (rows, tail)), ends)
        whole = jnp.concatenate([packed, ends], axis=1)
        term = coeff * jnp.where(shifted, pltpu.roll(whole, 1, 0), whole)
        value = term if value is None else value + term
    out_ref[...] = value.astype(out_ref.dtype)


def combine(sides, base, places, groups, width, dtype):
    arrays = [a for group in groups for a in group]
    return pl.pallas_call(
        functools.partial(combine_kernel, len(base), tuple(places), tuple(len(g) for g in groups)),
        out_shape=jax.ShapeDtypeStruct((arrays[0].shape[0], width), dtype),
        compiler_params=params(),
        name="combine",
    )(sides, *base, *arrays)


def local(tokens, expert_ids, route_weights, gate_weight, up_weight, down_weight):
    rows, width = tokens.shape
    attn = lax.axis_size("attn")
    pair = lax.axis_size("ffn")
    span = attn // EXPERTS

    def over_experts(value, other):
        return lax.ppermute(value, "attn", [(i, (i // span ^ other) * span + i % span) for i in range(attn)])

    def over_span(value, shift):
        return lax.ppermute(value, "attn", [(i, i // span * span + (i + shift) % span) for i in range(attn)])

    def over_pair(value, shift):
        return lax.ppermute(value, "ffn", [(i, (i + shift) % pair) for i in range(pair)])

    own_expert = (lax.axis_index("attn") // span).astype(jnp.int32).reshape(1)
    sides, *packed = pack(own_expert, tokens, expert_ids, route_weights)
    column = {s: over_experts(packed[s], s) if s else packed[0] for s in range(EXPERTS)}
    column = [column[s] for s in BLOCK_ORDER]
    parts = [column] + [[over_span(b, t) for b in column] for t in range(1, span)]
    groups = [stack(column)]
    for part in parts[1:]:
        groups += [stack(part[:-1]), stack(part[-1:], (), LAST_FLOPS)]
    *others, last = [over_pair(g, p) for p in range(1, pair) for g in groups]
    first = unpack([b for part in parts for b in part] + others, rows, width)
    hidden = gate_up(first, last, gate_weight, up_weight)

    def paired(keep, sends):
        return [keep] + [over_pair(b, -p) for p, b in enumerate(sends, 1)]

    sums = [[] for _ in range(EXPERTS)]
    for t, (keep, *sends) in enumerate(down(hidden, down_weight, span, pair, rows)):
        arrays = paired(keep, sends)
        blocks = pair_sum(arrays, rows, jnp.bfloat16 if t else jnp.float32, range(EXPERTS))
        for s, block in zip(BLOCK_ORDER, blocks):
            sums[s].append(over_span(block, -t) if t else block)

    returned = {s: over_experts(span_sum(sums[s]), s) for s in RETURN_ORDER}
    first, *later = RETURN_ORDER
    early = combine(sides, [], [0, first], [sums[0], [returned[first]]], width, jnp.float32)
    return combine(sides, [early], later, [[returned[s]] for s in later], width, jnp.bfloat16)


def solution(mesh):
    return jax.shard_map(
        local,
        mesh=mesh,
        in_specs=(
            P(("groups", "attn", "ffn"), None),
            P(("groups", "attn", "ffn"), None),
            P(("groups", "attn", "ffn"), None),
            P(None, ("attn", "ffn")),
            P(None, ("attn", "ffn")),
            P(("attn", "ffn"), None),
        ),
        out_specs=P(("groups", "attn", "ffn"), None),
        check_vma=False,
    )
```

```python
import functools

import jax
import jax.numpy as jnp
from jax import lax
from jax.experimental import pallas as pl
from jax.experimental.pallas import tpu as pltpu
from jax.sharding import PartitionSpec as P

EXPERTS = 4
LANES = 128
RETURN_ORDER = (3, 2, 1)
BLOCK_ORDER = (0, 3, 1, 2)
N_BLOCK = 512
LAST_FLOPS = 5_000_000_000
EXCHANGE_FLOPS = 20_000_000_000


def params(rows=0):
    return pltpu.CompilerParams(vmem_limit_bytes=4 * max(1, -(-rows // 128)) * 1024 * 1024)


def cost(flops):
    return pl.CostEstimate(flops=flops, bytes_accessed=0, transcendentals=0)


def block_of(width, most):
    size = most
    while width % size:
        size -= 128
    return size


def in_vmem(value):
    return pltpu.with_memory_space_constraint(value, pltpu.VMEM)


def joined(refs):
    return jnp.concatenate([ref[...].astype(jnp.float32) for ref in refs], axis=0)


def stack_kernel(count, *refs):
    refs[-1][...] = joined(refs[:count]).astype(jnp.bfloat16)


def stack(values, after=(), flops=0):
    rows = sum(v.shape[0] for v in values)
    return pl.pallas_call(
        functools.partial(stack_kernel, len(values)),
        in_specs=[pl.BlockSpec(memory_space=pltpu.VMEM)] * len(values) + [pl.BlockSpec(memory_space=pl.ANY)] * len(after),
        out_shape=jax.ShapeDtypeStruct((rows, values[0].shape[1]), jnp.bfloat16),
        compiler_params=params(),
        cost_estimate=cost(flops),
        name="stack",
    )(*values, *after)


def unpacked(refs, out_ref, rows):
    total, width = out_ref.shape
    tail = width // rows
    blocks = (total // rows, rows, tail)
    row = lax.broadcasted_iota(jnp.int32, blocks, 1)
    ends = jnp.zeros(blocks, jnp.float32)
    for i in range(rows - 1):
        piece = joined([ref.at[:, i * tail:(i + 1) * tail] for ref in refs])
        out_ref[:, i * tail:(i + 1) * tail] = piece.astype(jnp.bfloat16)
        ends = jnp.where(row == i, jnp.broadcast_to(piece.reshape(blocks)[:, rows - 1:, :], blocks), ends)
    out_ref[:, width - tail:] = ends.reshape(total, tail).astype(jnp.bfloat16)


def unpack_kernel(rows, *refs):
    unpacked(refs[:-1], refs[-1], rows)


def unpack(values, rows, width):
    total = sum(v.shape[0] for v in values)
    return pl.pallas_call(
        functools.partial(unpack_kernel, rows),
        out_shape=jax.ShapeDtypeStruct((total, width), jnp.bfloat16),
        compiler_params=params(total),
        cost_estimate=cost(1_000_000_000),
        name="unpack",
    )(*values)


def gate_up_kernel(n_block, first_ref, last_ref, gate_ref, up_ref, hidden_ref, rows_ref):
    rows = last_ref.shape[0]
    total, width = rows_ref.shape
    whole = total - 2 * rows
    rows_ref[:whole, :] = first_ref[:whole, :]
    tail = width // rows
    row = lax.broadcasted_iota(jnp.int32, (rows, tail), 0)
    ends = jnp.zeros((rows, tail), jnp.float32)
    for i in range(rows):
        columns = slice(i * tail, (i + 1) * tail)
        if i < rows - 1:
            piece = last_ref[:, columns].astype(jnp.float32)
            ends = jnp.where(row == i, jnp.broadcast_to(piece[rows - 1:, :], (rows, tail)), ends)
        else:
            piece = ends
        both = jnp.concatenate([first_ref[whole:, columns].astype(jnp.float32), piece], axis=0)
        rows_ref[whole:, columns] = both.astype(jnp.bfloat16)
    for n in range(0, gate_ref.shape[1], n_block):
        columns = slice(n, n + n_block)
        gate = jnp.dot(rows_ref[...], gate_ref[:, columns], preferred_element_type=jnp.float32)
        up = jnp.dot(rows_ref[...], up_ref[:, columns], preferred_element_type=jnp.float32)
        hidden_ref[:, columns] = (gate / (1.0 + jnp.exp(-gate)) * up).astype(jnp.bfloat16)


def gate_up(first, last, gate_weight, up_weight):
    total = first.shape[0] + last.shape[0]
    width, units = gate_weight.shape
    return pl.pallas_call(
        functools.partial(gate_up_kernel, block_of(units, N_BLOCK)),
        in_specs=[pl.BlockSpec(memory_space=pltpu.VMEM)] * 4,
        out_shape=jax.ShapeDtypeStruct((total, units), jnp.bfloat16),
        scratch_shapes=[pltpu.VMEM((total, width), jnp.bfloat16)],
        compiler_params=params(total),
        cost_estimate=cost(4 * total * width * units),
        name="gate_up",
    )(first, last, in_vmem(gate_weight), in_vmem(up_weight))


def down_kernel(rows, sources, hidden_ref, down_ref, *outs):
    width = outs[0].shape[1]
    tail = down_ref.shape[1] // rows
    blocks = (hidden_ref.shape[0] // rows, rows, tail)
    last = lax.broadcasted_iota(jnp.int32, blocks, 1) == rows - 1
    hidden = hidden_ref[...]
    ends = None
    for i in [rows - 2] + list(range(0, rows - 2, 2)):
        both = jnp.dot(hidden, down_ref[:, i * tail:(i + 2) * tail], preferred_element_type=jnp.float32)
        pieces = {i: both[:, :tail].reshape(blocks), i + 1: both[:, tail:].reshape(blocks)}
        if ends is None:
            ends = pieces.pop(i + 1)
        for j, value in pieces.items():
            value = jnp.where(last, jnp.broadcast_to(ends[:, j:j + 1, :], blocks), value).reshape(blocks[0] * rows, tail)
            for ref, starts in zip(outs, sources):
                taken = [value[start:start + rows] for start in starts]
                taken = jnp.concatenate(taken, axis=0) if len(taken) > 1 else taken[0]
                ref[:, j * tail:(j + 1) * tail] = taken.astype(ref.dtype)


def down(hidden, down_weight, span, pair, rows, first):
    total, units = hidden.shape
    width = down_weight.shape[1] // rows * (rows - 1)
    part = total // (span * pair)
    places = [first] + [i for i in range(part // rows) if i != first]

    def starts(p, t, chosen):
        return [(p * span + t) * part + i * rows for i in chosen]

    sources = [starts(0, t, range(part // rows)) for t in range(span)]
    for p in range(1, pair):
        sources.append([x for t in range(1, span) for x in starts(p, t, places[:1])])
        sources.append([x for t in range(1, span) for x in starts(p, t, places[1:])] + starts(p, 0, range(part // rows)))
    outs = pl.pallas_call(
        functools.partial(down_kernel, rows, sources),
        in_specs=[pl.BlockSpec(memory_space=pltpu.VMEM)] * 2,
        out_shape=[jax.ShapeDtypeStruct((rows * len(x), width), jnp.float32 if i < span else jnp.bfloat16) for i, x in enumerate(sources)],
        compiler_params=params(total),
        cost_estimate=cost(2 * total * width * units),
        name="down",
    )(hidden, in_vmem(down_weight))
    return outs[:span], outs[span::2], outs[span + 1::2]


def pair_sum_kernel(places, offset, keep_ref, *refs):
    received, outs = refs[:-len(places)], refs[-len(places):]
    rows = outs[0].shape[0]
    for i, (place, out_ref) in enumerate(zip(places, outs), offset):
        value = keep_ref[place * rows:(place + 1) * rows, :]
        for ref in received:
            value += ref[i * rows:(i + 1) * rows, :].astype(jnp.float32)
        out_ref[...] = value.astype(out_ref.dtype)


def pair_sum(keep, received, rows, dtype, places, offset):
    return pl.pallas_call(
        functools.partial(pair_sum_kernel, places, offset),
        out_shape=[jax.ShapeDtypeStruct((rows, keep.shape[1]), dtype)] * len(places),
        compiler_params=params(),
        name="pair_sum",
    )(keep, *received)


def span_sum_kernel(*refs):
    value = refs[0][...]
    for ref in refs[1:-1]:
        value += ref[...].astype(jnp.float32)
    refs[-1][...] = value.astype(refs[-1].dtype)


def span_sum(arrays):
    return pl.pallas_call(
        span_sum_kernel,
        out_shape=jax.ShapeDtypeStruct(arrays[0].shape, jnp.bfloat16),
        compiler_params=params(),
        name="span_sum",
    )(*arrays)


def pack_kernel(own_expert, tokens_hbm, ids_hbm, weights_hbm, sides_ref, *refs):
    packed_refs, (tokens_ref, ids_ref, weights_ref, semaphores) = refs[:EXPERTS], refs[EXPERTS:]
    pairs = [(tokens_hbm, tokens_ref), (ids_hbm, ids_ref), (weights_hbm, weights_ref)]
    copies = [pltpu.make_async_copy(src, dst, semaphores.at[i]) for i, (src, dst) in enumerate(pairs)]
    for copy in copies:
        copy.start()
    for copy in copies:
        copy.wait()
    ids, weights = ids_ref[...], weights_ref[...]
    rows, width = tokens_ref.shape
    tail = width // rows
    square = (rows, rows)
    row, column = lax.broadcasted_iota(jnp.int32, square, 0), lax.broadcasted_iota(jnp.int32, square, 1)
    last = lax.broadcasted_iota(jnp.int32, (rows, tail), 0) == rows - 1
    here = tokens_ref[...].astype(jnp.float32)
    below = pltpu.roll(here, rows - 1, 0)
    for s, packed_ref in enumerate(packed_refs):
        expert = lax.bitwise_xor(own_expert[0], s)
        named = ids == expert
        chosen = jnp.sum(jnp.where(named, weights, 0.0), axis=0, keepdims=True)
        coeff = jnp.sum(jnp.where(row == column, jnp.broadcast_to(chosen, square), 0.0), axis=1, keepdims=True)
        unnamed = 1.0 - jnp.sum(jnp.where(named, 1.0, 0.0), axis=0, keepdims=True)
        shift = jnp.max(jnp.where(column <= row, jnp.broadcast_to(unnamed, square), 0.0), axis=1, keepdims=True)
        sides_ref[:, s * LANES:(s + 1) * LANES] = jnp.broadcast_to(coeff, (rows, LANES))
        sides_ref[:, (EXPERTS + s) * LANES:(EXPERTS + s + 1) * LANES] = jnp.broadcast_to(shift, (rows, LANES))
        kept = jnp.where(shift > 0.5, below, here)
        for i in range(rows - 1):
            moved = jnp.broadcast_to(kept[i:i + 1, width - tail:], (rows, tail))
            piece = jnp.where(last, moved, kept[:, i * tail:(i + 1) * tail])
            packed_ref[:, i * tail:(i + 1) * tail] = piece.astype(jnp.bfloat16)


def pack(own_expert, tokens, ids, weights):
    rows, width = tokens.shape
    packed = jax.ShapeDtypeStruct((rows, width - width // rows), jnp.bfloat16)
    inputs = [tokens, ids.T, weights.T]
    return pl.pallas_call(
        pack_kernel,
        in_specs=[pl.BlockSpec(memory_space=pltpu.SMEM)] + [pl.BlockSpec(memory_space=pl.ANY)] * 3,
        out_shape=[jax.ShapeDtypeStruct((rows, 2 * EXPERTS * LANES), jnp.float32)] + [packed] * EXPERTS,
        scratch_shapes=[pltpu.VMEM(a.shape, a.dtype) for a in inputs] + [pltpu.SemaphoreType.DMA((len(inputs),))],
        compiler_params=params(),
        cost_estimate=cost(EXCHANGE_FLOPS),
        name="pack",
    )(own_expert, *[pltpu.with_memory_space_constraint(a, pltpu.HBM) for a in inputs])


def combine_kernel(base, places, counts, parts, sides_ref, *refs):
    if parts:
        *refs, out_hbm, out_ref, semaphores = refs
    else:
        *refs, out_ref = refs
    rows, width = out_ref.shape
    tail = width // rows
    row = lax.broadcasted_iota(jnp.int32, (rows, tail), 0)
    first, groups = refs[:base], refs[base:]
    terms = []
    for s, count in zip(places, counts):
        group, groups = groups[:count], groups[count:]
        packed = sum([ref[...].astype(jnp.float32) for ref in group[1:]], group[0][...].astype(jnp.float32))
        coeff = sides_ref[:, s * LANES:s * LANES + 1]
        shifted = sides_ref[:, (EXPERTS + s) * LANES:(EXPERTS + s) * LANES + 1] > 0.5
        terms.append((packed, coeff, shifted))
    copies = []
    for i in range(rows):
        columns = slice(i * tail, (i + 1) * tail)
        value = None
        for ref in first:
            value = ref[:, columns]
        for packed, coeff, shifted in terms:
            if i < rows - 1:
                piece = packed[:, columns]
            else:
                piece = jnp.zeros((rows, tail), jnp.float32)
                for j in range(rows - 1):
                    moved = jnp.broadcast_to(packed[rows - 1:, j * tail:(j + 1) * tail], (rows, tail))
                    piece = jnp.where(row == j, moved, piece)
            term = coeff * jnp.where(shifted, pltpu.roll(piece, 1, 0), piece)
            value = term if value is None else value + term
        out_ref[:, columns] = value.astype(out_ref.dtype)
        if parts and (i + 1) % (rows // parts) == 0:
            done = slice((len(copies) * (rows // parts)) * tail, (i + 1) * tail)
            copies.append(pltpu.make_async_copy(out_ref.at[:, done], out_hbm.at[:, done], semaphores.at[len(copies)]))
            copies[-1].start()
    for copy in copies:
        copy.wait()


def combine(sides, base, places, groups, width, dtype, parts=0):
    arrays = [a for group in groups for a in group]
    out_shape = jax.ShapeDtypeStruct((arrays[0].shape[0], width), dtype)
    return pl.pallas_call(
        functools.partial(combine_kernel, len(base), tuple(places), tuple(len(g) for g in groups), parts),
        out_shape=out_shape,
        out_specs=pl.BlockSpec(memory_space=pl.ANY if parts else pltpu.VMEM),
        scratch_shapes=[pltpu.VMEM(out_shape.shape, dtype), pltpu.SemaphoreType.DMA((parts,))] if parts else [],
        compiler_params=params(),
        name="combine",
    )(sides, *base, *arrays)


def local(tokens, expert_ids, route_weights, gate_weight, up_weight, down_weight):
    rows, width = tokens.shape
    attn = lax.axis_size("attn")
    pair = lax.axis_size("ffn")
    span = attn // EXPERTS

    def over_experts(value, other):
        return lax.ppermute(value, "attn", [(i, (i // span ^ other) * span + i % span) for i in range(attn)])

    def over_span(value, shift):
        return lax.ppermute(value, "attn", [(i, i // span * span + (i + shift) % span) for i in range(attn)])

    def over_pair(value, shift):
        return lax.ppermute(value, "ffn", [(i, (i + shift) % pair) for i in range(pair)])

    own_expert = (lax.axis_index("attn") // span).astype(jnp.int32).reshape(1)
    sides, *packed = pack(own_expert, tokens, expert_ids, route_weights)
    column = {s: over_experts(packed[s], s) if s else packed[0] for s in range(EXPERTS)}
    column = [column[s] for s in BLOCK_ORDER]
    parts = [column] + [[over_span(b, t) for b in column] for t in range(1, span)]
    groups = [stack(column)]
    for part in parts[1:]:
        groups += [stack(part[:-1]), stack(part[-1:], (), LAST_FLOPS)]
    *others, last = [over_pair(g, p) for p in range(1, pair) for g in groups]
    first = unpack([b for part in parts for b in part] + others, rows, width)
    hidden = gate_up(first, last, gate_weight, up_weight)

    first = BLOCK_ORDER.index(RETURN_ORDER[0])
    rest = [i for i in range(EXPERTS) if i != first]
    keeps, firsts, others = down(hidden, down_weight, span, pair, rows, first)
    received = [over_pair(b, -p) for p, b in enumerate(firsts, 1)]
    sums = {s: [] for s in range(EXPERTS)}
    for t in range(1, span):
        block, = pair_sum(keeps[t], received, rows, jnp.bfloat16, [first], t - 1)
        sums[RETURN_ORDER[0]].append(over_span(block, -t))
        after = [block]
    received = [over_pair(stack([b], after), -p) for p, b in enumerate(others, 1)]
    for t in range(1, span):
        blocks = pair_sum(keeps[t], received, rows, jnp.bfloat16, rest, (t - 1) * len(rest))
        for place, block in zip(rest, blocks):
            sums[BLOCK_ORDER[place]].append(over_span(block, -t))
    own = pair_sum(keeps[0], received, rows, jnp.float32, list(range(EXPERTS)), (span - 1) * len(rest))
    for place, block in enumerate(own):
        sums[BLOCK_ORDER[place]].insert(0, block)

    returned = {s: over_experts(span_sum(sums[s]), s) for s in RETURN_ORDER}
    far, *later = RETURN_ORDER
    early = combine(sides, [], [0, far], [sums[0], [returned[far]]], width, jnp.float32)
    return combine(sides, [early], later, [[returned[s]] for s in later], width, jnp.bfloat16, 2)


def solution(mesh):
    return jax.shard_map(
        local,
        mesh=mesh,
        in_specs=(
            P(("groups", "attn", "ffn"), None),
            P(("groups", "attn", "ffn"), None),
            P(("groups", "attn", "ffn"), None),
            P(None, ("attn", "ffn")),
            P(None, ("attn", "ffn")),
            P(("attn", "ffn"), None),
        ),
        out_specs=P(("groups", "attn", "ffn"), None),
        check_vma=False,
    )
```

```python
import functools

import jax
import jax.numpy as jnp
from jax import lax
from jax.experimental import pallas as pl
from jax.experimental.pallas import tpu as pltpu
from jax.sharding import PartitionSpec as P

EXPERTS = 4
LANES = 128
RETURN_ORDER = (3, 2, 1)
BLOCK_ORDER = (0, 3, 1, 2)
N_BLOCK = 512
LAST_FLOPS = 5_000_000_000
EXCHANGE_FLOPS = 20_000_000_000


def params(rows=0):
    return pltpu.CompilerParams(vmem_limit_bytes=4 * max(1, -(-rows // 128)) * 1024 * 1024)


def cost(flops):
    return pl.CostEstimate(flops=flops, bytes_accessed=0, transcendentals=0)


def block_of(width, most):
    size = most
    while width % size:
        size -= 128
    return size


def in_vmem(value):
    return pltpu.with_memory_space_constraint(value, pltpu.VMEM)


def joined(refs):
    return jnp.concatenate([ref[...].astype(jnp.float32) for ref in refs], axis=0)


def stack_kernel(count, *refs):
    refs[-1][...] = joined(refs[:count]).astype(jnp.bfloat16)


def stack(values, after=(), flops=0):
    rows = sum(v.shape[0] for v in values)
    return pl.pallas_call(
        functools.partial(stack_kernel, len(values)),
        in_specs=[pl.BlockSpec(memory_space=pltpu.VMEM)] * len(values) + [pl.BlockSpec(memory_space=pl.ANY)] * len(after),
        out_shape=jax.ShapeDtypeStruct((rows, values[0].shape[1]), jnp.bfloat16),
        compiler_params=params(),
        cost_estimate=cost(flops),
        name="stack",
    )(*values, *after)


def unpacked(refs, out_ref, rows):
    total, width = out_ref.shape
    tail = width // rows
    blocks = (total // rows, rows, tail)
    row = lax.broadcasted_iota(jnp.int32, blocks, 1)
    ends = jnp.zeros(blocks, jnp.float32)
    for i in range(rows - 1):
        piece = joined([ref.at[:, i * tail:(i + 1) * tail] for ref in refs])
        out_ref[:, i * tail:(i + 1) * tail] = piece.astype(jnp.bfloat16)
        ends = jnp.where(row == i, jnp.broadcast_to(piece.reshape(blocks)[:, rows - 1:, :], blocks), ends)
    out_ref[:, width - tail:] = ends.reshape(total, tail).astype(jnp.bfloat16)


def unpack_kernel(rows, *refs):
    unpacked(refs[:-1], refs[-1], rows)


def unpack(values, rows, width):
    total = sum(v.shape[0] for v in values)
    return pl.pallas_call(
        functools.partial(unpack_kernel, rows),
        out_shape=jax.ShapeDtypeStruct((total, width), jnp.bfloat16),
        compiler_params=params(total),
        cost_estimate=cost(1_000_000_000),
        name="unpack",
    )(*values)


def gate_up_kernel(n_block, first_ref, last_ref, gate_ref, up_ref, hidden_ref, rows_ref):
    rows = last_ref.shape[0]
    total, width = rows_ref.shape
    whole = total - 2 * rows
    rows_ref[:whole, :] = first_ref[:whole, :]
    tail = width // rows
    row = lax.broadcasted_iota(jnp.int32, (rows, tail), 0)
    ends = jnp.zeros((rows, tail), jnp.float32)
    for i in range(rows):
        columns = slice(i * tail, (i + 1) * tail)
        if i < rows - 1:
            piece = last_ref[:, columns].astype(jnp.float32)
            ends = jnp.where(row == i, jnp.broadcast_to(piece[rows - 1:, :], (rows, tail)), ends)
        else:
            piece = ends
        both = jnp.concatenate([first_ref[whole:, columns].astype(jnp.float32), piece], axis=0)
        rows_ref[whole:, columns] = both.astype(jnp.bfloat16)
    for n in range(0, gate_ref.shape[1], n_block):
        columns = slice(n, n + n_block)
        gate = jnp.dot(rows_ref[...], gate_ref[:, columns], preferred_element_type=jnp.float32)
        up = jnp.dot(rows_ref[...], up_ref[:, columns], preferred_element_type=jnp.float32)
        hidden_ref[:, columns] = (gate / (1.0 + jnp.exp(-gate)) * up).astype(jnp.bfloat16)


def gate_up(first, last, gate_weight, up_weight):
    total = first.shape[0] + last.shape[0]
    width, units = gate_weight.shape
    return pl.pallas_call(
        functools.partial(gate_up_kernel, block_of(units, N_BLOCK)),
        in_specs=[pl.BlockSpec(memory_space=pltpu.VMEM)] * 4,
        out_shape=jax.ShapeDtypeStruct((total, units), jnp.bfloat16),
        scratch_shapes=[pltpu.VMEM((total, width), jnp.bfloat16)],
        compiler_params=params(total),
        cost_estimate=cost(4 * total * width * units),
        name="gate_up",
    )(first, last, in_vmem(gate_weight), in_vmem(up_weight))


def down_kernel(rows, sources, hidden_ref, down_ref, *outs):
    width = outs[0].shape[1]
    tail = down_ref.shape[1] // rows
    blocks = (hidden_ref.shape[0] // rows, rows, tail)
    last = lax.broadcasted_iota(jnp.int32, blocks, 1) == rows - 1
    hidden = hidden_ref[...]
    ends = None
    for i in [rows - 2] + list(range(0, rows - 2, 2)):
        both = jnp.dot(hidden, down_ref[:, i * tail:(i + 2) * tail], preferred_element_type=jnp.float32)
        pieces = {i: both[:, :tail].reshape(blocks), i + 1: both[:, tail:].reshape(blocks)}
        if ends is None:
            ends = pieces.pop(i + 1)
        for j, value in pieces.items():
            value = jnp.where(last, jnp.broadcast_to(ends[:, j:j + 1, :], blocks), value).reshape(blocks[0] * rows, tail)
            for ref, starts in zip(outs, sources):
                taken = [value[start:start + rows] for start in starts]
                taken = jnp.concatenate(taken, axis=0) if len(taken) > 1 else taken[0]
                ref[:, j * tail:(j + 1) * tail] = taken.astype(ref.dtype)


def down(hidden, down_weight, span, pair, rows, first):
    total, units = hidden.shape
    width = down_weight.shape[1] // rows * (rows - 1)
    part = total // (span * pair)
    places = [first] + [i for i in range(part // rows) if i != first]

    def starts(p, t, chosen):
        return [(p * span + t) * part + i * rows for i in chosen]

    sources = [starts(0, t, range(part // rows)) for t in range(span)]
    for p in range(1, pair):
        sources.append([x for t in range(1, span) for x in starts(p, t, places[:1])])
        sources.append([x for t in range(1, span) for x in starts(p, t, places[1:])] + starts(p, 0, range(part // rows)))
    outs = pl.pallas_call(
        functools.partial(down_kernel, rows, sources),
        in_specs=[pl.BlockSpec(memory_space=pltpu.VMEM)] * 2,
        out_shape=[jax.ShapeDtypeStruct((rows * len(x), width), jnp.float32 if i < span else jnp.bfloat16) for i, x in enumerate(sources)],
        compiler_params=params(total),
        cost_estimate=cost(2 * total * width * units),
        name="down",
    )(hidden, in_vmem(down_weight))
    return outs[:span], outs[span::2], outs[span + 1::2]


def pair_sum_kernel(count, places, indices, keep_ref, *refs):
    received, outs = refs[:count], refs[-len(places):]
    rows = outs[0].shape[0]
    for place, i, out_ref in zip(places, indices, outs):
        value = keep_ref[place * rows:(place + 1) * rows, :]
        for ref in received:
            value += ref[i * rows:(i + 1) * rows, :].astype(jnp.float32)
        out_ref[...] = value.astype(out_ref.dtype)


def pair_sum(keep, received, rows, dtype, places, indices, after=()):
    vmem = [pl.BlockSpec(memory_space=pltpu.VMEM)] * (1 + len(received))
    return pl.pallas_call(
        functools.partial(pair_sum_kernel, len(received), places, indices),
        in_specs=vmem + [pl.BlockSpec(memory_space=pl.ANY)] * len(after),
        out_shape=[jax.ShapeDtypeStruct((rows, keep.shape[1]), dtype)] * len(places),
        compiler_params=params(),
        name="pair_sum",
    )(keep, *received, *after)


def span_sum_kernel(*refs):
    value = refs[0][...]
    for ref in refs[1:-1]:
        value += ref[...].astype(jnp.float32)
    refs[-1][...] = value.astype(refs[-1].dtype)


def span_sum(arrays):
    return pl.pallas_call(
        span_sum_kernel,
        out_shape=jax.ShapeDtypeStruct(arrays[0].shape, jnp.bfloat16),
        compiler_params=params(),
        name="span_sum",
    )(*arrays)


def pack_kernel(own_expert, tokens_hbm, ids_hbm, weights_hbm, sides_ref, *refs):
    packed_refs, (tokens_ref, ids_ref, weights_ref, semaphores) = refs[:EXPERTS], refs[EXPERTS:]
    pairs = [(tokens_hbm, tokens_ref), (ids_hbm, ids_ref), (weights_hbm, weights_ref)]
    copies = [pltpu.make_async_copy(src, dst, semaphores.at[i]) for i, (src, dst) in enumerate(pairs)]
    for copy in copies:
        copy.start()
    for copy in copies:
        copy.wait()
    ids, weights = ids_ref[...], weights_ref[...]
    rows, width = tokens_ref.shape
    tail = width // rows
    square = (rows, rows)
    row, column = lax.broadcasted_iota(jnp.int32, square, 0), lax.broadcasted_iota(jnp.int32, square, 1)
    last = lax.broadcasted_iota(jnp.int32, (rows, tail), 0) == rows - 1
    here = tokens_ref[...].astype(jnp.float32)
    below = pltpu.roll(here, rows - 1, 0)
    for s, packed_ref in enumerate(packed_refs):
        expert = lax.bitwise_xor(own_expert[0], s)
        named = ids == expert
        chosen = jnp.sum(jnp.where(named, weights, 0.0), axis=0, keepdims=True)
        coeff = jnp.sum(jnp.where(row == column, jnp.broadcast_to(chosen, square), 0.0), axis=1, keepdims=True)
        unnamed = 1.0 - jnp.sum(jnp.where(named, 1.0, 0.0), axis=0, keepdims=True)
        shift = jnp.max(jnp.where(column <= row, jnp.broadcast_to(unnamed, square), 0.0), axis=1, keepdims=True)
        sides_ref[:, s * LANES:(s + 1) * LANES] = jnp.broadcast_to(coeff, (rows, LANES))
        sides_ref[:, (EXPERTS + s) * LANES:(EXPERTS + s + 1) * LANES] = jnp.broadcast_to(shift, (rows, LANES))
        kept = jnp.where(shift > 0.5, below, here)
        for i in range(rows - 1):
            moved = jnp.broadcast_to(kept[i:i + 1, width - tail:], (rows, tail))
            piece = jnp.where(last, moved, kept[:, i * tail:(i + 1) * tail])
            packed_ref[:, i * tail:(i + 1) * tail] = piece.astype(jnp.bfloat16)


def pack(own_expert, tokens, ids, weights):
    rows, width = tokens.shape
    packed = jax.ShapeDtypeStruct((rows, width - width // rows), jnp.bfloat16)
    inputs = [tokens, ids.T, weights.T]
    return pl.pallas_call(
        pack_kernel,
        in_specs=[pl.BlockSpec(memory_space=pltpu.SMEM)] + [pl.BlockSpec(memory_space=pl.ANY)] * 3,
        out_shape=[jax.ShapeDtypeStruct((rows, 2 * EXPERTS * LANES), jnp.float32)] + [packed] * EXPERTS,
        scratch_shapes=[pltpu.VMEM(a.shape, a.dtype) for a in inputs] + [pltpu.SemaphoreType.DMA((len(inputs),))],
        compiler_params=params(),
        cost_estimate=cost(EXCHANGE_FLOPS),
        name="pack",
    )(own_expert, *[pltpu.with_memory_space_constraint(a, pltpu.HBM) for a in inputs])


def combine_kernel(base, places, counts, parts, sides_ref, *refs):
    if parts:
        *refs, out_hbm, out_ref, semaphores = refs
    else:
        *refs, out_ref = refs
    rows, width = out_ref.shape
    tail = width // rows
    row = lax.broadcasted_iota(jnp.int32, (rows, tail), 0)
    first, groups = refs[:base], refs[base:]
    terms = []
    for s, count in zip(places, counts):
        group, groups = groups[:count], groups[count:]
        packed = sum([ref[...].astype(jnp.float32) for ref in group[1:]], group[0][...].astype(jnp.float32))
        coeff = sides_ref[:, s * LANES:s * LANES + 1]
        shifted = sides_ref[:, (EXPERTS + s) * LANES:(EXPERTS + s) * LANES + 1] > 0.5
        terms.append((packed, coeff, shifted))
    copies = []
    for i in range(rows):
        columns = slice(i * tail, (i + 1) * tail)
        value = None
        for ref in first:
            value = ref[:, columns]
        for packed, coeff, shifted in terms:
            if i < rows - 1:
                piece = packed[:, columns]
            else:
                piece = jnp.zeros((rows, tail), jnp.float32)
                for j in range(rows - 1):
                    moved = jnp.broadcast_to(packed[rows - 1:, j * tail:(j + 1) * tail], (rows, tail))
                    piece = jnp.where(row == j, moved, piece)
            term = coeff * jnp.where(shifted, pltpu.roll(piece, 1, 0), piece)
            value = term if value is None else value + term
        out_ref[:, columns] = value.astype(out_ref.dtype)
        if parts and (i + 1) % (rows // parts) == 0:
            done = slice((len(copies) * (rows // parts)) * tail, (i + 1) * tail)
            copies.append(pltpu.make_async_copy(out_ref.at[:, done], out_hbm.at[:, done], semaphores.at[len(copies)]))
            copies[-1].start()
    for copy in copies:
        copy.wait()


def combine(sides, base, places, groups, width, dtype, parts=0):
    arrays = [a for group in groups for a in group]
    out_shape = jax.ShapeDtypeStruct((arrays[0].shape[0], width), dtype)
    return pl.pallas_call(
        functools.partial(combine_kernel, len(base), tuple(places), tuple(len(g) for g in groups), parts),
        out_shape=out_shape,
        out_specs=pl.BlockSpec(memory_space=pl.ANY if parts else pltpu.VMEM),
        scratch_shapes=[pltpu.VMEM(out_shape.shape, dtype), pltpu.SemaphoreType.DMA((parts,))] if parts else [],
        compiler_params=params(),
        name="combine",
    )(sides, *base, *arrays)


def local(tokens, expert_ids, route_weights, gate_weight, up_weight, down_weight):
    rows, width = tokens.shape
    attn = lax.axis_size("attn")
    pair = lax.axis_size("ffn")
    span = attn // EXPERTS

    def over_experts(value, other):
        return lax.ppermute(value, "attn", [(i, (i // span ^ other) * span + i % span) for i in range(attn)])

    def over_span(value, shift):
        return lax.ppermute(value, "attn", [(i, i // span * span + (i + shift) % span) for i in range(attn)])

    def over_pair(value, shift):
        return lax.ppermute(value, "ffn", [(i, (i + shift) % pair) for i in range(pair)])

    own_expert = (lax.axis_index("attn") // span).astype(jnp.int32).reshape(1)
    sides, *packed = pack(own_expert, tokens, expert_ids, route_weights)
    column = {s: over_experts(packed[s], s) if s else packed[0] for s in range(EXPERTS)}
    column = [column[s] for s in BLOCK_ORDER]
    parts = [column] + [[over_span(b, t) for b in column] for t in range(1, span)]
    groups = [stack(column)]
    for part in parts[1:]:
        groups += [stack(part[:-1]), stack(part[-1:], (), LAST_FLOPS)]
    *others, last = [over_pair(g, p) for p in range(1, pair) for g in groups]
    first = unpack([b for part in parts for b in part] + others, rows, width)
    hidden = gate_up(first, last, gate_weight, up_weight)

    first = BLOCK_ORDER.index(RETURN_ORDER[0])
    rest = [i for i in range(EXPERTS) if i != first]
    keeps, firsts, others = down(hidden, down_weight, span, pair, rows, first)
    received = [over_pair(b, -p) for p, b in enumerate(firsts, 1)]
    sums, after = {s: [] for s in range(EXPERTS)}, []
    for t in range(1, span):
        after += pair_sum(keeps[t], received, rows, jnp.bfloat16, [first], [t - 1])
        sums[RETURN_ORDER[0]].append(over_span(after[-1], -t))
    received = [over_pair(stack([b], after[:1]), -p) for p, b in enumerate(others, 1)]
    own = pair_sum(keeps[0], received, rows, jnp.float32, range(EXPERTS), [(span - 1) * len(rest) + i for i in range(EXPERTS)])
    for place, block in enumerate(own):
        sums[BLOCK_ORDER[place]].insert(0, block)

    def send_rest(planes, after):
        for t in range(1, span):
            places = [BLOCK_ORDER.index(s) for s in planes]
            indices = [(t - 1) * len(rest) + rest.index(place) for place in places]
            blocks = pair_sum(keeps[t], received, rows, jnp.bfloat16, places, indices, after)
            for s, block in zip(planes, blocks):
                sums[s].append(over_span(block, -t))

    send_rest(RETURN_ORDER[1:], [])
    totals = {s: span_sum(sums[s]) for s in RETURN_ORDER}
    send_rest([0], [totals[RETURN_ORDER[1]]])
    returned = {s: over_experts(totals[s], s) for s in RETURN_ORDER}
    far, *later = RETURN_ORDER
    early = combine(sides, [], [0, far], [sums[0], [returned[far]]], width, jnp.float32)
    return combine(sides, [early], later, [[returned[s]] for s in later], width, jnp.bfloat16, 2)


def solution(mesh):
    return jax.shard_map(
        local,
        mesh=mesh,
        in_specs=(
            P(("groups", "attn", "ffn"), None),
            P(("groups", "attn", "ffn"), None),
            P(("groups", "attn", "ffn"), None),
            P(None, ("attn", "ffn")),
            P(None, ("attn", "ffn")),
            P(("attn", "ffn"), None),
        ),
        out_specs=P(("groups", "attn", "ffn"), None),
        check_vma=False,
    )
```

```python
import functools

import jax
import jax.numpy as jnp
from jax import lax
from jax.experimental import pallas as pl
from jax.experimental.pallas import tpu as pltpu
from jax.sharding import PartitionSpec as P

EXPERTS = 4
LANES = 128
RETURN_ORDER = (3, 2, 1)
BLOCK_ORDER = (0, 3, 1, 2)
N_BLOCK = 512
LAST_FLOPS = 5_000_000_000
EXCHANGE_FLOPS = 20_000_000_000


def params(rows=0):
    return pltpu.CompilerParams(vmem_limit_bytes=4 * max(1, -(-rows // 128)) * 1024 * 1024)


def cost(flops):
    return pl.CostEstimate(flops=flops, bytes_accessed=0, transcendentals=0)


def block_of(width, most):
    size = most
    while width % size:
        size -= 128
    return size


def in_vmem(value):
    return pltpu.with_memory_space_constraint(value, pltpu.VMEM)


def joined(refs):
    return jnp.concatenate([ref[...].astype(jnp.float32) for ref in refs], axis=0)


def stack_kernel(count, *refs):
    refs[-1][...] = joined(refs[:count]).astype(jnp.bfloat16)


def stack(values, after=(), flops=0):
    rows = sum(v.shape[0] for v in values)
    return pl.pallas_call(
        functools.partial(stack_kernel, len(values)),
        in_specs=[pl.BlockSpec(memory_space=pltpu.VMEM)] * len(values) + [pl.BlockSpec(memory_space=pl.ANY)] * len(after),
        out_shape=jax.ShapeDtypeStruct((rows, values[0].shape[1]), jnp.bfloat16),
        compiler_params=params(),
        cost_estimate=cost(flops),
        name="stack",
    )(*values, *after)


def unpacked(refs, out_ref, rows):
    total, width = out_ref.shape
    tail = width // rows
    blocks = (total // rows, rows, tail)
    row = lax.broadcasted_iota(jnp.int32, blocks, 1)
    ends = jnp.zeros(blocks, jnp.float32)
    for i in range(rows - 1):
        piece = joined([ref.at[:, i * tail:(i + 1) * tail] for ref in refs])
        out_ref[:, i * tail:(i + 1) * tail] = piece.astype(jnp.bfloat16)
        ends = jnp.where(row == i, jnp.broadcast_to(piece.reshape(blocks)[:, rows - 1:, :], blocks), ends)
    out_ref[:, width - tail:] = ends.reshape(total, tail).astype(jnp.bfloat16)


def unpack_kernel(rows, *refs):
    unpacked(refs[:-1], refs[-1], rows)


def unpack(values, rows, width):
    total = sum(v.shape[0] for v in values)
    return pl.pallas_call(
        functools.partial(unpack_kernel, rows),
        out_shape=jax.ShapeDtypeStruct((total, width), jnp.bfloat16),
        compiler_params=params(total),
        cost_estimate=cost(1_000_000_000),
        name="unpack",
    )(*values)


def gate_up_kernel(n_block, first_ref, last_ref, gate_ref, up_ref, hidden_ref, rows_ref):
    rows = last_ref.shape[0]
    total, width = rows_ref.shape
    whole = total - 2 * rows
    rows_ref[:whole, :] = first_ref[:whole, :]
    tail = width // rows
    row = lax.broadcasted_iota(jnp.int32, (rows, tail), 0)
    ends = jnp.zeros((rows, tail), jnp.float32)
    for i in range(rows):
        columns = slice(i * tail, (i + 1) * tail)
        if i < rows - 1:
            piece = last_ref[:, columns].astype(jnp.float32)
            ends = jnp.where(row == i, jnp.broadcast_to(piece[rows - 1:, :], (rows, tail)), ends)
        else:
            piece = ends
        both = jnp.concatenate([first_ref[whole:, columns].astype(jnp.float32), piece], axis=0)
        rows_ref[whole:, columns] = both.astype(jnp.bfloat16)
    for n in range(0, gate_ref.shape[1], n_block):
        columns = slice(n, n + n_block)
        gate = jnp.dot(rows_ref[...], gate_ref[:, columns], preferred_element_type=jnp.float32)
        up = jnp.dot(rows_ref[...], up_ref[:, columns], preferred_element_type=jnp.float32)
        hidden_ref[:, columns] = (gate / (1.0 + jnp.exp(-gate)) * up).astype(jnp.bfloat16)


def gate_up(first, last, gate_weight, up_weight):
    total = first.shape[0] + last.shape[0]
    width, units = gate_weight.shape
    return pl.pallas_call(
        functools.partial(gate_up_kernel, block_of(units, N_BLOCK)),
        in_specs=[pl.BlockSpec(memory_space=pltpu.VMEM)] * 4,
        out_shape=jax.ShapeDtypeStruct((total, units), jnp.bfloat16),
        scratch_shapes=[pltpu.VMEM((total, width), jnp.bfloat16)],
        compiler_params=params(total),
        cost_estimate=cost(4 * total * width * units),
        name="gate_up",
    )(first, last, in_vmem(gate_weight), in_vmem(up_weight))


def down_kernel(rows, sources, hidden_ref, down_ref, *outs):
    width = outs[0].shape[1]
    tail = down_ref.shape[1] // rows
    blocks = (hidden_ref.shape[0] // rows, rows, tail)
    last = lax.broadcasted_iota(jnp.int32, blocks, 1) == rows - 1
    hidden = hidden_ref[...]
    ends = None
    for i in [rows - 2] + list(range(0, rows - 2, 2)):
        both = jnp.dot(hidden, down_ref[:, i * tail:(i + 2) * tail], preferred_element_type=jnp.float32)
        pieces = {i: both[:, :tail].reshape(blocks), i + 1: both[:, tail:].reshape(blocks)}
        if ends is None:
            ends = pieces.pop(i + 1)
        for j, value in pieces.items():
            value = jnp.where(last, jnp.broadcast_to(ends[:, j:j + 1, :], blocks), value).reshape(blocks[0] * rows, tail)
            for ref, starts in zip(outs, sources):
                taken = [value[start:start + rows] for start in starts]
                taken = jnp.concatenate(taken, axis=0) if len(taken) > 1 else taken[0]
                ref[:, j * tail:(j + 1) * tail] = taken.astype(ref.dtype)


def down(hidden, down_weight, span, pair, rows, first):
    total, units = hidden.shape
    width = down_weight.shape[1] // rows * (rows - 1)
    part = total // (span * pair)
    places = [first] + [i for i in range(part // rows) if i != first]

    def starts(p, t, chosen):
        return [(p * span + t) * part + i * rows for i in chosen]

    sources = [starts(0, t, range(part // rows)) for t in range(span)]
    for p in range(1, pair):
        sources.append([x for t in range(1, span) for x in starts(p, t, places[:1])])
        sources.append([x for t in range(1, span) for x in starts(p, t, places[1:])] + starts(p, 0, range(part // rows)))
    outs = pl.pallas_call(
        functools.partial(down_kernel, rows, sources),
        in_specs=[pl.BlockSpec(memory_space=pltpu.VMEM)] * 2,
        out_shape=[jax.ShapeDtypeStruct((rows * len(x), width), jnp.float32 if i < span else jnp.bfloat16) for i, x in enumerate(sources)],
        compiler_params=params(total),
        cost_estimate=cost(2 * total * width * units),
        name="down",
    )(hidden, in_vmem(down_weight))
    return outs[:span], outs[span::2], outs[span + 1::2]


def pair_sum_kernel(count, places, indices, keep_ref, *refs):
    received, outs = refs[:count], refs[-len(places):]
    rows = outs[0].shape[0]
    for place, i, out_ref in zip(places, indices, outs):
        value = keep_ref[place * rows:(place + 1) * rows, :]
        for ref in received:
            value += ref[i * rows:(i + 1) * rows, :].astype(jnp.float32)
        out_ref[...] = value.astype(out_ref.dtype)


def pair_sum(keep, received, rows, dtype, places, indices, after=()):
    vmem = [pl.BlockSpec(memory_space=pltpu.VMEM)] * (1 + len(received))
    return pl.pallas_call(
        functools.partial(pair_sum_kernel, len(received), places, indices),
        in_specs=vmem + [pl.BlockSpec(memory_space=pl.ANY)] * len(after),
        out_shape=[jax.ShapeDtypeStruct((rows, keep.shape[1]), dtype)] * len(places),
        compiler_params=params(),
        name="pair_sum",
    )(keep, *received, *after)


def span_sum_kernel(*refs):
    value = refs[0][...]
    for ref in refs[1:-1]:
        value += ref[...].astype(jnp.float32)
    refs[-1][...] = value.astype(refs[-1].dtype)


def span_sum(arrays):
    return pl.pallas_call(
        span_sum_kernel,
        out_shape=jax.ShapeDtypeStruct(arrays[0].shape, jnp.bfloat16),
        compiler_params=params(),
        name="span_sum",
    )(*arrays)


def pack_kernel(own_expert, tokens_hbm, ids_hbm, weights_hbm, sides_ref, *refs):
    packed_refs, (tokens_ref, ids_ref, weights_ref, semaphores) = refs[:EXPERTS], refs[EXPERTS:]
    pairs = [(tokens_hbm, tokens_ref), (ids_hbm, ids_ref), (weights_hbm, weights_ref)]
    copies = [pltpu.make_async_copy(src, dst, semaphores.at[i]) for i, (src, dst) in enumerate(pairs)]
    for copy in copies:
        copy.start()
    for copy in copies:
        copy.wait()
    ids, weights = ids_ref[...], weights_ref[...]
    rows, width = tokens_ref.shape
    tail = width // rows
    square = (rows, rows)
    row, column = lax.broadcasted_iota(jnp.int32, square, 0), lax.broadcasted_iota(jnp.int32, square, 1)
    last = lax.broadcasted_iota(jnp.int32, (rows, tail), 0) == rows - 1
    here = tokens_ref[...].astype(jnp.float32)
    below = pltpu.roll(here, rows - 1, 0)
    for s, packed_ref in enumerate(packed_refs):
        expert = lax.bitwise_xor(own_expert[0], s)
        named = ids == expert
        chosen = jnp.sum(jnp.where(named, weights, 0.0), axis=0, keepdims=True)
        coeff = jnp.sum(jnp.where(row == column, jnp.broadcast_to(chosen, square), 0.0), axis=1, keepdims=True)
        unnamed = 1.0 - jnp.sum(jnp.where(named, 1.0, 0.0), axis=0, keepdims=True)
        shift = jnp.max(jnp.where(column <= row, jnp.broadcast_to(unnamed, square), 0.0), axis=1, keepdims=True)
        sides_ref[:, s * LANES:(s + 1) * LANES] = jnp.broadcast_to(coeff, (rows, LANES))
        sides_ref[:, (EXPERTS + s) * LANES:(EXPERTS + s + 1) * LANES] = jnp.broadcast_to(shift, (rows, LANES))
        kept = jnp.where(shift > 0.5, below, here)
        for i in range(rows - 1):
            moved = jnp.broadcast_to(kept[i:i + 1, width - tail:], (rows, tail))
            piece = jnp.where(last, moved, kept[:, i * tail:(i + 1) * tail])
            packed_ref[:, i * tail:(i + 1) * tail] = piece.astype(jnp.bfloat16)


def pack(own_expert, tokens, ids, weights):
    rows, width = tokens.shape
    packed = jax.ShapeDtypeStruct((rows, width - width // rows), jnp.bfloat16)
    inputs = [tokens, ids.T, weights.T]
    return pl.pallas_call(
        pack_kernel,
        in_specs=[pl.BlockSpec(memory_space=pltpu.SMEM)] + [pl.BlockSpec(memory_space=pl.ANY)] * 3,
        out_shape=[jax.ShapeDtypeStruct((rows, 2 * EXPERTS * LANES), jnp.float32)] + [packed] * EXPERTS,
        scratch_shapes=[pltpu.VMEM(a.shape, a.dtype) for a in inputs] + [pltpu.SemaphoreType.DMA((len(inputs),))],
        compiler_params=params(),
        cost_estimate=cost(EXCHANGE_FLOPS),
        name="pack",
    )(own_expert, *[pltpu.with_memory_space_constraint(a, pltpu.HBM) for a in inputs])


def combine_kernel(base, places, counts, parts, sides_ref, *refs):
    if parts:
        *refs, out_hbm, out_ref, semaphores = refs
    else:
        *refs, out_ref = refs
    rows, width = out_ref.shape
    tail = width // rows
    row = lax.broadcasted_iota(jnp.int32, (rows, tail), 0)
    first, groups = refs[:base], refs[base:]
    terms = []
    for s, count in zip(places, counts):
        group, groups = groups[:count], groups[count:]
        packed = sum([ref[...].astype(jnp.float32) for ref in group[1:]], group[0][...].astype(jnp.float32))
        coeff = sides_ref[:, s * LANES:s * LANES + 1]
        shifted = sides_ref[:, (EXPERTS + s) * LANES:(EXPERTS + s) * LANES + 1] > 0.5
        terms.append((packed, coeff, shifted))
    copies = []
    for i in range(rows):
        columns = slice(i * tail, (i + 1) * tail)
        value = None
        for ref in first:
            value = ref[:, columns]
        for packed, coeff, shifted in terms:
            if i < rows - 1:
                piece = packed[:, columns]
            else:
                piece = jnp.zeros((rows, tail), jnp.float32)
                for j in range(rows - 1):
                    moved = jnp.broadcast_to(packed[rows - 1:, j * tail:(j + 1) * tail], (rows, tail))
                    piece = jnp.where(row == j, moved, piece)
            term = coeff * jnp.where(shifted, pltpu.roll(piece, 1, 0), piece)
            value = term if value is None else value + term
        out_ref[:, columns] = value.astype(out_ref.dtype)
        if parts and (i + 1) % (rows // parts) == 0:
            done = slice((len(copies) * (rows // parts)) * tail, (i + 1) * tail)
            copies.append(pltpu.make_async_copy(out_ref.at[:, done], out_hbm.at[:, done], semaphores.at[len(copies)]))
            copies[-1].start()
    for copy in copies:
        copy.wait()


def combine(sides, base, places, groups, width, dtype, parts=0):
    arrays = [a for group in groups for a in group]
    out_shape = jax.ShapeDtypeStruct((arrays[0].shape[0], width), dtype)
    return pl.pallas_call(
        functools.partial(combine_kernel, len(base), tuple(places), tuple(len(g) for g in groups), parts),
        out_shape=out_shape,
        out_specs=pl.BlockSpec(memory_space=pl.ANY if parts else pltpu.VMEM),
        scratch_shapes=[pltpu.VMEM(out_shape.shape, dtype), pltpu.SemaphoreType.DMA((parts,))] if parts else [],
        compiler_params=params(),
        name="combine",
    )(sides, *base, *arrays)


def local(tokens, expert_ids, route_weights, gate_weight, up_weight, down_weight):
    rows, width = tokens.shape
    attn = lax.axis_size("attn")
    pair = lax.axis_size("ffn")
    span = attn // EXPERTS

    def over_experts(value, other):
        return lax.ppermute(value, "attn", [(i, (i // span ^ other) * span + i % span) for i in range(attn)])

    def over_span(value, shift):
        return lax.ppermute(value, "attn", [(i, i // span * span + (i + shift) % span) for i in range(attn)])

    def over_pair(value, shift):
        return lax.ppermute(value, "ffn", [(i, (i + shift) % pair) for i in range(pair)])

    own_expert = (lax.axis_index("attn") // span).astype(jnp.int32).reshape(1)
    sides, *packed = pack(own_expert, tokens, expert_ids, route_weights)
    column = {s: over_experts(packed[s], s) if s else packed[0] for s in range(EXPERTS)}
    column = [column[s] for s in BLOCK_ORDER]
    parts = [column] + [[over_span(b, t) for b in column] for t in range(1, span)]
    groups = [stack(column)]
    for part in parts[1:]:
        groups += [stack(part[:-1]), stack(part[-1:], (), LAST_FLOPS)]
    *others, last = [over_pair(g, p) for p in range(1, pair) for g in groups]
    first = unpack([b for part in parts for b in part] + others, rows, width)
    hidden = gate_up(first, last, gate_weight, up_weight)

    first = BLOCK_ORDER.index(RETURN_ORDER[0])
    rest = [i for i in range(EXPERTS) if i != first]
    keeps, firsts, others = down(hidden, down_weight, span, pair, rows, first)
    received = [over_pair(b, -p) for p, b in enumerate(firsts, 1)]
    sums, after = {s: [] for s in range(EXPERTS)}, []
    for t in range(1, span):
        after += pair_sum(keeps[t], received, rows, jnp.bfloat16, [first], [t - 1])
        sums[RETURN_ORDER[0]].append(over_span(after[-1], -t))
    received = [over_pair(stack([b], after[:1]), -p) for p, b in enumerate(others, 1)]
    own = pair_sum(keeps[0], received, rows, jnp.float32, range(EXPERTS), [(span - 1) * len(rest) + i for i in range(EXPERTS)])
    for place, block in enumerate(own):
        sums[BLOCK_ORDER[place]].insert(0, block)

    def send_rest(planes, after):
        for t in range(1, span):
            places = [BLOCK_ORDER.index(s) for s in planes]
            indices = [(t - 1) * len(rest) + rest.index(place) for place in places]
            blocks = pair_sum(keeps[t], received, rows, jnp.bfloat16, places, indices, after)
            for s, block in zip(planes, blocks):
                sums[s].append(over_span(block, -t))

    send_rest(RETURN_ORDER[1:], [])
    totals = {s: span_sum(sums[s]) for s in RETURN_ORDER}
    send_rest([0], [totals[RETURN_ORDER[1]]])
    returned = {s: over_experts(totals[s], s) for s in RETURN_ORDER}
    far, *later = RETURN_ORDER
    early = combine(sides, [], [far], [[returned[far]]], width, jnp.float32)
    return combine(sides, [early], later + [0], [[returned[s]] for s in later] + [sums[0]], width, jnp.bfloat16, 2)


def solution(mesh):
    return jax.shard_map(
        local,
        mesh=mesh,
        in_specs=(
            P(("groups", "attn", "ffn"), None),
            P(("groups", "attn", "ffn"), None),
            P(("groups", "attn", "ffn"), None),
            P(None, ("attn", "ffn")),
            P(None, ("attn", "ffn")),
            P(("attn", "ffn"), None),
        ),
        out_specs=P(("groups", "attn", "ffn"), None),
        check_vma=False,
    )
```

```python
import functools

import jax
import jax.numpy as jnp
from jax import lax
from jax.experimental import pallas as pl
from jax.experimental.pallas import tpu as pltpu
from jax.sharding import PartitionSpec as P

EXPERTS = 4
LANES = 128
RETURN_ORDER = (3, 2, 1)
BLOCK_ORDER = (0, 3, 1, 2)
N_BLOCK = 512
LAST_FLOPS = 5_000_000_000
EXCHANGE_FLOPS = 20_000_000_000


def params(rows=0):
    return pltpu.CompilerParams(vmem_limit_bytes=4 * max(1, -(-rows // 128)) * 1024 * 1024)


def cost(flops):
    return pl.CostEstimate(flops=flops, bytes_accessed=0, transcendentals=0)


def block_of(width, most):
    size = most
    while width % size:
        size -= 128
    return size


def in_vmem(value):
    return pltpu.with_memory_space_constraint(value, pltpu.VMEM)


def joined(refs):
    return jnp.concatenate([ref[...].astype(jnp.float32) for ref in refs], axis=0)


def stack_kernel(count, *refs):
    refs[-1][...] = joined(refs[:count]).astype(jnp.bfloat16)


def stack(values, after=(), flops=0):
    rows = sum(v.shape[0] for v in values)
    return pl.pallas_call(
        functools.partial(stack_kernel, len(values)),
        in_specs=[pl.BlockSpec(memory_space=pltpu.VMEM)] * len(values) + [pl.BlockSpec(memory_space=pl.ANY)] * len(after),
        out_shape=jax.ShapeDtypeStruct((rows, values[0].shape[1]), jnp.bfloat16),
        compiler_params=params(),
        cost_estimate=cost(flops),
        name="stack",
    )(*values, *after)


def unpacked(refs, out_ref, rows):
    total, width = out_ref.shape
    tail = width // rows
    blocks = (total // rows, rows, tail)
    row = lax.broadcasted_iota(jnp.int32, blocks, 1)
    ends = jnp.zeros(blocks, jnp.float32)
    for i in range(rows - 1):
        piece = joined([ref.at[:, i * tail:(i + 1) * tail] for ref in refs])
        out_ref[:, i * tail:(i + 1) * tail] = piece.astype(jnp.bfloat16)
        ends = jnp.where(row == i, jnp.broadcast_to(piece.reshape(blocks)[:, rows - 1:, :], blocks), ends)
    out_ref[:, width - tail:] = ends.reshape(total, tail).astype(jnp.bfloat16)


def unpack_kernel(rows, *refs):
    unpacked(refs[:-1], refs[-1], rows)


def unpack(values, rows, width):
    total = sum(v.shape[0] for v in values)
    return pl.pallas_call(
        functools.partial(unpack_kernel, rows),
        out_shape=jax.ShapeDtypeStruct((total, width), jnp.bfloat16),
        compiler_params=params(total),
        cost_estimate=cost(1_000_000_000),
        name="unpack",
    )(*values)


def gate_up_kernel(n_block, first_ref, last_ref, gate_ref, up_ref, hidden_ref, rows_ref):
    rows = last_ref.shape[0]
    total, width = rows_ref.shape
    whole = total - 2 * rows
    rows_ref[:whole, :] = first_ref[:whole, :]
    tail = width // rows
    row = lax.broadcasted_iota(jnp.int32, (rows, tail), 0)
    ends = jnp.zeros((rows, tail), jnp.float32)
    for i in range(rows):
        columns = slice(i * tail, (i + 1) * tail)
        if i < rows - 1:
            piece = last_ref[:, columns].astype(jnp.float32)
            ends = jnp.where(row == i, jnp.broadcast_to(piece[rows - 1:, :], (rows, tail)), ends)
        else:
            piece = ends
        both = jnp.concatenate([first_ref[whole:, columns].astype(jnp.float32), piece], axis=0)
        rows_ref[whole:, columns] = both.astype(jnp.bfloat16)
    for n in range(0, gate_ref.shape[1], n_block):
        columns = slice(n, n + n_block)
        gate = jnp.dot(rows_ref[...], gate_ref[:, columns], preferred_element_type=jnp.float32)
        up = jnp.dot(rows_ref[...], up_ref[:, columns], preferred_element_type=jnp.float32)
        hidden_ref[:, columns] = (gate / (1.0 + jnp.exp(-gate)) * up).astype(jnp.bfloat16)


def gate_up(first, last, gate_weight, up_weight):
    total = first.shape[0] + last.shape[0]
    width, units = gate_weight.shape
    return pl.pallas_call(
        functools.partial(gate_up_kernel, block_of(units, N_BLOCK)),
        in_specs=[pl.BlockSpec(memory_space=pltpu.VMEM)] * 4,
        out_shape=jax.ShapeDtypeStruct((total, units), jnp.bfloat16),
        scratch_shapes=[pltpu.VMEM((total, width), jnp.bfloat16)],
        compiler_params=params(total),
        cost_estimate=cost(4 * total * width * units),
        name="gate_up",
    )(first, last, in_vmem(gate_weight), in_vmem(up_weight))


def down_kernel(rows, sources, hidden_ref, down_ref, *outs):
    width = outs[0].shape[1]
    tail = down_ref.shape[1] // rows
    blocks = (hidden_ref.shape[0] // rows, rows, tail)
    last = lax.broadcasted_iota(jnp.int32, blocks, 1) == rows - 1
    hidden = hidden_ref[...]
    ends = None
    for i in [rows - 2] + list(range(0, rows - 2, 2)):
        both = jnp.dot(hidden, down_ref[:, i * tail:(i + 2) * tail], preferred_element_type=jnp.float32)
        pieces = {i: both[:, :tail].reshape(blocks), i + 1: both[:, tail:].reshape(blocks)}
        if ends is None:
            ends = pieces.pop(i + 1)
        for j, value in pieces.items():
            value = jnp.where(last, jnp.broadcast_to(ends[:, j:j + 1, :], blocks), value).reshape(blocks[0] * rows, tail)
            for ref, starts in zip(outs, sources):
                taken = [value[start:start + rows] for start in starts]
                taken = jnp.concatenate(taken, axis=0) if len(taken) > 1 else taken[0]
                ref[:, j * tail:(j + 1) * tail] = taken.astype(ref.dtype)


def down(hidden, down_weight, span, pair, rows, first):
    total, units = hidden.shape
    width = down_weight.shape[1] // rows * (rows - 1)
    part = total // (span * pair)
    places = [first] + [i for i in range(part // rows) if i != first]

    def starts(p, t, chosen):
        return [(p * span + t) * part + i * rows for i in chosen]

    sources = [starts(0, t, range(part // rows)) for t in range(span)]
    for p in range(1, pair):
        sources.append([x for t in range(1, span) for x in starts(p, t, places[:1])])
        sources.append([x for t in range(1, span) for x in starts(p, t, places[1:])] + starts(p, 0, range(part // rows)))
    outs = pl.pallas_call(
        functools.partial(down_kernel, rows, sources),
        in_specs=[pl.BlockSpec(memory_space=pltpu.VMEM)] * 2,
        out_shape=[jax.ShapeDtypeStruct((rows * len(x), width), jnp.float32 if i < span else jnp.bfloat16) for i, x in enumerate(sources)],
        compiler_params=params(total),
        cost_estimate=cost(2 * total * width * units),
        name="down",
    )(hidden, in_vmem(down_weight))
    return outs[:span], outs[span::2], outs[span + 1::2]


def pair_sum_kernel(count, places, indices, keep_ref, *refs):
    received, outs = refs[:count], refs[-len(places):]
    rows = outs[0].shape[0]
    for place, i, out_ref in zip(places, indices, outs):
        value = keep_ref[place * rows:(place + 1) * rows, :]
        for ref in received:
            value += ref[i * rows:(i + 1) * rows, :].astype(jnp.float32)
        out_ref[...] = value.astype(out_ref.dtype)


def pair_sum(keep, received, rows, dtype, places, indices, after=()):
    vmem = [pl.BlockSpec(memory_space=pltpu.VMEM)] * (1 + len(received))
    return pl.pallas_call(
        functools.partial(pair_sum_kernel, len(received), places, indices),
        in_specs=vmem + [pl.BlockSpec(memory_space=pl.ANY)] * len(after),
        out_shape=[jax.ShapeDtypeStruct((rows, keep.shape[1]), dtype)] * len(places),
        compiler_params=params(),
        name="pair_sum",
    )(keep, *received, *after)


def span_sum_kernel(*refs):
    value = refs[0][...]
    for ref in refs[1:-1]:
        value += ref[...].astype(jnp.float32)
    refs[-1][...] = value.astype(refs[-1].dtype)


def span_sum(arrays):
    return pl.pallas_call(
        span_sum_kernel,
        out_shape=jax.ShapeDtypeStruct(arrays[0].shape, jnp.bfloat16),
        compiler_params=params(),
        name="span_sum",
    )(*arrays)


def load_kernel(count, *refs):
    semaphores = refs[-1]
    copies = [pltpu.make_async_copy(refs[i], refs[count + i], semaphores.at[i]) for i in range(count)]
    for copy in copies:
        copy.start()
    for copy in copies:
        copy.wait()


def load(arrays):
    return pl.pallas_call(
        functools.partial(load_kernel, len(arrays)),
        in_specs=[pl.BlockSpec(memory_space=pl.ANY)] * len(arrays),
        out_specs=[pl.BlockSpec(memory_space=pltpu.VMEM)] * len(arrays),
        out_shape=[jax.ShapeDtypeStruct(a.shape, a.dtype) for a in arrays],
        scratch_shapes=[pltpu.SemaphoreType.DMA((len(arrays),))],
        compiler_params=params(),
        cost_estimate=cost(0),
        name="load",
    )(*[pltpu.with_memory_space_constraint(a, pltpu.HBM) for a in arrays])


def pack_kernel(own_expert, tokens_ref, ids_ref, weights_ref, sides_ref, *packed_refs):
    ids, weights = ids_ref[...], weights_ref[...]
    rows, width = tokens_ref.shape
    tail = width // rows
    square = (rows, rows)
    row, column = lax.broadcasted_iota(jnp.int32, square, 0), lax.broadcasted_iota(jnp.int32, square, 1)
    last = lax.broadcasted_iota(jnp.int32, (rows, tail), 0) == rows - 1
    here = tokens_ref[...].astype(jnp.float32)
    below = pltpu.roll(here, rows - 1, 0)
    for s, packed_ref in enumerate(packed_refs):
        expert = lax.bitwise_xor(own_expert[0], s)
        named = ids == expert
        chosen = jnp.sum(jnp.where(named, weights, 0.0), axis=0, keepdims=True)
        coeff = jnp.sum(jnp.where(row == column, jnp.broadcast_to(chosen, square), 0.0), axis=1, keepdims=True)
        unnamed = 1.0 - jnp.sum(jnp.where(named, 1.0, 0.0), axis=0, keepdims=True)
        shift = jnp.max(jnp.where(column <= row, jnp.broadcast_to(unnamed, square), 0.0), axis=1, keepdims=True)
        sides_ref[:, s * LANES:(s + 1) * LANES] = jnp.broadcast_to(coeff, (rows, LANES))
        sides_ref[:, (EXPERTS + s) * LANES:(EXPERTS + s + 1) * LANES] = jnp.broadcast_to(shift, (rows, LANES))
        kept = jnp.where(shift > 0.5, below, here)
        for i in range(rows - 1):
            moved = jnp.broadcast_to(kept[i:i + 1, width - tail:], (rows, tail))
            piece = jnp.where(last, moved, kept[:, i * tail:(i + 1) * tail])
            packed_ref[:, i * tail:(i + 1) * tail] = piece.astype(jnp.bfloat16)


def pack(own_expert, tokens, ids, weights):
    rows, width = tokens.shape
    packed = jax.ShapeDtypeStruct((rows, width - width // rows), jnp.bfloat16)
    return pl.pallas_call(
        pack_kernel,
        in_specs=[pl.BlockSpec(memory_space=pltpu.SMEM)] + [pl.BlockSpec(memory_space=pltpu.VMEM)] * 3,
        out_shape=[jax.ShapeDtypeStruct((rows, 2 * EXPERTS * LANES), jnp.float32)] + [packed] * EXPERTS,
        compiler_params=params(),
        cost_estimate=cost(EXCHANGE_FLOPS),
        name="pack",
    )(own_expert, *load([tokens, ids.T, weights.T]))


def combine_kernel(base, places, counts, parts, sides_ref, *refs):
    if parts:
        *refs, out_hbm, out_ref, semaphores = refs
    else:
        *refs, out_ref = refs
    rows, width = out_ref.shape
    tail = width // rows
    row = lax.broadcasted_iota(jnp.int32, (rows, tail), 0)
    first, groups = refs[:base], refs[base:]
    terms = []
    for s, count in zip(places, counts):
        group, groups = groups[:count], groups[count:]
        packed = sum([ref[...].astype(jnp.float32) for ref in group[1:]], group[0][...].astype(jnp.float32))
        coeff = sides_ref[:, s * LANES:s * LANES + 1]
        shifted = sides_ref[:, (EXPERTS + s) * LANES:(EXPERTS + s) * LANES + 1] > 0.5
        terms.append((packed, coeff, shifted))
    copies = []
    for i in range(rows):
        columns = slice(i * tail, (i + 1) * tail)
        value = None
        for ref in first:
            value = ref[:, columns]
        for packed, coeff, shifted in terms:
            if i < rows - 1:
                piece = packed[:, columns]
            else:
                piece = jnp.zeros((rows, tail), jnp.float32)
                for j in range(rows - 1):
                    moved = jnp.broadcast_to(packed[rows - 1:, j * tail:(j + 1) * tail], (rows, tail))
                    piece = jnp.where(row == j, moved, piece)
            term = coeff * jnp.where(shifted, pltpu.roll(piece, 1, 0), piece)
            value = term if value is None else value + term
        out_ref[:, columns] = value.astype(out_ref.dtype)
        if parts and (i + 1) % (rows // parts) == 0:
            done = slice((len(copies) * (rows // parts)) * tail, (i + 1) * tail)
            copies.append(pltpu.make_async_copy(out_ref.at[:, done], out_hbm.at[:, done], semaphores.at[len(copies)]))
            copies[-1].start()
    for copy in copies:
        copy.wait()


def combine(sides, base, places, groups, width, dtype, parts=0):
    arrays = [a for group in groups for a in group]
    out_shape = jax.ShapeDtypeStruct((arrays[0].shape[0], width), dtype)
    return pl.pallas_call(
        functools.partial(combine_kernel, len(base), tuple(places), tuple(len(g) for g in groups), parts),
        out_shape=out_shape,
        out_specs=pl.BlockSpec(memory_space=pl.ANY if parts else pltpu.VMEM),
        scratch_shapes=[pltpu.VMEM(out_shape.shape, dtype), pltpu.SemaphoreType.DMA((parts,))] if parts else [],
        compiler_params=params(),
        name="combine",
    )(sides, *base, *arrays)


def local(tokens, expert_ids, route_weights, gate_weight, up_weight, down_weight):
    rows, width = tokens.shape
    attn = lax.axis_size("attn")
    pair = lax.axis_size("ffn")
    span = attn // EXPERTS

    def over_experts(value, other):
        return lax.ppermute(value, "attn", [(i, (i // span ^ other) * span + i % span) for i in range(attn)])

    def over_span(value, shift):
        return lax.ppermute(value, "attn", [(i, i // span * span + (i + shift) % span) for i in range(attn)])

    def over_pair(value, shift):
        return lax.ppermute(value, "ffn", [(i, (i + shift) % pair) for i in range(pair)])

    own_expert = (lax.axis_index("attn") // span).astype(jnp.int32).reshape(1)
    sides, *packed = pack(own_expert, tokens, expert_ids, route_weights)
    column = {s: over_experts(packed[s], s) if s else packed[0] for s in range(EXPERTS)}
    column = [column[s] for s in BLOCK_ORDER]
    parts = [column] + [[over_span(b, t) for b in column] for t in range(1, span)]
    groups = [stack(column)]
    for part in parts[1:]:
        groups += [stack(part[:-1]), stack(part[-1:], (), LAST_FLOPS)]
    *others, last = [over_pair(g, p) for p in range(1, pair) for g in groups]
    first = unpack([b for part in parts for b in part] + others, rows, width)
    hidden = gate_up(first, last, gate_weight, up_weight)

    first = BLOCK_ORDER.index(RETURN_ORDER[0])
    rest = [i for i in range(EXPERTS) if i != first]
    keeps, firsts, others = down(hidden, down_weight, span, pair, rows, first)
    received = [over_pair(b, -p) for p, b in enumerate(firsts, 1)]
    sums, after = {s: [] for s in range(EXPERTS)}, []
    for t in range(1, span):
        after += pair_sum(keeps[t], received, rows, jnp.bfloat16, [first], [t - 1])
        sums[RETURN_ORDER[0]].append(over_span(after[-1], -t))
    received = [over_pair(stack([b], after[:1]), -p) for p, b in enumerate(others, 1)]
    own = pair_sum(keeps[0], received, rows, jnp.float32, range(EXPERTS), [(span - 1) * len(rest) + i for i in range(EXPERTS)])
    for place, block in enumerate(own):
        sums[BLOCK_ORDER[place]].insert(0, block)

    def send_rest(planes, after):
        for t in range(1, span):
            places = [BLOCK_ORDER.index(s) for s in planes]
            indices = [(t - 1) * len(rest) + rest.index(place) for place in places]
            blocks = pair_sum(keeps[t], received, rows, jnp.bfloat16, places, indices, after)
            for s, block in zip(planes, blocks):
                sums[s].append(over_span(block, -t))

    send_rest(RETURN_ORDER[1:], [])
    totals = {s: span_sum(sums[s]) for s in RETURN_ORDER}
    send_rest([0], [totals[RETURN_ORDER[1]]])
    returned = {s: over_experts(totals[s], s) for s in RETURN_ORDER}
    far, *later = RETURN_ORDER
    early = combine(sides, [], [far], [[returned[far]]], width, jnp.float32)
    return combine(sides, [early], later + [0], [[returned[s]] for s in later] + [sums[0]], width, jnp.bfloat16, 2)


def solution(mesh):
    return jax.shard_map(
        local,
        mesh=mesh,
        in_specs=(
            P(("groups", "attn", "ffn"), None),
            P(("groups", "attn", "ffn"), None),
            P(("groups", "attn", "ffn"), None),
            P(None, ("attn", "ffn")),
            P(None, ("attn", "ffn")),
            P(("attn", "ffn"), None),
        ),
        out_specs=P(("groups", "attn", "ffn"), None),
        check_vma=False,
    )
```

```python
import functools

import jax
import jax.numpy as jnp
from jax import lax
from jax.experimental import pallas as pl
from jax.experimental.pallas import tpu as pltpu
from jax.sharding import PartitionSpec as P

EXPERTS = 4
LANES = 128
RETURN_ORDER = (3, 2, 1)
BLOCK_ORDER = (0, 3, 2, 1)
N_BLOCK = 512
LAST_FLOPS = 5_000_000_000
EXCHANGE_FLOPS = 20_000_000_000


def params(rows=0):
    return pltpu.CompilerParams(vmem_limit_bytes=4 * max(1, -(-rows // 128)) * 1024 * 1024)


def cost(flops):
    return pl.CostEstimate(flops=flops, bytes_accessed=0, transcendentals=0)


def block_of(width, most):
    size = most
    while width % size:
        size -= 128
    return size


def in_vmem(value):
    return pltpu.with_memory_space_constraint(value, pltpu.VMEM)


def joined(refs):
    return jnp.concatenate([ref[...].astype(jnp.float32) for ref in refs], axis=0)


def stack_kernel(count, *refs):
    refs[-1][...] = joined(refs[:count]).astype(jnp.bfloat16)


def stack(values, after=(), flops=0):
    rows = sum(v.shape[0] for v in values)
    return pl.pallas_call(
        functools.partial(stack_kernel, len(values)),
        in_specs=[pl.BlockSpec(memory_space=pltpu.VMEM)] * len(values) + [pl.BlockSpec(memory_space=pl.ANY)] * len(after),
        out_shape=jax.ShapeDtypeStruct((rows, values[0].shape[1]), jnp.bfloat16),
        compiler_params=params(),
        cost_estimate=cost(flops),
        name="stack",
    )(*values, *after)


def unpacked(refs, out_ref, rows):
    total, width = out_ref.shape
    tail = width // rows
    blocks = (total // rows, rows, tail)
    row = lax.broadcasted_iota(jnp.int32, blocks, 1)
    ends = jnp.zeros(blocks, jnp.float32)
    for i in range(rows - 1):
        piece = joined([ref.at[:, i * tail:(i + 1) * tail] for ref in refs])
        out_ref[:, i * tail:(i + 1) * tail] = piece.astype(jnp.bfloat16)
        ends = jnp.where(row == i, jnp.broadcast_to(piece.reshape(blocks)[:, rows - 1:, :], blocks), ends)
    out_ref[:, width - tail:] = ends.reshape(total, tail).astype(jnp.bfloat16)


def unpack_kernel(rows, *refs):
    unpacked(refs[:-1], refs[-1], rows)


def unpack(values, rows, width):
    total = sum(v.shape[0] for v in values)
    return pl.pallas_call(
        functools.partial(unpack_kernel, rows),
        out_shape=jax.ShapeDtypeStruct((total, width), jnp.bfloat16),
        compiler_params=params(total),
        cost_estimate=cost(1_000_000_000),
        name="unpack",
    )(*values)


def gate_up_kernel(n_block, first_ref, last_ref, gate_ref, up_ref, hidden_ref, rows_ref):
    rows = last_ref.shape[0]
    total, width = rows_ref.shape
    whole = total - 2 * rows
    rows_ref[:whole, :] = first_ref[:whole, :]
    tail = width // rows
    row = lax.broadcasted_iota(jnp.int32, (rows, tail), 0)
    ends = jnp.zeros((rows, tail), jnp.float32)
    for i in range(rows):
        columns = slice(i * tail, (i + 1) * tail)
        if i < rows - 1:
            piece = last_ref[:, columns].astype(jnp.float32)
            ends = jnp.where(row == i, jnp.broadcast_to(piece[rows - 1:, :], (rows, tail)), ends)
        else:
            piece = ends
        both = jnp.concatenate([first_ref[whole:, columns].astype(jnp.float32), piece], axis=0)
        rows_ref[whole:, columns] = both.astype(jnp.bfloat16)
    for n in range(0, gate_ref.shape[1], n_block):
        columns = slice(n, n + n_block)
        gate = jnp.dot(rows_ref[...], gate_ref[:, columns], preferred_element_type=jnp.float32)
        up = jnp.dot(rows_ref[...], up_ref[:, columns], preferred_element_type=jnp.float32)
        hidden_ref[:, columns] = (gate / (1.0 + jnp.exp(-gate)) * up).astype(jnp.bfloat16)


def gate_up(first, last, gate_weight, up_weight):
    total = first.shape[0] + last.shape[0]
    width, units = gate_weight.shape
    return pl.pallas_call(
        functools.partial(gate_up_kernel, block_of(units, N_BLOCK)),
        in_specs=[pl.BlockSpec(memory_space=pltpu.VMEM)] * 4,
        out_shape=jax.ShapeDtypeStruct((total, units), jnp.bfloat16),
        scratch_shapes=[pltpu.VMEM((total, width), jnp.bfloat16)],
        compiler_params=params(total),
        cost_estimate=cost(4 * total * width * units),
        name="gate_up",
    )(first, last, in_vmem(gate_weight), in_vmem(up_weight))


def down_kernel(rows, sources, hidden_ref, down_ref, *outs):
    width = outs[0].shape[1]
    tail = down_ref.shape[1] // rows
    blocks = (hidden_ref.shape[0] // rows, rows, tail)
    last = lax.broadcasted_iota(jnp.int32, blocks, 1) == rows - 1
    hidden = hidden_ref[...]
    ends = None
    for i in [rows - 2] + list(range(0, rows - 2, 2)):
        both = jnp.dot(hidden, down_ref[:, i * tail:(i + 2) * tail], preferred_element_type=jnp.float32)
        pieces = {i: both[:, :tail].reshape(blocks), i + 1: both[:, tail:].reshape(blocks)}
        if ends is None:
            ends = pieces.pop(i + 1)
        for j, value in pieces.items():
            value = jnp.where(last, jnp.broadcast_to(ends[:, j:j + 1, :], blocks), value).reshape(blocks[0] * rows, tail)
            for ref, starts in zip(outs, sources):
                taken = [value[start:start + rows] for start in starts]
                taken = jnp.concatenate(taken, axis=0) if len(taken) > 1 else taken[0]
                ref[:, j * tail:(j + 1) * tail] = taken.astype(ref.dtype)


def down(hidden, down_weight, span, pair, rows, first):
    total, units = hidden.shape
    width = down_weight.shape[1] // rows * (rows - 1)
    part = total // (span * pair)
    places = [first] + [i for i in range(part // rows) if i != first]

    def starts(p, t, chosen):
        return [(p * span + t) * part + i * rows for i in chosen]

    sources = [starts(0, t, range(part // rows)) for t in range(span)]
    for p in range(1, pair):
        sources.append([x for t in range(1, span) for x in starts(p, t, places[:1])])
        sources.append([x for t in range(1, span) for x in starts(p, t, places[1:])] + starts(p, 0, range(part // rows)))
    outs = pl.pallas_call(
        functools.partial(down_kernel, rows, sources),
        in_specs=[pl.BlockSpec(memory_space=pltpu.VMEM)] * 2,
        out_shape=[jax.ShapeDtypeStruct((rows * len(x), width), jnp.float32 if i < span else jnp.bfloat16) for i, x in enumerate(sources)],
        compiler_params=params(total),
        cost_estimate=cost(2 * total * width * units),
        name="down",
    )(hidden, in_vmem(down_weight))
    return outs[:span], outs[span::2], outs[span + 1::2]


def pair_sum_kernel(count, places, indices, keep_ref, *refs):
    received, outs = refs[:count], refs[-len(places):]
    rows = outs[0].shape[0]
    for place, i, out_ref in zip(places, indices, outs):
        value = keep_ref[place * rows:(place + 1) * rows, :]
        for ref in received:
            value += ref[i * rows:(i + 1) * rows, :].astype(jnp.float32)
        out_ref[...] = value.astype(out_ref.dtype)


def pair_sum(keep, received, rows, dtype, places, indices, after=()):
    vmem = [pl.BlockSpec(memory_space=pltpu.VMEM)] * (1 + len(received))
    return pl.pallas_call(
        functools.partial(pair_sum_kernel, len(received), places, indices),
        in_specs=vmem + [pl.BlockSpec(memory_space=pl.ANY)] * len(after),
        out_shape=[jax.ShapeDtypeStruct((rows, keep.shape[1]), dtype)] * len(places),
        compiler_params=params(),
        name="pair_sum",
    )(keep, *received, *after)


def span_sum_kernel(*refs):
    value = refs[0][...]
    for ref in refs[1:-1]:
        value += ref[...].astype(jnp.float32)
    refs[-1][...] = value.astype(refs[-1].dtype)


def span_sum(arrays):
    return pl.pallas_call(
        span_sum_kernel,
        out_shape=jax.ShapeDtypeStruct(arrays[0].shape, jnp.bfloat16),
        compiler_params=params(),
        name="span_sum",
    )(*arrays)


def load_kernel(count, *refs):
    semaphores = refs[-1]
    copies = [pltpu.make_async_copy(refs[i], refs[count + i], semaphores.at[i]) for i in range(count)]
    for copy in copies:
        copy.start()
    for copy in copies:
        copy.wait()


def load(arrays):
    return pl.pallas_call(
        functools.partial(load_kernel, len(arrays)),
        in_specs=[pl.BlockSpec(memory_space=pl.ANY)] * len(arrays),
        out_specs=[pl.BlockSpec(memory_space=pltpu.VMEM)] * len(arrays),
        out_shape=[jax.ShapeDtypeStruct(a.shape, a.dtype) for a in arrays],
        scratch_shapes=[pltpu.SemaphoreType.DMA((len(arrays),))],
        compiler_params=params(),
        cost_estimate=cost(0),
        name="load",
    )(*[pltpu.with_memory_space_constraint(a, pltpu.HBM) for a in arrays])


def pack_kernel(own_expert, tokens_ref, ids_ref, weights_ref, sides_ref, *packed_refs):
    ids, weights = ids_ref[...], weights_ref[...]
    rows, width = tokens_ref.shape
    tail = width // rows
    square = (rows, rows)
    row, column = lax.broadcasted_iota(jnp.int32, square, 0), lax.broadcasted_iota(jnp.int32, square, 1)
    last = lax.broadcasted_iota(jnp.int32, (rows, tail), 0) == rows - 1
    here = tokens_ref[...].astype(jnp.float32)
    below = pltpu.roll(here, rows - 1, 0)
    for s, packed_ref in enumerate(packed_refs):
        expert = lax.bitwise_xor(own_expert[0], s)
        named = ids == expert
        chosen = jnp.sum(jnp.where(named, weights, 0.0), axis=0, keepdims=True)
        coeff = jnp.sum(jnp.where(row == column, jnp.broadcast_to(chosen, square), 0.0), axis=1, keepdims=True)
        unnamed = 1.0 - jnp.sum(jnp.where(named, 1.0, 0.0), axis=0, keepdims=True)
        shift = jnp.max(jnp.where(column <= row, jnp.broadcast_to(unnamed, square), 0.0), axis=1, keepdims=True)
        sides_ref[:, s * LANES:(s + 1) * LANES] = jnp.broadcast_to(coeff, (rows, LANES))
        sides_ref[:, (EXPERTS + s) * LANES:(EXPERTS + s + 1) * LANES] = jnp.broadcast_to(shift, (rows, LANES))
        kept = jnp.where(shift > 0.5, below, here)
        for i in range(rows - 1):
            moved = jnp.broadcast_to(kept[i:i + 1, width - tail:], (rows, tail))
            piece = jnp.where(last, moved, kept[:, i * tail:(i + 1) * tail])
            packed_ref[:, i * tail:(i + 1) * tail] = piece.astype(jnp.bfloat16)


def pack(own_expert, tokens, ids, weights):
    rows, width = tokens.shape
    packed = jax.ShapeDtypeStruct((rows, width - width // rows), jnp.bfloat16)
    return pl.pallas_call(
        pack_kernel,
        in_specs=[pl.BlockSpec(memory_space=pltpu.SMEM)] + [pl.BlockSpec(memory_space=pltpu.VMEM)] * 3,
        out_shape=[jax.ShapeDtypeStruct((rows, 2 * EXPERTS * LANES), jnp.float32)] + [packed] * EXPERTS,
        compiler_params=params(),
        cost_estimate=cost(EXCHANGE_FLOPS),
        name="pack",
    )(own_expert, *load([tokens, ids.T, weights.T]))


def combine_kernel(base, places, counts, parts, sides_ref, *refs):
    if parts:
        *refs, out_hbm, out_ref, semaphores = refs
    else:
        *refs, out_ref = refs
    rows, width = out_ref.shape
    tail = width // rows
    row = lax.broadcasted_iota(jnp.int32, (rows, tail), 0)
    first, groups = refs[:base], refs[base:]
    terms = []
    for s, count in zip(places, counts):
        group, groups = groups[:count], groups[count:]
        packed = sum([ref[...].astype(jnp.float32) for ref in group[1:]], group[0][...].astype(jnp.float32))
        coeff = sides_ref[:, s * LANES:s * LANES + 1]
        shifted = sides_ref[:, (EXPERTS + s) * LANES:(EXPERTS + s) * LANES + 1] > 0.5
        terms.append((packed, coeff, shifted))
    copies = []
    for i in range(rows):
        columns = slice(i * tail, (i + 1) * tail)
        value = None
        for ref in first:
            value = ref[:, columns]
        for packed, coeff, shifted in terms:
            if i < rows - 1:
                piece = packed[:, columns]
            else:
                piece = jnp.zeros((rows, tail), jnp.float32)
                for j in range(rows - 1):
                    moved = jnp.broadcast_to(packed[rows - 1:, j * tail:(j + 1) * tail], (rows, tail))
                    piece = jnp.where(row == j, moved, piece)
            term = coeff * jnp.where(shifted, pltpu.roll(piece, 1, 0), piece)
            value = term if value is None else value + term
        out_ref[:, columns] = value.astype(out_ref.dtype)
        if parts and (i + 1) % (rows // parts) == 0:
            done = slice((len(copies) * (rows // parts)) * tail, (i + 1) * tail)
            copies.append(pltpu.make_async_copy(out_ref.at[:, done], out_hbm.at[:, done], semaphores.at[len(copies)]))
            copies[-1].start()
    for copy in copies:
        copy.wait()


def combine(sides, base, places, groups, width, dtype, parts=0):
    arrays = [a for group in groups for a in group]
    out_shape = jax.ShapeDtypeStruct((arrays[0].shape[0], width), dtype)
    return pl.pallas_call(
        functools.partial(combine_kernel, len(base), tuple(places), tuple(len(g) for g in groups), parts),
        out_shape=out_shape,
        out_specs=pl.BlockSpec(memory_space=pl.ANY if parts else pltpu.VMEM),
        scratch_shapes=[pltpu.VMEM(out_shape.shape, dtype), pltpu.SemaphoreType.DMA((parts,))] if parts else [],
        compiler_params=params(),
        name="combine",
    )(sides, *base, *arrays)


def local(tokens, expert_ids, route_weights, gate_weight, up_weight, down_weight):
    rows, width = tokens.shape
    attn = lax.axis_size("attn")
    pair = lax.axis_size("ffn")
    span = attn // EXPERTS

    def over_experts(value, other):
        return lax.ppermute(value, "attn", [(i, (i // span ^ other) * span + i % span) for i in range(attn)])

    def over_span(value, shift):
        return lax.ppermute(value, "attn", [(i, i // span * span + (i + shift) % span) for i in range(attn)])

    def over_pair(value, shift):
        return lax.ppermute(value, "ffn", [(i, (i + shift) % pair) for i in range(pair)])

    own_expert = (lax.axis_index("attn") // span).astype(jnp.int32).reshape(1)
    sides, *packed = pack(own_expert, tokens, expert_ids, route_weights)
    column = {s: over_experts(packed[s], s) if s else packed[0] for s in range(EXPERTS)}
    column = [column[s] for s in BLOCK_ORDER]
    parts = [column] + [[over_span(b, t) for b in column] for t in range(1, span)]
    groups = [stack(column)]
    for part in parts[1:]:
        groups += [stack(part[:-1]), stack(part[-1:], (), LAST_FLOPS)]
    *others, last = [over_pair(g, p) for p in range(1, pair) for g in groups]
    first = unpack([b for part in parts for b in part] + others, rows, width)
    hidden = gate_up(first, last, gate_weight, up_weight)

    first = BLOCK_ORDER.index(RETURN_ORDER[0])
    rest = [i for i in range(EXPERTS) if i != first]
    keeps, firsts, others = down(hidden, down_weight, span, pair, rows, first)
    received = [over_pair(b, -p) for p, b in enumerate(firsts, 1)]
    sums, after = {s: [] for s in range(EXPERTS)}, []
    for t in range(1, span):
        after += pair_sum(keeps[t], received, rows, jnp.bfloat16, [first], [t - 1])
        sums[RETURN_ORDER[0]].append(over_span(after[-1], -t))
    received = [over_pair(stack([b], after[:1]), -p) for p, b in enumerate(others, 1)]
    own = pair_sum(keeps[0], received, rows, jnp.float32, range(EXPERTS), [(span - 1) * len(rest) + i for i in range(EXPERTS)])
    for place, block in enumerate(own):
        sums[BLOCK_ORDER[place]].insert(0, block)

    def send_rest(planes, after):
        for t in range(1, span):
            places = [BLOCK_ORDER.index(s) for s in planes]
            indices = [(t - 1) * len(rest) + rest.index(place) for place in places]
            blocks = pair_sum(keeps[t], received, rows, jnp.bfloat16, places, indices, after)
            for s, block in zip(planes, blocks):
                sums[s].append(over_span(block, -t))

    send_rest(RETURN_ORDER[1:], [])
    totals = {s: span_sum(sums[s]) for s in RETURN_ORDER}
    send_rest([0], [totals[RETURN_ORDER[1]]])
    returned = {s: over_experts(totals[s], s) for s in RETURN_ORDER}
    far, *later = RETURN_ORDER
    early = combine(sides, [], [far], [[returned[far]]], width, jnp.float32)
    return combine(sides, [early], later + [0], [[returned[s]] for s in later] + [sums[0]], width, jnp.bfloat16, 2)


def solution(mesh):
    return jax.shard_map(
        local,
        mesh=mesh,
        in_specs=(
            P(("groups", "attn", "ffn"), None),
            P(("groups", "attn", "ffn"), None),
            P(("groups", "attn", "ffn"), None),
            P(None, ("attn", "ffn")),
            P(None, ("attn", "ffn")),
            P(("attn", "ffn"), None),
        ),
        out_specs=P(("groups", "attn", "ffn"), None),
        check_vma=False,
    )
```

```python
import functools

import jax
import jax.numpy as jnp
from jax import lax
from jax.experimental import pallas as pl
from jax.experimental.pallas import tpu as pltpu
from jax.sharding import PartitionSpec as P

EXPERTS = 4
LANES = 128
RETURN_ORDER = (3, 2, 1)
BLOCK_ORDER = (0, 3, 1, 2)
N_BLOCK = 512
LAST_FLOPS = 5_000_000_000
EXCHANGE_FLOPS = 20_000_000_000


def params(rows=0):
    return pltpu.CompilerParams(vmem_limit_bytes=4 * max(1, -(-rows // 128)) * 1024 * 1024)


def cost(flops):
    return pl.CostEstimate(flops=flops, bytes_accessed=0, transcendentals=0)


def block_of(width, most):
    size = most
    while width % size:
        size -= 128
    return size


def in_vmem(value):
    return pltpu.with_memory_space_constraint(value, pltpu.VMEM)


def joined(refs):
    return jnp.concatenate([ref[...].astype(jnp.float32) for ref in refs], axis=0)


def stack_kernel(count, *refs):
    refs[-1][...] = joined(refs[:count]).astype(jnp.bfloat16)


def stack(values, after=(), flops=0):
    rows = sum(v.shape[0] for v in values)
    return pl.pallas_call(
        functools.partial(stack_kernel, len(values)),
        in_specs=[pl.BlockSpec(memory_space=pltpu.VMEM)] * len(values) + [pl.BlockSpec(memory_space=pl.ANY)] * len(after),
        out_shape=jax.ShapeDtypeStruct((rows, values[0].shape[1]), jnp.bfloat16),
        compiler_params=params(),
        cost_estimate=cost(flops),
        name="stack",
    )(*values, *after)


def unpacked(refs, out_ref, rows):
    total, width = out_ref.shape
    tail = width // rows
    blocks = (total // rows, rows, tail)
    row = lax.broadcasted_iota(jnp.int32, blocks, 1)
    ends = jnp.zeros(blocks, jnp.float32)
    for i in range(rows - 1):
        piece = joined([ref.at[:, i * tail:(i + 1) * tail] for ref in refs])
        out_ref[:, i * tail:(i + 1) * tail] = piece.astype(jnp.bfloat16)
        ends = jnp.where(row == i, jnp.broadcast_to(piece.reshape(blocks)[:, rows - 1:, :], blocks), ends)
    out_ref[:, width - tail:] = ends.reshape(total, tail).astype(jnp.bfloat16)


def unpack_kernel(rows, *refs):
    unpacked(refs[:-1], refs[-1], rows)


def unpack(values, rows, width):
    total = sum(v.shape[0] for v in values)
    return pl.pallas_call(
        functools.partial(unpack_kernel, rows),
        out_shape=jax.ShapeDtypeStruct((total, width), jnp.bfloat16),
        compiler_params=params(total),
        cost_estimate=cost(1_000_000_000),
        name="unpack",
    )(*values)


def gate_up_kernel(n_block, first_ref, last_ref, gate_ref, up_ref, hidden_ref, rows_ref):
    rows = last_ref.shape[0]
    total, width = rows_ref.shape
    whole = total - 2 * rows
    rows_ref[:whole, :] = first_ref[:whole, :]
    tail = width // rows
    row = lax.broadcasted_iota(jnp.int32, (rows, tail), 0)
    ends = jnp.zeros((rows, tail), jnp.float32)
    for i in range(rows):
        columns = slice(i * tail, (i + 1) * tail)
        if i < rows - 1:
            piece = last_ref[:, columns].astype(jnp.float32)
            ends = jnp.where(row == i, jnp.broadcast_to(piece[rows - 1:, :], (rows, tail)), ends)
        else:
            piece = ends
        both = jnp.concatenate([first_ref[whole:, columns].astype(jnp.float32), piece], axis=0)
        rows_ref[whole:, columns] = both.astype(jnp.bfloat16)
    for n in range(0, gate_ref.shape[1], n_block):
        columns = slice(n, n + n_block)
        gate = jnp.dot(rows_ref[...], gate_ref[:, columns], preferred_element_type=jnp.float32)
        up = jnp.dot(rows_ref[...], up_ref[:, columns], preferred_element_type=jnp.float32)
        hidden_ref[:, columns] = (gate / (1.0 + jnp.exp(-gate)) * up).astype(jnp.bfloat16)


def gate_up(first, last, gate_weight, up_weight):
    total = first.shape[0] + last.shape[0]
    width, units = gate_weight.shape
    return pl.pallas_call(
        functools.partial(gate_up_kernel, block_of(units, N_BLOCK)),
        in_specs=[pl.BlockSpec(memory_space=pltpu.VMEM)] * 4,
        out_shape=jax.ShapeDtypeStruct((total, units), jnp.bfloat16),
        scratch_shapes=[pltpu.VMEM((total, width), jnp.bfloat16)],
        compiler_params=params(total),
        cost_estimate=cost(4 * total * width * units),
        name="gate_up",
    )(first, last, in_vmem(gate_weight), in_vmem(up_weight))


def down_kernel(rows, sources, hidden_ref, down_ref, *outs):
    width = outs[0].shape[1]
    tail = down_ref.shape[1] // rows
    blocks = (hidden_ref.shape[0] // rows, rows, tail)
    last = lax.broadcasted_iota(jnp.int32, blocks, 1) == rows - 1
    hidden = hidden_ref[...]
    ends = None
    for i in [rows - 2] + list(range(0, rows - 2, 2)):
        both = jnp.dot(hidden, down_ref[:, i * tail:(i + 2) * tail], preferred_element_type=jnp.float32)
        pieces = {i: both[:, :tail].reshape(blocks), i + 1: both[:, tail:].reshape(blocks)}
        if ends is None:
            ends = pieces.pop(i + 1)
        for j, value in pieces.items():
            value = jnp.where(last, jnp.broadcast_to(ends[:, j:j + 1, :], blocks), value).reshape(blocks[0] * rows, tail)
            for ref, starts in zip(outs, sources):
                taken = [value[start:start + rows] for start in starts]
                taken = jnp.concatenate(taken, axis=0) if len(taken) > 1 else taken[0]
                ref[:, j * tail:(j + 1) * tail] = taken.astype(ref.dtype)


def down(hidden, down_weight, span, pair, rows, first):
    total, units = hidden.shape
    width = down_weight.shape[1] // rows * (rows - 1)
    part = total // (span * pair)
    places = [first] + [i for i in range(part // rows) if i != first]

    def starts(p, t, chosen):
        return [(p * span + t) * part + i * rows for i in chosen]

    sources = [starts(0, t, range(part // rows)) for t in range(span)]
    for p in range(1, pair):
        sources.append([x for t in range(1, span) for x in starts(p, t, places[:1])])
        sources.append([x for t in range(1, span) for x in starts(p, t, places[1:])] + starts(p, 0, range(part // rows)))
    outs = pl.pallas_call(
        functools.partial(down_kernel, rows, sources),
        in_specs=[pl.BlockSpec(memory_space=pltpu.VMEM)] * 2,
        out_shape=[jax.ShapeDtypeStruct((rows * len(x), width), jnp.float32 if i < span else jnp.bfloat16) for i, x in enumerate(sources)],
        compiler_params=params(total),
        cost_estimate=cost(2 * total * width * units),
        name="down",
    )(hidden, in_vmem(down_weight))
    return outs[:span], outs[span::2], outs[span + 1::2]


def pair_sum_kernel(count, places, indices, keep_ref, *refs):
    received, outs = refs[:count], refs[-len(places):]
    rows = outs[0].shape[0]
    for place, i, out_ref in zip(places, indices, outs):
        value = keep_ref[place * rows:(place + 1) * rows, :]
        for ref in received:
            value += ref[i * rows:(i + 1) * rows, :].astype(jnp.float32)
        out_ref[...] = value.astype(out_ref.dtype)


def pair_sum(keep, received, rows, dtype, places, indices, after=()):
    vmem = [pl.BlockSpec(memory_space=pltpu.VMEM)] * (1 + len(received))
    return pl.pallas_call(
        functools.partial(pair_sum_kernel, len(received), places, indices),
        in_specs=vmem + [pl.BlockSpec(memory_space=pl.ANY)] * len(after),
        out_shape=[jax.ShapeDtypeStruct((rows, keep.shape[1]), dtype)] * len(places),
        compiler_params=params(),
        name="pair_sum",
    )(keep, *received, *after)


def span_sum_kernel(*refs):
    value = refs[0][...]
    for ref in refs[1:-1]:
        value += ref[...].astype(jnp.float32)
    refs[-1][...] = value.astype(refs[-1].dtype)


def span_sum(arrays):
    return pl.pallas_call(
        span_sum_kernel,
        out_shape=jax.ShapeDtypeStruct(arrays[0].shape, jnp.bfloat16),
        compiler_params=params(),
        name="span_sum",
    )(*arrays)


def load_kernel(count, *refs):
    semaphores = refs[-1]
    copies = [pltpu.make_async_copy(refs[i], refs[count + i], semaphores.at[i]) for i in range(count)]
    for copy in copies:
        copy.start()
    for copy in copies:
        copy.wait()


def load(arrays):
    return pl.pallas_call(
        functools.partial(load_kernel, len(arrays)),
        in_specs=[pl.BlockSpec(memory_space=pl.ANY)] * len(arrays),
        out_specs=[pl.BlockSpec(memory_space=pltpu.VMEM)] * len(arrays),
        out_shape=[jax.ShapeDtypeStruct(a.shape, a.dtype) for a in arrays],
        scratch_shapes=[pltpu.SemaphoreType.DMA((len(arrays),))],
        compiler_params=params(),
        cost_estimate=cost(0),
        name="load",
    )(*[pltpu.with_memory_space_constraint(a, pltpu.HBM) for a in arrays])


def pack_kernel(own_expert, tokens_ref, ids_ref, weights_ref, sides_ref, *packed_refs):
    ids, weights = ids_ref[...], weights_ref[...]
    rows, width = tokens_ref.shape
    tail = width // rows
    square = (rows, rows)
    row, column = lax.broadcasted_iota(jnp.int32, square, 0), lax.broadcasted_iota(jnp.int32, square, 1)
    last = lax.broadcasted_iota(jnp.int32, (rows, tail), 0) == rows - 1
    here = tokens_ref[...].astype(jnp.float32)
    below = pltpu.roll(here, rows - 1, 0)
    for s, packed_ref in enumerate(packed_refs):
        expert = lax.bitwise_xor(own_expert[0], s)
        named = ids == expert
        chosen = jnp.sum(jnp.where(named, weights, 0.0), axis=0, keepdims=True)
        coeff = jnp.sum(jnp.where(row == column, jnp.broadcast_to(chosen, square), 0.0), axis=1, keepdims=True)
        unnamed = 1.0 - jnp.sum(jnp.where(named, 1.0, 0.0), axis=0, keepdims=True)
        shift = jnp.max(jnp.where(column <= row, jnp.broadcast_to(unnamed, square), 0.0), axis=1, keepdims=True)
        sides_ref[:, s * LANES:(s + 1) * LANES] = jnp.broadcast_to(coeff, (rows, LANES))
        sides_ref[:, (EXPERTS + s) * LANES:(EXPERTS + s + 1) * LANES] = jnp.broadcast_to(shift, (rows, LANES))
        kept = jnp.where(shift > 0.5, below, here)
        for i in range(rows - 1):
            moved = jnp.broadcast_to(kept[i:i + 1, width - tail:], (rows, tail))
            piece = jnp.where(last, moved, kept[:, i * tail:(i + 1) * tail])
            packed_ref[:, i * tail:(i + 1) * tail] = piece.astype(jnp.bfloat16)


def pack(own_expert, tokens, ids, weights):
    rows, width = tokens.shape
    packed = jax.ShapeDtypeStruct((rows, width - width // rows), jnp.bfloat16)
    return pl.pallas_call(
        pack_kernel,
        in_specs=[pl.BlockSpec(memory_space=pltpu.SMEM)] + [pl.BlockSpec(memory_space=pltpu.VMEM)] * 3,
        out_shape=[jax.ShapeDtypeStruct((rows, 2 * EXPERTS * LANES), jnp.float32)] + [packed] * EXPERTS,
        compiler_params=params(),
        cost_estimate=cost(EXCHANGE_FLOPS),
        name="pack",
    )(own_expert, *load([tokens, ids.T, weights.T]))


def combine_kernel(base, places, counts, parts, sides_ref, *refs):
    if parts:
        *refs, out_hbm, out_ref, semaphores = refs
    else:
        *refs, out_ref = refs
    rows, width = out_ref.shape
    tail = width // rows
    row = lax.broadcasted_iota(jnp.int32, (rows, tail), 0)
    first, groups = refs[:base], refs[base:]
    terms = []
    for s, count in zip(places, counts):
        group, groups = groups[:count], groups[count:]
        packed = sum([ref[...].astype(jnp.float32) for ref in group[1:]], group[0][...].astype(jnp.float32))
        coeff = sides_ref[:, s * LANES:s * LANES + 1]
        shifted = sides_ref[:, (EXPERTS + s) * LANES:(EXPERTS + s) * LANES + 1] > 0.5
        terms.append((packed, coeff, shifted))
    copies = []
    for i in range(rows):
        columns = slice(i * tail, (i + 1) * tail)
        value = None
        for ref in first:
            value = ref[:, columns]
        for packed, coeff, shifted in terms:
            if i < rows - 1:
                piece = packed[:, columns]
            else:
                piece = jnp.zeros((rows, tail), jnp.float32)
                for j in range(rows - 1):
                    moved = jnp.broadcast_to(packed[rows - 1:, j * tail:(j + 1) * tail], (rows, tail))
                    piece = jnp.where(row == j, moved, piece)
            term = coeff * jnp.where(shifted, pltpu.roll(piece, 1, 0), piece)
            value = term if value is None else value + term
        out_ref[:, columns] = value.astype(out_ref.dtype)
        if parts and (i + 1) % (rows // parts) == 0:
            done = slice((len(copies) * (rows // parts)) * tail, (i + 1) * tail)
            copies.append(pltpu.make_async_copy(out_ref.at[:, done], out_hbm.at[:, done], semaphores.at[len(copies)]))
            copies[-1].start()
    for copy in copies:
        copy.wait()


def combine(sides, base, places, groups, width, dtype, parts=0):
    arrays = [a for group in groups for a in group]
    out_shape = jax.ShapeDtypeStruct((arrays[0].shape[0], width), dtype)
    return pl.pallas_call(
        functools.partial(combine_kernel, len(base), tuple(places), tuple(len(g) for g in groups), parts),
        out_shape=out_shape,
        out_specs=pl.BlockSpec(memory_space=pl.ANY if parts else pltpu.VMEM),
        scratch_shapes=[pltpu.VMEM(out_shape.shape, dtype), pltpu.SemaphoreType.DMA((parts,))] if parts else [],
        compiler_params=params(),
        name="combine",
    )(sides, *base, *arrays)


def local(tokens, expert_ids, route_weights, gate_weight, up_weight, down_weight):
    rows, width = tokens.shape
    attn = lax.axis_size("attn")
    pair = lax.axis_size("ffn")
    span = attn // EXPERTS

    def over_experts(value, other):
        return lax.ppermute(value, "attn", [(i, (i // span ^ other) * span + i % span) for i in range(attn)])

    def over_span(value, shift):
        return lax.ppermute(value, "attn", [(i, i // span * span + (i + shift) % span) for i in range(attn)])

    def over_pair(value, shift):
        return lax.ppermute(value, "ffn", [(i, (i + shift) % pair) for i in range(pair)])

    own_expert = (lax.axis_index("attn") // span).astype(jnp.int32).reshape(1)
    sides, *packed = pack(own_expert, tokens, expert_ids, route_weights)
    column = {s: over_experts(packed[s], s) if s else packed[0] for s in range(EXPERTS)}
    column = [column[s] for s in BLOCK_ORDER]
    parts = [column] + [[over_span(b, t) for b in column] for t in range(1, span)]
    groups = [stack(column)]
    for part in parts[1:]:
        groups += [stack(part[:-1]), stack(part[-1:], (), LAST_FLOPS)]
    *others, last = [over_pair(g, p) for p in range(1, pair) for g in groups]
    first = unpack([b for part in parts for b in part] + others, rows, width)
    hidden = gate_up(first, last, gate_weight, up_weight)

    first = BLOCK_ORDER.index(RETURN_ORDER[0])
    rest = [i for i in range(EXPERTS) if i != first]
    keeps, firsts, others = down(hidden, down_weight, span, pair, rows, first)
    received = [over_pair(b, -p) for p, b in enumerate(firsts, 1)]
    sums, after = {s: [] for s in range(EXPERTS)}, []
    for t in range(1, span):
        after += pair_sum(keeps[t], received, rows, jnp.bfloat16, [first], [t - 1])
        sums[RETURN_ORDER[0]].append(over_span(after[-1], -t))
    received = [over_pair(stack([b], after[:1]), -p) for p, b in enumerate(others, 1)]
    own = pair_sum(keeps[0], received, rows, jnp.float32, range(EXPERTS), [(span - 1) * len(rest) + i for i in range(EXPERTS)])
    for place, block in enumerate(own):
        sums[BLOCK_ORDER[place]].insert(0, block)

    def send_rest(planes, after):
        for t in range(1, span):
            places = [BLOCK_ORDER.index(s) for s in planes]
            indices = [(t - 1) * len(rest) + rest.index(place) for place in places]
            blocks = pair_sum(keeps[t], received, rows, jnp.bfloat16, places, indices, after)
            for s, block in zip(planes, blocks):
                sums[s].append(over_span(block, -t))

    send_rest(RETURN_ORDER[1:], [])
    totals = {s: span_sum(sums[s]) for s in RETURN_ORDER}
    send_rest([0], [totals[RETURN_ORDER[1]]])
    returned = {s: over_experts(totals[s], s) for s in RETURN_ORDER}
    far, *later = RETURN_ORDER
    early = combine(sides, [], [far], [[returned[far]]], width, jnp.float32)
    return combine(sides, [early], later + [0], [[returned[s]] for s in later] + [sums[0]], width, jnp.bfloat16, 4)


def solution(mesh):
    return jax.shard_map(
        local,
        mesh=mesh,
        in_specs=(
            P(("groups", "attn", "ffn"), None),
            P(("groups", "attn", "ffn"), None),
            P(("groups", "attn", "ffn"), None),
            P(None, ("attn", "ffn")),
            P(None, ("attn", "ffn")),
            P(("attn", "ffn"), None),
        ),
        out_specs=P(("groups", "attn", "ffn"), None),
        check_vma=False,
    )
```
